32 devices in a mesh: tx: 8 (over z, x), ty: 4 (over y, core).
Axes of the slice: x: 2, y: 2, z: 4, core: 2. Of those that a mesh axis runs over, the one named last changes fastest.
Arguments:
- features: bfloat16 [128, 128, 128], P(('tx', 'ty')), may hold values from -6 to 6
- occupancy: int32 [128, 128], P(('tx', 'ty')), may hold values from 0 to 1, as said below
- neighbors: int32 [27, 128], P(None, ('tx', 'ty')), may hold values from -1 to 127, as said below
- point_voxel: int32 [32768], P(('tx', 'ty')), may hold values from 0 to 511, as said below
- conv_weight: bfloat16 [27, 128, 128], replicated, may hold values from -0.109375 to 0.109375
- head_weight: bfloat16 [16, 128], replicated, may hold values from -0.5 to 0.5
- teacher: bfloat16 [16, 32768], P(None, ('tx', 'ty')), may hold values from -15 to 15
Outputs:
- grad_features: bfloat16 [128, 128, 128], P(('tx', 'ty'))
- grad_weight: float32 [27, 128, 128], replicated
The draws below stay inside these ranges and needn't reach their ends.
Inputs may be any that keep to these rules, and one draw needn't show every extreme that they name: `occupancy`: every voxel of a slot that holds no active brick is 0; every active brick has one or more occupied voxels. A brick's global slot is 4 times its tile's index (tx index times the number of ty devices plus ty index) plus (2 i + j) + k for its place (i, j, k) in the tile's 2 x 2 x 1 grid of bricks. neighbors[o, b] is the global slot of the brick at brick offset o from b if that brick is active and b is active, else -1; neighbors[13, b] is b exactly when b is active. At most 3 bricks of a tile are active, and some tile has exactly 3. `point_voxel`: each entry is 128 s + v for an occupied voxel v of slot s of the point's own tile.
All inputs are finite; a program needn't handle non-finite values.
Results may differ from the reference program's by a relative error of at most 0.0052.
Values may be sent and summed in bfloat16 or wider, within the bound.
No kernel may reach another device: no remote copies, remote signals or barrier semaphores. Data moves between devices by JAX's collectives and lax.ppermute only.
A program may use at most 64 MiB of HBM per device.

```python
import jax
import jax.numpy as jnp
from jax import lax

C = 128
K = 16
GX = 2
GY = 2
GZ = 1
POINTS_DEV = 1024
TILE_POS = 4
ACTIVE_MAX = 3
BRICKS = 128
POINTS = 32768
N_TX = 8
N_TY = 4


def layout_draw(key):
    base_key = jax.random.fold_in(key, 7)
    key_count, key_full, key_order, key_occupy, key_keep = jax.random.split(base_key, 5)
    tile_count = N_TX * N_TY
    uniform_pick = jax.random.randint(key_count, (tile_count,), 0, ACTIVE_MAX + 1)
    counts = jnp.minimum(ACTIVE_MAX, jnp.maximum(2, uniform_pick))
    fullest = jax.random.randint(key_full, (), 0, tile_count)
    counts = jnp.where(jnp.arange(tile_count) == fullest, ACTIVE_MAX, counts)
    scores = jax.random.randint(key_order, (tile_count, TILE_POS), 0, 1 << 30)
    scores = scores.at[tile_count - 1, TILE_POS - 1].set(-1)
    slot_order = jnp.argsort(scores, axis=1, stable=True)
    slot_ranks = jnp.argsort(slot_order, axis=1, stable=True)
    active = (slot_ranks < counts[:, None]).astype(jnp.int32)
    bricks = tile_count * TILE_POS
    filled = (jax.random.randint(key_occupy, (bricks, 128), 0, 8) < 5).astype(jnp.int32)
    single = jax.random.randint(key_keep, (bricks, 1), 0, 128)
    filled = jnp.maximum(filled, (jnp.arange(128)[None, :] == single).astype(jnp.int32))
    filled = filled.at[bricks - 1, 127].set(1)
    occupancy = filled * active.reshape(bricks, 1)
    return (active, occupancy)


def draw_occupancy(key, part):
    return layout_draw(key)[1].astype(jnp.int32)


def draw_neighbors(key, part):
    active, occupancy = layout_draw(key)
    tile_count = N_TX * N_TY
    bricks = tile_count * TILE_POS
    brick_ids = jnp.arange(bricks)
    tile_ids = brick_ids // TILE_POS
    places = brick_ids % TILE_POS
    coord_x = tile_ids // N_TY * GX + places // (GY * GZ)
    coord_y = tile_ids % N_TY * GY + places // GZ % GY
    coord_z = places % GZ
    active_flat = active.reshape(bricks)
    rows_list = []
    for move_x in (-1, 0, 1):
        for move_y in (-1, 0, 1):
            for move_z in (-1, 0, 1):
                near_x = coord_x + move_x
                near_y = coord_y + move_y
                near_z = coord_z + move_z
                inside = (near_x >= 0) & (near_x < N_TX * GX) & (near_y >= 0) & (near_y < N_TY * GY) & (near_z >= 0) & (near_z < GZ)
                safe_x = jnp.clip(near_x, 0, N_TX * GX - 1)
                safe_y = jnp.clip(near_y, 0, N_TY * GY - 1)
                safe_z = jnp.clip(near_z, 0, GZ - 1)
                near_tile = safe_x // GX * N_TY + safe_y // GY
                near_place = (safe_x % GX * GY + safe_y % GY) * GZ + safe_z
                near_id = near_tile * TILE_POS + near_place
                usable = inside & (active_flat[near_id] > 0) & (active_flat > 0)
                rows_list.append(jnp.where(usable, near_id, -1))
    return jnp.stack(rows_list).astype(jnp.int32)


def locate(running_row, wanted):
    return jnp.searchsorted(running_row, wanted, side='left')


def draw_point_voxel(key, part):
    active, occupancy = layout_draw(key)
    tile_count = N_TX * N_TY
    per_tile = occupancy.reshape(tile_count, TILE_POS * 128)
    running = jnp.cumsum(per_tile, axis=1)
    totals = running[:, -1]
    picks = jax.random.randint(jax.random.fold_in(key, 11), (tile_count, POINTS_DEV), 0, 1 << 30)
    wanted = picks % totals[:, None] + 1
    voxels = jax.vmap(locate)(running, wanted)
    voxels = voxels.at[tile_count - 1, POINTS_DEV - 1].set(TILE_POS * 128 - 1)
    return voxels.reshape(-1).astype(jnp.int32)


def block_levels(own_key, shape, cuts, low, largest):
    def one(position, shards_of):
        steps = jax.random.uniform(jax.random.fold_in(jax.random.fold_in(own_key, 6), position), (shards_of,), jnp.float32, low / len(cuts), largest / len(cuts))
        return jnp.repeat(jnp.exp(steps), shape[position] // shards_of).reshape((-1,) + (1,) * (len(shape) - position - 1))

    gain = one(*cuts[0])
    for cut in cuts[1:]:
        gain = gain * one(*cut)
    return gain


def centred(key, shape, width, reach, shards=(), dtype=jnp.bfloat16):
    entries = width * jax.random.normal(key, shape, jnp.float32)
    if shards:
        entries = entries * block_levels(key, shape, shards, -0.22, 0.18)
    return jnp.clip(entries, -reach, reach).astype(dtype)


def setup_inputs(seed: int = 0) -> dict:
    keys = jax.random.split(jax.random.key(seed), 8)
    return {
        "features": centred(keys[0], (BRICKS, 128, C), 1.0, 6.0, ((0, 32),)),
        "occupancy": draw_occupancy(jax.random.fold_in(keys[7], 71), 0),
        "neighbors": draw_neighbors(jax.random.fold_in(keys[7], 71), 0),
        "point_voxel": draw_point_voxel(jax.random.fold_in(keys[7], 71), 0),
        "conv_weight": centred(keys[4], (27, C, C), (27 * C) ** -0.5, 0.109375),
        "head_weight": centred(keys[5], (K, C), C ** -0.5, 0.5),
        "teacher": centred(keys[6], (K, POINTS), 3.0, 15.0, ((1, 32),)),
    }


def span_of(move, length):
    if move < 0:
        return (length - 1, length)
    if move == 0:
        return (0, length)
    return (0, 1)

def assemble_blocks(table, index):
    planes = []
    for move_x in (-1, 0, 1):
        columns = []
        for move_y in (-1, 0, 1):
            pieces = []
            for move_z in (-1, 0, 1):
                offset = 9 * (move_x + 1) + 3 * (move_y + 1) + (move_z + 1)
                start_x, stop_x = span_of(move_x, 4)
                start_y, stop_y = span_of(move_y, 4)
                start_z, stop_z = span_of(move_z, 8)
                window = table[:, start_x:stop_x, start_y:stop_y, start_z:stop_z, :]
                pieces.append(jnp.take(window, index[offset], axis=0))
            columns.append(jnp.concatenate(pieces, axis=3))
        planes.append(jnp.concatenate(columns, axis=2))
    return jnp.concatenate(planes, axis=1)

def plane_columns(padded, move_x, transpose):
    channels = padded.shape[-1]
    windows = []
    for move_y in (-1, 0, 1):
        for move_z in (-1, 0, 1):
            if transpose:
                anchor = (1 - move_x, 1 - move_y, 1 - move_z)
            else:
                anchor = (1 + move_x, 1 + move_y, 1 + move_z)
            window = padded[:, anchor[0]:anchor[0] + 4, anchor[1]:anchor[1] + 4, anchor[2]:anchor[2] + 8, :]
            windows.append(window.reshape(-1, channels))
    return jnp.concatenate(windows, axis=1)

def convolve(padded, weight, transpose):
    channels = padded.shape[-1]
    summed = jnp.zeros((padded.shape[0] * 128, channels), jnp.float32)
    for move_x in (-1, 0, 1):
        first = 9 * (move_x + 1)
        if transpose:
            matrix = jnp.concatenate([weight[first + inner].T for inner in range(9)], axis=0)
        else:
            matrix = weight[first:first + 9].reshape(9 * channels, channels)
        columns = plane_columns(padded, move_x, transpose)
        summed = summed + jnp.dot(columns, matrix, preferred_element_type=jnp.float32)
    return summed

def weight_terms(padded, gradient):
    channels = padded.shape[-1]
    flat_grad = gradient.reshape(-1, channels)
    terms = []
    for move_x in (-1, 0, 1):
        columns = plane_columns(padded, move_x, False)
        product = lax.dot_general(columns, flat_grad, (((0,), (0,)), ((), ())), preferred_element_type=jnp.float32)
        terms.append(product.reshape(9, channels, channels))
    return jnp.concatenate(terms, axis=0)

def silu_slope(value):
    logistic = jax.nn.sigmoid(value)
    return logistic * (1.0 + value * (1.0 - logistic))

def tile_gradient(pre, occupied, voxel_index, teacher_block, head_weight):
    channels = pre.shape[-1]
    occupied_cells = occupied[..., None]
    hidden = (jax.nn.silu(pre) * occupied_cells).astype(jnp.bfloat16)
    chosen = jnp.take(hidden.reshape(-1, channels), voxel_index, axis=0)
    logits = lax.dot_general(head_weight, chosen, (((1,), (1,)), ((), ())), preferred_element_type=jnp.float32)
    student = jnp.exp(logits)
    student = student / lax.optimization_barrier(jnp.sum(student, axis=0, keepdims=True))
    target = jnp.exp(teacher_block.astype(jnp.float32))
    target = target / lax.optimization_barrier(jnp.sum(target, axis=0, keepdims=True))
    slope_logits = student - target
    per_point = jnp.dot(slope_logits.T, head_weight.astype(jnp.float32), precision=lax.Precision.HIGHEST)
    per_voxel = jnp.zeros((pre.shape[0] * 128, channels), jnp.float32).at[voxel_index].add(per_point)
    return (per_voxel.reshape(pre.shape) * silu_slope(pre) * occupied_cells).astype(jnp.bfloat16)

def reference(features, occupancy, neighbors, point_voxel, conv_weight, head_weight, teacher):
    tile_count = N_TX * N_TY
    masked = features * occupancy.astype(jnp.bfloat16)[..., None]
    zero_brick = jnp.zeros((1, 4, 4, 8, C), jnp.bfloat16)
    table_x = jnp.concatenate([masked.reshape(BRICKS, 4, 4, 8, C), zero_brick], axis=0)
    index_all = jnp.where(neighbors < 0, BRICKS, neighbors).astype(jnp.int32)
    index_tiles = index_all.reshape(27, tile_count, TILE_POS).transpose(1, 0, 2)
    occupied_tiles = occupancy.reshape(tile_count, TILE_POS, 128).astype(jnp.float32)
    voxel_tiles = point_voxel.reshape(tile_count, POINTS_DEV).astype(jnp.int32)
    teacher_tiles = teacher.reshape(K, tile_count, POINTS_DEV).transpose(1, 0, 2)

    def forward_tile(inputs):
        index, occupied, voxel_index, teacher_block = inputs
        padded = assemble_blocks(table_x, index)
        pre = convolve(padded, conv_weight, False).reshape(TILE_POS, 128, C)
        return tile_gradient(pre, occupied, voxel_index, teacher_block, head_weight)
    gradient = lax.map(forward_tile, (index_tiles, occupied_tiles, voxel_tiles, teacher_tiles))
    table_g = jnp.concatenate([gradient.reshape(BRICKS, 4, 4, 8, C), zero_brick], axis=0)

    def backward_tile(carry, inputs):
        index, occupied, tile_grad = inputs
        padded_g = assemble_blocks(table_g, index)
        back_sum = convolve(padded_g, conv_weight, True).reshape(TILE_POS, 128, C)
        result = (back_sum * occupied[..., None]).astype(jnp.bfloat16)
        padded_x = assemble_blocks(table_x, index)
        return (carry + weight_terms(padded_x, tile_grad), result)
    summed, grad_tiles = lax.scan(backward_tile, jnp.zeros((27, C, C), jnp.float32), (index_tiles, occupied_tiles, gradient))
    grad_weight = summed / jnp.sqrt(jnp.mean(summed * summed) + 1e-06)
    return (grad_tiles.reshape(BRICKS, 128, C), grad_weight)
```

```python
import jax
import jax.numpy as jnp
from jax import lax
from jax.experimental import pallas as pl
from jax.experimental.pallas import tpu as pltpu
from jax.sharding import PartitionSpec as P

GX = 2
GY = 2
BX = 4
BY = 4
SIDE = 8
PLANE = SIDE * SIDE
TAPS = 9
BF16 = jnp.bfloat16
F32 = jnp.float32
PARTS = 8


def vmem(count):
    return [pl.BlockSpec(memory_space=pltpu.VMEM)] * count


def call(body, outs, inputs, scratch=(), limit=32 * 2**20, name=None):
    return pl.pallas_call(
        body,
        out_shape=outs,
        in_specs=vmem(len(inputs)),
        out_specs=jax.tree.map(lambda _: pl.BlockSpec(memory_space=pltpu.VMEM), outs),
        scratch_shapes=list(scratch),
        compiler_params=pltpu.CompilerParams(vmem_limit_bytes=limit),
        name=name,
    )(*inputs)


def shape(dims, dtype):
    return jax.ShapeDtypeStruct(dims, dtype)


def slot_planes(slot):
    return BX * (slot // GY), (slot % GY) * BY * SIDE


def parity(axis):
    return lax.rem(lax.axis_index(axis), 2) == 0


def occupancy_columns(occ_ref, rows):
    occ = occ_ref[...].astype(F32)
    padded = jnp.concatenate([occ, jnp.zeros((8 - occ.shape[0], occ.shape[1]), F32)], axis=0)
    return padded.T


def write_grid(grid_ref, planes):
    for x in range(SIDE):
        grid_ref[x + 1, SIDE : SIDE + PLANE, :] = planes(x)


def y_faces(planes):
    low = jnp.concatenate([planes(x)[:SIDE] for x in range(SIDE)], axis=0)
    high = jnp.concatenate([planes(x)[PLANE - SIDE :] for x in range(SIDE)], axis=0)
    return low, high


def send_faces(low_plane, high_plane, low_y, high_y, a_ref, b_ref, edge_ref):
    even = parity("tx")
    a_ref[...] = jnp.where(even, high_plane, low_plane).astype(BF16)
    b_ref[...] = jnp.where(even, low_plane, high_plane).astype(BF16)
    edge_ref[0] = low_y.astype(BF16)
    edge_ref[1] = high_y.astype(BF16)


def first_faces_kernel(feat_ref, occ_ref, a_ref, b_ref, edge_ref):
    columns = occupancy_columns(occ_ref, 8)
    channels = feat_ref.shape[2]

    def masked(slot, first, rows):
        mask = jnp.broadcast_to(columns[first : first + rows, slot : slot + 1], (rows, channels))
        return feat_ref[slot, first : first + rows, :].astype(F32) * mask

    def plane(x):
        i, a = x // BX, x % BX
        return jnp.concatenate(
            [masked(i * GY + j, a * BY * SIDE, BY * SIDE) for j in range(GY)], axis=0
        )

    every = [plane(x) for x in range(SIDE)]
    low_y, high_y = y_faces(lambda x: every[x])
    send_faces(every[0], every[SIDE - 1], low_y, high_y, a_ref, b_ref, edge_ref)


def edge_kernel(edge_ref, got_a_ref, got_b_ref, a_ref, b_ref):
    even_x, even_y = parity("tx"), parity("ty")
    got_a, got_b = got_a_ref[...].astype(F32), got_b_ref[...].astype(F32)
    low, high = jnp.where(even_x, got_b, got_a), jnp.where(even_x, got_a, got_b)
    bottom = jnp.concatenate([low[:SIDE], edge_ref[0].astype(F32), high[:SIDE]], axis=0)
    last = PLANE - SIDE
    top = jnp.concatenate([low[last:], edge_ref[1].astype(F32), high[last:]], axis=0)
    a_ref[...] = jnp.where(even_y, top, bottom).astype(BF16)
    b_ref[...] = jnp.where(even_y, bottom, top).astype(BF16)


def write_halo(grid_ref, x_a_ref, x_b_ref, y_a_ref, y_b_ref):
    even_x, even_y = parity("tx"), parity("ty")
    x_a, x_b = x_a_ref[...].astype(F32), x_b_ref[...].astype(F32)
    grid_ref[0, SIDE : SIDE + PLANE, :] = jnp.where(even_x, x_b, x_a)
    grid_ref[SIDE + 1, SIDE : SIDE + PLANE, :] = jnp.where(even_x, x_a, x_b)
    y_a, y_b = y_a_ref[...].astype(F32), y_b_ref[...].astype(F32)
    low, high = jnp.where(even_y, y_b, y_a), jnp.where(even_y, y_a, y_b)
    for x in range(SIDE + 2):
        grid_ref[x, :SIDE, :] = low[x * SIDE : (x + 1) * SIDE]
        grid_ref[x, SIDE + PLANE :, :] = high[x * SIDE : (x + 1) * SIDE]


def write_columns(grid_ref, cols_ref):
    channels = grid_ref.shape[2]
    z = lax.broadcasted_iota(jnp.int32, ((SIDE + 2) * SIDE, channels), 0) % SIDE
    for x in range(SIDE + 2):
        plane = grid_ref[x]
        zeros = jnp.zeros((1, channels), F32)
        before = jnp.where(z == 0, 0.0, jnp.concatenate([zeros, plane[:-1]], axis=0))
        after = jnp.where(z == SIDE - 1, 0.0, jnp.concatenate([plane[1:], zeros], axis=0))
        for dz, moved in enumerate((before, plane, after)):
            for dy in range(3):
                tap = 3 * dy + dz
                cols_ref[x, :, tap * channels : (tap + 1) * channels] = moved[
                    dy * SIDE : dy * SIDE + PLANE
                ].astype(BF16)


def split3(value):
    high = value.astype(BF16)
    rest = value - high.astype(F32)
    middle = rest.astype(BF16)
    low = (rest - middle.astype(F32)).astype(BF16)
    return high, middle, low


def contract(a, b, dim_a, dim_b):
    return lax.dot_general(a, b, (((dim_a,), (dim_b,)), ((), ())), preferred_element_type=F32)


def write_mask(occ_ref, mask_ref):
    columns = occupancy_columns(occ_ref, 8)
    rows, channels = BY * SIDE, mask_ref.shape[2]
    for slot in range(GX * GY):
        x0, row0 = slot_planes(slot)
        wide = jnp.broadcast_to(columns[:, slot : slot + 1], (columns.shape[0], channels))
        for a in range(BX):
            mask_ref[x0 + a, row0 : row0 + rows, :] = wide[a * rows : (a + 1) * rows]


def tile_kernel(
    feat_ref, occ_ref, x_a_ref, x_b_ref, y_a_ref, y_b_ref, weight_ref, head_ref, point_ref, teach_ref,
    grad_ref, a_ref, b_ref, edge_ref, keep_ref, send_ref,
    grid_ref, cols_ref, mask_ref, terms_ref,
):
    channels = feat_ref.shape[2]
    classes = head_ref.shape[0]
    voxels = SIDE * PLANE
    write_mask(occ_ref, mask_ref)
    rows = BY * SIDE
    for slot in range(GX * GY):
        x0, row0 = slot_planes(slot)
        for a in range(BX):
            part = feat_ref[slot, a * rows : (a + 1) * rows, :].astype(F32)
            part = part * mask_ref[x0 + a, row0 : row0 + rows, :]
            grid_ref[x0 + a + 1, SIDE + row0 : SIDE + row0 + rows, :] = part
    write_halo(grid_ref, x_a_ref, x_b_ref, y_a_ref, y_b_ref)
    write_columns(grid_ref, cols_ref)

    pre = jnp.zeros((voxels, channels), F32)
    for dx in range(3):
        window = cols_ref[dx : dx + SIDE].reshape(voxels, TAPS * channels)
        matrix = weight_ref[TAPS * dx : TAPS * (dx + 1)].reshape(TAPS * channels, channels)
        pre = pre + jnp.dot(window, matrix, preferred_element_type=F32)
    mask = mask_ref[...].reshape(voxels, channels)
    logistic = 1.0 / (1.0 + jnp.exp(-pre))
    slope = logistic * (1.0 + pre * (1.0 - logistic)) * mask
    hidden = (pre / (1.0 + jnp.exp(-pre)) * mask).astype(BF16)

    logits = contract(head_ref[...], hidden, 1, 1)
    student = jnp.exp(logits)
    student = student / jnp.sum(student, axis=0, keepdims=True)
    target = jnp.exp(teach_ref[...].astype(F32))
    target = target / jnp.sum(target, axis=0, keepdims=True)
    points = target.shape[1]
    place = point_ref[...]
    place = (place & 0x11F) | ((place & 0x80) >> 2) | ((place & 0x60) << 1)
    chosen = lax.broadcasted_iota(jnp.int32, (voxels, points), 0) == place
    chosen = jnp.where(chosen, 1.0, 0.0).astype(BF16)
    stack = jnp.concatenate([*split3(target), jnp.ones((classes, points), BF16)], axis=0)
    sums = contract(stack, chosen, 1, 1)
    target_sum = sums[:classes] + sums[classes : 2 * classes] + sums[2 * classes : 3 * classes]
    count = sums[3 * classes :]
    slope_logits = jnp.where(count > 0.0, count * student, 0.0) - target_sum
    heads = jnp.concatenate([head_ref[...]] * 3, axis=0)
    pieces = jnp.concatenate([piece.astype(F32) for piece in split3(slope_logits)], axis=0)
    dhidden = contract(pieces.T.astype(BF16), heads, 1, 0)
    gradient = dhidden * slope
    rounded = gradient.astype(BF16)
    grad_ref[...] = rounded.reshape(SIDE, PLANE, channels)
    low_y, high_y = y_faces(lambda x: gradient[x * PLANE : (x + 1) * PLANE])
    send_faces(gradient[:PLANE], gradient[voxels - PLANE :], low_y, high_y, a_ref, b_ref, edge_ref)

    for dx in range(3):
        window = cols_ref[dx : dx + SIDE].reshape(voxels, TAPS * channels)
        product = contract(window, rounded, 0, 0)
        terms_ref[TAPS * dx : TAPS * (dx + 1)] = product.reshape(TAPS, channels, channels)
    length = channels // PARTS
    for r in range(PARTS):
        first = pl.multiple_of(part_index(r) * length, length)
        part = terms_ref[:, pl.ds(first, length), :].reshape(-1, channels)
        if r < PARTS // 2:
            keep_ref[r] = part
        else:
            send_ref[r - PARTS // 2] = part.astype(BF16)


def part_index(r):
    tx, ty = lax.axis_index("tx"), lax.axis_index("ty")
    core, across, along = (ty & 1) ^ (r >> 2), (ty >> 1) & 1, tx & 1
    first = jnp.where(core == 0, across, along)
    second = jnp.where(core == 0, along, across)
    return core * 4 + ((first * 2 + second) ^ (r & 3))


def back_kernel(
    grad_ref, occ_ref, x_a_ref, x_b_ref, y_a_ref, y_b_ref, weight_ref, out_ref,
    grid_ref, cols_ref, mask_ref,
):
    channels = grad_ref.shape[2]
    voxels = SIDE * PLANE
    write_mask(occ_ref, mask_ref)
    write_grid(grid_ref, lambda x: grad_ref[x].astype(F32))
    write_halo(grid_ref, x_a_ref, x_b_ref, y_a_ref, y_b_ref)
    write_columns(grid_ref, cols_ref)
    total = jnp.zeros((voxels, channels), F32)
    for dx in range(3):
        window = cols_ref[dx : dx + SIDE].reshape(voxels, TAPS * channels)
        taps = [weight_ref[3 * TAPS - 1 - (TAPS * dx + tap)] for tap in range(TAPS)]
        total = total + contract(window, jnp.concatenate(taps, axis=1), 1, 1)
    total = (total * mask_ref[...].reshape(voxels, channels)).reshape(SIDE, PLANE, channels)
    rows = BY * SIDE
    for slot in range(GX * GY):
        x0, row0 = slot_planes(slot)
        for a in range(BX):
            part = total[x0 + a, row0 : row0 + rows].astype(BF16)
            out_ref[slot, a * rows : (a + 1) * rows, :] = part


def norm_kernel(*refs):
    pieces, out_ref = refs[:-1], refs[-1]
    kernels, channels = out_ref.shape[0], out_ref.shape[2]
    length = channels // PARTS
    squares = jnp.zeros((kernels * length, channels), F32)
    for piece in pieces:
        value = piece[...].astype(F32)
        squares = squares + value * value
    mean = jnp.sum(squares) / (kernels * channels * channels)
    scale = 1.0 / jnp.sqrt(jnp.broadcast_to(mean, (1, channels)) + 1e-06)
    for r, piece in enumerate(pieces):
        value = piece[...].astype(F32) * scale
        first = pl.multiple_of(part_index(r) * length, length)
        out_ref[:, pl.ds(first, length), :] = value.reshape(kernels, length, channels)


def swap_pairs(first, count):
    return [pair for i in range(first, count - 1, 2) for pair in ((i, i + 1), (i + 1, i))]


def exchange(axis, a, b):
    count = lax.axis_size(axis)
    return (
        lax.ppermute(a, axis, swap_pairs(0, count)),
        lax.ppermute(b, axis, swap_pairs(1, count)),
    )


def halo(a, b, edges):
    channels = a.shape[1]
    x_a, x_b = exchange("tx", a, b)
    face = shape(((SIDE + 2) * SIDE, channels), BF16)
    ya, yb = call(edge_kernel, (face, face), (edges, x_a, x_b), name="edge_faces")
    return (x_a, x_b, *exchange("ty", ya, yb))


def exchange_with(value, partner):
    n_tx, n_ty = lax.axis_size("tx"), lax.axis_size("ty")
    pairs = []
    for tx in range(n_tx):
        for ty in range(n_ty):
            other_tx, other_ty = partner(tx, ty)
            pairs.append((tx * n_ty + ty, other_tx * n_ty + other_ty))
    return lax.ppermute(value, ("tx", "ty"), pairs)


def on_device(features, occupancy, neighbors, point_voxel, conv_weight, head_weight, teacher):
    slots, brick, channels = features.shape
    kernels = conv_weight.shape[0]
    plane = shape((PLANE, channels), BF16)
    edges = shape((2, PLANE, channels), BF16)
    ext = (SIDE + 2, (SIDE + 2) * SIDE, channels)
    grid = pltpu.VMEM(ext, F32)
    cols = pltpu.VMEM((SIDE + 2, PLANE, TAPS * channels), BF16)
    mask = pltpu.VMEM((SIDE, PLANE, channels), F32)

    x_faces = call(
        first_faces_kernel, (plane, plane, edges), (features, occupancy), name="first_faces"
    )
    x_halo = halo(*x_faces)
    part = kernels * channels // PARTS
    gradient, ga, gb, g_edges, keep, send = call(
        tile_kernel,
        (
            shape((SIDE, PLANE, channels), BF16),
            plane,
            plane,
            edges,
            shape((PARTS // 2, part, channels), F32),
            shape((PARTS // 2, part, channels), BF16),
        ),
        (features, occupancy, *x_halo, conv_weight, head_weight, point_voxel.reshape(1, -1), teacher),
        (grid, cols, mask, pltpu.VMEM((kernels, channels, channels), F32)),
        name="tile",
    )

    n_tx, n_ty = lax.axis_size("tx"), lax.axis_size("ty")

    def by_core(tx, ty):
        return tx, ty ^ 1

    def first_way(tx, ty):
        return (tx, ty ^ 2) if ty % 2 == 0 else (tx ^ 1, ty)

    def second_way(tx, ty):
        return (tx ^ 1, ty) if ty % 2 == 0 else (tx, ty ^ 2)

    got0 = exchange_with(send, by_core).astype(F32)
    send1 = (keep[2:4] + got0[2:4]).astype(BF16)
    got1 = exchange_with(send1, first_way).astype(F32)
    send2 = (keep[1] + got0[1] + got1[1]).astype(BF16)
    got2 = exchange_with(send2, second_way).astype(F32)
    total = (keep[0] + got0[0] + got1[0] + got2).astype(BF16)
    bit = 2
    while bit < n_tx:
        flip = 2 * bit - 2
        got = exchange_with(total, lambda tx, ty, flip=flip: (tx ^ flip, ty))
        total = (total.astype(F32) + got.astype(F32)).astype(BF16)
        bit *= 2
    bit = 4
    while bit < n_ty:
        flip = 2 * bit - 4
        got = exchange_with(total, lambda tx, ty, flip=flip: (tx, ty ^ flip))
        total = (total.astype(F32) + got.astype(F32)).astype(BF16)
        bit *= 2
    piece1 = exchange_with(total, second_way)
    piece2 = exchange_with(total, first_way)
    piece3 = exchange_with(piece1, first_way)
    pieces = [total, piece1, piece2, piece3]
    pieces = pieces + [exchange_with(piece, by_core) for piece in pieces]
    grad_weight = call(
        norm_kernel, shape((kernels, channels, channels), F32), tuple(pieces), name="normalise"
    )

    g_halo = halo(ga, gb, g_edges)
    grad_features = call(
        back_kernel,
        shape((slots, brick, channels), BF16),
        (gradient, occupancy, *g_halo, conv_weight),
        (grid, cols, mask),
        name="back",
    )
    return (grad_features, grad_weight)


def solution(mesh):
    in_specs = (
        P(("tx", "ty"), None, None),
        P(("tx", "ty"), None),
        P(None, ("tx", "ty")),
        P(("tx", "ty")),
        P(),
        P(),
        P(None, ("tx", "ty")),
    )
    out_specs = (P(("tx", "ty"), None, None), P())
    return jax.shard_map(
        on_device, mesh=mesh, in_specs=in_specs, out_specs=out_specs, check_vma=False
    )
```

```python
import functools

import jax
import jax.numpy as jnp
from jax import lax
from jax.experimental import pallas as pl
from jax.experimental.pallas import tpu as pltpu
from jax.sharding import PartitionSpec as P

GX = 2
GY = 2
BX = 4
BY = 4
SIDE = 8
PLANE = SIDE * SIDE
TAPS = 9
BF16 = jnp.bfloat16
F32 = jnp.float32
PARTS = 8


def vmem(count):
    return [pl.BlockSpec(memory_space=pltpu.VMEM)] * count


def pin(array):
    return pltpu.with_memory_space_constraint(array, pltpu.HBM)


def call(body, outs, inputs, scratch=(), limit=32 * 2**20, name=None, fetched=0):
    return pl.pallas_call(
        body,
        out_shape=outs,
        in_specs=[pl.BlockSpec(memory_space=pltpu.HBM)] * fetched + vmem(len(inputs) - fetched),
        out_specs=jax.tree.map(lambda _: pl.BlockSpec(memory_space=pltpu.VMEM), outs),
        scratch_shapes=list(scratch),
        compiler_params=pltpu.CompilerParams(vmem_limit_bytes=limit),
        name=name,
    )(*[pin(array) for array in inputs[:fetched]], *inputs[fetched:])


def buffers(*arrays):
    rooms = [pltpu.VMEM(array.shape, array.dtype) for array in arrays]
    return (*rooms, pltpu.SemaphoreType.DMA((len(arrays),)))


def fetch(sources, rooms, semaphores):
    copies = [
        pltpu.make_async_copy(source, room, semaphores.at[i])
        for i, (source, room) in enumerate(zip(sources, rooms))
    ]
    for copy in copies:
        copy.start()
    return copies


def shape(dims, dtype):
    return jax.ShapeDtypeStruct(dims, dtype)


def slot_planes(slot):
    return BX * (slot // GY), (slot % GY) * BY * SIDE


def parity(axis):
    return lax.rem(lax.axis_index(axis), 2) == 0


def occupancy_columns(occ_ref, rows):
    occ = occ_ref[...].astype(F32)
    padded = jnp.concatenate([occ, jnp.zeros((8 - occ.shape[0], occ.shape[1]), F32)], axis=0)
    return padded.T


def write_grid(grid_ref, planes):
    for x in range(SIDE):
        grid_ref[x + 1, SIDE : SIDE + PLANE, :] = planes(x)


def y_faces(planes):
    low = jnp.concatenate([planes(x)[:SIDE] for x in range(SIDE)], axis=0)
    high = jnp.concatenate([planes(x)[PLANE - SIDE :] for x in range(SIDE)], axis=0)
    return low, high


def store_faces(low_plane, high_plane, low_y, high_y, pair_ref, next_ref, edge_ref):
    even = parity("tx")
    pair_ref[...] = jnp.where(even, high_plane, low_plane).astype(BF16)
    next_ref[...] = jnp.where(even, low_plane, high_plane).astype(BF16)
    edge_ref[0] = low_y.astype(BF16)
    edge_ref[1] = high_y.astype(BF16)


def first_faces_kernel(
    feat_hbm, occ_hbm, pair_ref, next_ref, edge_ref, feat_ref, occ_ref, semaphores
):
    for copy in fetch((feat_hbm, occ_hbm), (feat_ref, occ_ref), semaphores):
        copy.wait()
    columns = occupancy_columns(occ_ref, 8)
    channels = feat_ref.shape[2]

    def masked(slot, first, rows):
        mask = jnp.broadcast_to(columns[first : first + rows, slot : slot + 1], (rows, channels))
        return feat_ref[slot, first : first + rows, :].astype(F32) * mask

    def plane(x):
        i, a = x // BX, x % BX
        return jnp.concatenate(
            [masked(i * GY + j, a * BY * SIDE, BY * SIDE) for j in range(GY)], axis=0
        )

    every = [plane(x) for x in range(SIDE)]
    low_y, high_y = y_faces(lambda x: every[x])
    store_faces(every[0], every[SIDE - 1], low_y, high_y, pair_ref, next_ref, edge_ref)


def store_edges(low, high, edge_ref, a_ref, b_ref, planes_ref):
    even_y = parity("ty")
    planes_ref[0] = low.astype(BF16)
    planes_ref[1] = high.astype(BF16)
    last = PLANE - SIDE
    bottom = jnp.concatenate([low[:SIDE], edge_ref[0].astype(F32), high[:SIDE]], axis=0)
    top = jnp.concatenate([low[last:], edge_ref[1].astype(F32), high[last:]], axis=0)
    a_ref[...] = jnp.where(even_y, top, bottom).astype(BF16)
    b_ref[...] = jnp.where(even_y, bottom, top).astype(BF16)


def edge_kernel(edge_ref, next_ref, pair_ref, *refs):
    even = parity("tx")
    pair, other = pair_ref[...].astype(F32), next_ref[...].astype(F32)
    low, high = jnp.where(even, other, pair), jnp.where(even, pair, other)
    store_edges(low, high, edge_ref, *refs[-3:])


def hand_on_edge_kernel(flips, first_row, edge_ref, got1_ref, got2_ref, *refs):
    lines, (a_ref, b_ref, planes_ref) = refs[: len(flips)], refs[-3:]
    even = parity("tx")
    pair = picked_face(got1_ref[first_row[0] : first_row[0] + PLANE], got2_ref[first_row[1] : first_row[1] + PLANE])
    place = lax.axis_index("tx") // 2
    behind = jnp.where(even, place - 1, place + 1)
    other = jnp.zeros(pair.shape, F32)
    for flip, line_ref in zip(flips, lines):
        face = line_ref[first_row[2] : first_row[2] + PLANE].astype(F32)
        other = jnp.where((place ^ behind) == flip, face, other)
    low, high = jnp.where(even, other, pair), jnp.where(even, pair, other)
    store_edges(low, high, edge_ref, a_ref, b_ref, planes_ref)


def picked_face(by_first_way, by_second_way):
    lane = lane_of(lax.axis_index("tx"), lax.axis_index("ty"))
    return jnp.where(lane == 0, by_second_way.astype(F32), by_first_way.astype(F32))


def write_halo(grid_ref, planes_ref, y_a_ref, y_b_ref):
    even_y = parity("ty")
    grid_ref[0, SIDE : SIDE + PLANE, :] = planes_ref[0].astype(F32)
    grid_ref[SIDE + 1, SIDE : SIDE + PLANE, :] = planes_ref[1].astype(F32)
    y_a, y_b = y_a_ref[...].astype(F32), y_b_ref[...].astype(F32)
    low, high = jnp.where(even_y, y_b, y_a), jnp.where(even_y, y_a, y_b)
    for x in range(SIDE + 2):
        grid_ref[x, :SIDE, :] = low[x * SIDE : (x + 1) * SIDE]
        grid_ref[x, SIDE + PLANE :, :] = high[x * SIDE : (x + 1) * SIDE]


def write_columns(grid_ref, cols_ref):
    channels = grid_ref.shape[2]
    z = lax.broadcasted_iota(jnp.int32, ((SIDE + 2) * SIDE, channels), 0) % SIDE
    for x in range(SIDE + 2):
        plane = grid_ref[x]
        zeros = jnp.zeros((1, channels), F32)
        before = jnp.where(z == 0, 0.0, jnp.concatenate([zeros, plane[:-1]], axis=0))
        after = jnp.where(z == SIDE - 1, 0.0, jnp.concatenate([plane[1:], zeros], axis=0))
        for dz, moved in enumerate((before, plane, after)):
            for dy in range(3):
                tap = 3 * dy + dz
                cols_ref[x, :, tap * channels : (tap + 1) * channels] = moved[
                    dy * SIDE : dy * SIDE + PLANE
                ].astype(BF16)


def split3(value):
    high = value.astype(BF16)
    rest = value - high.astype(F32)
    middle = rest.astype(BF16)
    low = (rest - middle.astype(F32)).astype(BF16)
    return high, middle, low


def contract(a, b, dim_a, dim_b):
    return lax.dot_general(a, b, (((dim_a,), (dim_b,)), ((), ())), preferred_element_type=F32)


def write_mask(occ_ref, mask_ref):
    columns = occupancy_columns(occ_ref, 8)
    rows, channels = BY * SIDE, mask_ref.shape[2]
    for slot in range(GX * GY):
        x0, row0 = slot_planes(slot)
        wide = jnp.broadcast_to(columns[:, slot : slot + 1], (columns.shape[0], channels))
        for a in range(BX):
            mask_ref[x0 + a, row0 : row0 + rows, :] = wide[a * rows : (a + 1) * rows]


def prepare_kernel(
    feat_hbm, occ_hbm, point_hbm, teach_hbm, head_hbm, weight_hbm, order_ref,
    masked_ref, mask_ref, sums_ref, head_ref, weight_ref,
    feat_ref, occ_ref, point_ref, teach_ref, semaphores,
):
    del order_ref
    sources = (feat_hbm, occ_hbm, point_hbm, teach_hbm, head_hbm, weight_hbm)
    rooms = (feat_ref, occ_ref, point_ref, teach_ref, head_ref, weight_ref)
    copies = fetch(sources, rooms, semaphores)
    for copy in copies[:4]:
        copy.wait()
    rows = BY * SIDE
    write_mask(occ_ref, mask_ref)
    for slot in range(GX * GY):
        x0, row0 = slot_planes(slot)
        for a in range(BX):
            part = feat_ref[slot, a * rows : (a + 1) * rows, :].astype(F32)
            part = part * mask_ref[x0 + a, row0 : row0 + rows, :]
            masked_ref[x0 + a, row0 : row0 + rows, :] = part
    target = jnp.exp(teach_ref[...].astype(F32))
    target = target / jnp.sum(target, axis=0, keepdims=True)
    classes, points = target.shape
    place = point_ref[...]
    place = (place & 0x11F) | ((place & 0x80) >> 2) | ((place & 0x60) << 1)
    chosen = lax.broadcasted_iota(jnp.int32, (SIDE * PLANE, points), 0) == place
    chosen = jnp.where(chosen, 1.0, 0.0).astype(BF16)
    stack = jnp.concatenate([*split3(target), jnp.ones((classes, points), BF16)], axis=0)
    sums = contract(stack, chosen, 1, 1)
    target_sum = sums[:classes] + sums[classes : 2 * classes] + sums[2 * classes : 3 * classes]
    sums_ref[...] = jnp.concatenate([target_sum, sums[3 * classes :]], axis=0)
    for copy in copies[4:]:
        copy.wait()


def tile_kernel(
    masked_ref, mask_ref, sums_ref, head_ref, weight_ref, planes_ref, y_b_ref, y_a_ref,
    grad_ref, next_ref, edge_ref, keep_ref, send_ref,
    grid_ref, cols_ref, terms_ref,
):
    channels = masked_ref.shape[2]
    classes = head_ref.shape[0]
    voxels = SIDE * PLANE
    write_grid(grid_ref, lambda x: masked_ref[x])
    write_halo(grid_ref, planes_ref, y_a_ref, y_b_ref)
    write_columns(grid_ref, cols_ref)

    pre = jnp.zeros((voxels, channels), F32)
    for dx in range(3):
        window = cols_ref[dx : dx + SIDE].reshape(voxels, TAPS * channels)
        matrix = weight_ref[TAPS * dx : TAPS * (dx + 1)].reshape(TAPS * channels, channels)
        pre = pre + jnp.dot(window, matrix, preferred_element_type=F32)
    mask = mask_ref[...].reshape(voxels, channels)
    logistic = 1.0 / (1.0 + jnp.exp(-pre))
    slope = logistic * (1.0 + pre * (1.0 - logistic)) * mask
    hidden = (pre / (1.0 + jnp.exp(-pre)) * mask).astype(BF16)

    logits = contract(head_ref[...], hidden, 1, 1)
    student = jnp.exp(logits)
    student = student / jnp.sum(student, axis=0, keepdims=True)
    target_sum, count = sums_ref[:classes], sums_ref[classes:]
    slope_logits = jnp.where(count > 0.0, count * student, 0.0) - target_sum
    heads = jnp.concatenate([head_ref[...]] * 3, axis=0)
    pieces = jnp.concatenate([piece.astype(F32) for piece in split3(slope_logits)], axis=0)
    dhidden = contract(pieces.T.astype(BF16), heads, 1, 0)
    gradient = dhidden * slope
    rounded = gradient.astype(BF16)
    grad_ref[...] = rounded.reshape(SIDE, PLANE, channels)
    low_y, high_y = y_faces(lambda x: gradient[x * PLANE : (x + 1) * PLANE])
    ends = gradient[:PLANE], gradient[voxels - PLANE :]
    pair_ref = send_ref.at[send_ref.shape[0] - PLANE :]
    store_faces(*ends, low_y, high_y, pair_ref, next_ref, edge_ref)

    for dx in range(3):
        window = cols_ref[dx : dx + SIDE].reshape(voxels, TAPS * channels)
        product = contract(window, rounded, 0, 0)
        terms_ref[TAPS * dx : TAPS * (dx + 1)] = product.reshape(TAPS, channels, channels)
    length = channels // PARTS
    for r in range(PARTS):
        first = pl.multiple_of(part_index(r) * length, length)
        part = terms_ref[:, pl.ds(first, length), :].reshape(-1, channels)
        row = (r % (PARTS // 2)) * part.shape[0]
        if r < PARTS // 2:
            keep_ref[row : row + part.shape[0]] = part
        else:
            send_ref[row : row + part.shape[0]] = part.astype(BF16)


def lane_of(tx, ty):
    return (ty ^ (ty >> 1) ^ tx ^ (tx >> 1)) & 1


def part_index(r):
    tx, ty = lax.axis_index("tx"), lax.axis_index("ty")
    lane, across, along = lane_of(tx, ty) ^ (r >> 2), (ty >> 1) & 1, tx & 1
    first = jnp.where(lane == 0, across, along)
    second = jnp.where(lane == 0, along, across)
    return lane * 4 + ((first * 2 + second) ^ (r & 3))


def back_kernel(
    mask_ref, weight_ref, grad_ref, planes_ref, y_b_ref, y_a_ref, out_ref, token_ref,
    grid_ref, cols_ref,
):
    channels = grad_ref.shape[2]
    voxels = SIDE * PLANE
    write_grid(grid_ref, lambda x: grad_ref[x].astype(F32))
    write_halo(grid_ref, planes_ref, y_a_ref, y_b_ref)
    write_columns(grid_ref, cols_ref)
    token_ref[...] = jnp.zeros(token_ref.shape, F32)
    total = jnp.zeros((voxels, channels), F32)
    for dx in range(3):
        window = cols_ref[dx : dx + SIDE].reshape(voxels, TAPS * channels)
        taps = [weight_ref[3 * TAPS - 1 - (TAPS * dx + tap)] for tap in range(TAPS)]
        total = total + contract(window, jnp.concatenate(taps, axis=1), 1, 1)
    total = (total * mask_ref[...].reshape(voxels, channels)).reshape(SIDE, PLANE, channels)
    rows = BY * SIDE
    for slot in range(GX * GY):
        x0, row0 = slot_planes(slot)
        for a in range(BX):
            part = total[x0 + a, row0 : row0 + rows].astype(BF16)
            out_ref[slot, a * rows : (a + 1) * rows, :] = part


def norm_kernel(near_ref, far_ref, got_near_ref, got_far_ref, out_ref):
    kernels, channels = out_ref.shape[0], out_ref.shape[2]
    length = channels // PARTS
    refs = (near_ref, far_ref, got_near_ref, got_far_ref)
    rows = kernels * length
    pieces = [ref.at[i * rows : (i + 1) * rows] for ref in refs for i in range(2)]
    squares = jnp.zeros((kernels * length, channels), F32)
    for piece in pieces:
        value = piece[...].astype(F32)
        squares = squares + value * value
    mean = jnp.sum(squares) / (kernels * channels * channels)
    scale = 1.0 / jnp.sqrt(jnp.broadcast_to(mean, (1, channels)) + 1e-06)
    for r, piece in enumerate(pieces):
        value = piece[...].astype(F32) * scale
        first = pl.multiple_of(part_index(r) * length, length)
        out_ref[:, pl.ds(first, length), :] = value.reshape(kernels, length, channels)


def swap_pairs(first, count):
    return [pair for i in range(first, count - 1, 2) for pair in ((i, i + 1), (i + 1, i))]


def swap_along_y(a, b):
    count = lax.axis_size("ty")
    got_b = lax.ppermute(b, "ty", swap_pairs(1, count))
    return lax.ppermute(a, "ty", swap_pairs(0, count)), got_b


def edge_faces(kernel, edges, faces, waits=()):
    face = shape(((SIDE + 2) * SIDE, edges.shape[2]), BF16)
    return pl.pallas_call(
        kernel,
        out_shape=(face, face, shape(edges.shape, BF16)),
        in_specs=vmem(1 + len(faces)) + [pl.BlockSpec(memory_space=pl.ANY)] * len(waits),
        out_specs=tuple(vmem(3)),
        compiler_params=pltpu.CompilerParams(vmem_limit_bytes=16 * 2**20),
        name="edge_faces",
    )(edges, *faces, *waits)


def exchange_with(value, partner):
    n_tx, n_ty = lax.axis_size("tx"), lax.axis_size("ty")
    pairs = []
    for tx in range(n_tx):
        for ty in range(n_ty):
            other = partner(tx, ty)
            if other is not None:
                pairs.append((tx * n_ty + ty, other[0] * n_ty + other[1]))
    return lax.ppermute(value, ("tx", "ty"), pairs)


def by_core(tx, ty):
    return tx, ty ^ 1


def same_lane(tx, ty, other_tx, other_ty):
    return other_tx, other_ty ^ lane_of(tx, ty) ^ lane_of(other_tx, other_ty)


def first_way(tx, ty):
    other = (tx, ty ^ 2) if lane_of(tx, ty) == 0 else (tx ^ 1, ty)
    return same_lane(tx, ty, *other)


def second_way(tx, ty):
    other = (tx ^ 1, ty) if lane_of(tx, ty) == 0 else (tx, ty ^ 2)
    return same_lane(tx, ty, *other)


def along_line(flip):
    return lambda tx, ty: same_lane(tx, ty, tx ^ (2 * flip), ty)


def add(*terms):
    total = terms[0]
    for term in terms[1:]:
        total = total + term
    return total


def message(sections, waits=(), passes=()):
    arrays = []
    for _, _, *terms in sections:
        for array, _ in terms:
            if not any(array is known for known in arrays):
                arrays.append(array)
    place = [[next(i for i, x in enumerate(arrays) if x is array) for array, _ in terms] for _, _, *terms in sections]
    count, others = len(arrays), len(waits) + len(passes)
    total_rows = sum(section[0] for section in sections)

    def body(*refs):
        out_ref, row = refs[count + others], 0
        for places, (rows, fn, *terms) in zip(place, sections):
            values = [refs[i][first : first + rows].astype(F32) for i, (_, first) in zip(places, terms)]
            out_ref[row : row + rows] = fn(*values).astype(BF16)
            row += rows

    plain = pl.BlockSpec(memory_space=pl.ANY)
    outs = [shape((total_rows, arrays[0].shape[1]), BF16)]
    out, *passed = pl.pallas_call(
        body,
        out_shape=outs + [shape(x.shape, x.dtype) for x in passes],
        in_specs=vmem(count) + [plain] * others,
        out_specs=vmem(1) + [plain] * len(passes),
        input_output_aliases={count + len(waits) + i: 1 + i for i in range(len(passes))},
        compiler_params=pltpu.CompilerParams(vmem_limit_bytes=16 * 2**20),
        name="message",
    )(*arrays, *waits, *passes)
    return (out, *passed) if passes else out


def after(value, token):
    plain = pl.BlockSpec(memory_space=pl.ANY)
    return pl.pallas_call(
        lambda value_ref, token_ref, out_ref: None,
        out_shape=shape(value.shape, value.dtype),
        in_specs=[plain] * 2,
        out_specs=plain,
        input_output_aliases={0: 0},
        compiler_params=pltpu.CompilerParams(vmem_limit_bytes=16 * 2**20),
        name="after",
    )(value, token)


def on_device(features, occupancy, neighbors, point_voxel, conv_weight, head_weight, teacher):
    slots, brick, channels = features.shape
    kernels = conv_weight.shape[0]
    n_tx, n_ty = lax.axis_size("tx"), lax.axis_size("ty")
    edges = shape((2, PLANE, channels), BF16)
    ext = (SIDE + 2, (SIDE + 2) * SIDE, channels)
    grid = pltpu.VMEM(ext, F32)
    cols = pltpu.VMEM((SIDE + 2, PLANE, TAPS * channels), BF16)

    fetched = (features, occupancy)
    face = shape((PLANE, channels), BF16)
    pair_face, next_face, x_edges = call(
        first_faces_kernel, (face, face, edges), fetched, buffers(*fetched),
        name="first_faces", fetched=2,
    )
    x_next = lax.ppermute(next_face, "tx", swap_pairs(1, n_tx))
    x_pair = lax.ppermute(pair_face, "tx", swap_pairs(0, n_tx))
    fetched = (
        features, occupancy, point_voxel.reshape(1, -1), teacher, head_weight, conv_weight
    )
    classes = head_weight.shape[0]
    planes = shape((SIDE, PLANE, channels), F32)
    prepared = call(
        prepare_kernel,
        (
            planes,
            planes,
            shape((2 * classes, SIDE * PLANE), F32),
            shape(head_weight.shape, BF16),
            shape(conv_weight.shape, BF16),
        ),
        (*fetched, x_edges),
        (*buffers(*fetched[:4])[:-1], pltpu.SemaphoreType.DMA((len(fetched),))),
        name="prepare",
        fetched=len(fetched),
    )
    y_a, y_b, planes = edge_faces(edge_kernel, x_edges, (x_next, x_pair), prepared[:1])
    y_a, y_b = swap_along_y(y_a, y_b)
    part = kernels * channels // PARTS
    gradient, g_next, g_edges, keep, send = call(
        tile_kernel,
        (
            shape((SIDE, PLANE, channels), BF16),
            face,
            edges,
            shape((PARTS // 2 * part, channels), F32),
            shape((PARTS // 2 * part + PLANE, channels), BF16),
        ),
        (*prepared, planes, y_b, y_a),
        (grid, cols, pltpu.VMEM((kernels, channels, channels), F32)),
        name="tile",
    )
    mask, weight = prepared[1], prepared[4]

    got0 = exchange_with(send, by_core)
    faces = [(PLANE, add, (got0, 4 * part)), (PLANE, add, (g_next, 0))]
    kept = [(2 * part, add, (keep, 2 * part), (got0, 2 * part))]
    got1 = exchange_with(message(kept + faces), first_way)
    kept = [(part, add, (keep, part), (got0, part), (got1, part))]
    got2 = exchange_with(message(kept + faces), second_way)
    at = (2 * part, part, part)
    hand_on = (PLANE, picked_face, (got1, at[0] + PLANE), (got2, at[1] + PLANE))
    total = [(part, add, (keep, 0), (got0, 0), (got1, 0), (got2, 0))]
    flips, lines = [], []
    while 2 ** len(flips) < n_tx // 2:
        flips.append(2 ** (len(flips) + 1) - 1)
        own = message(total + [hand_on])
        lines.append(exchange_with(own, along_line(flips[-1])))
        total = [(part, add, (own, 0), (lines[-1], 0))]
        hand_on = (PLANE, add, (own, part))
    bit = 4
    while bit < n_ty:
        own = message(total)
        flip = 2 * bit - 4
        got = exchange_with(own, lambda tx, ty, flip=flip: same_lane(tx, ty, tx, ty ^ flip))
        total = [(part, add, (own, 0), (got, 0))]
        bit *= 2
    total, g_edges = message(total, (), (g_edges,))
    got3 = exchange_with(total, second_way)
    kernel = functools.partial(hand_on_edge_kernel, flips, at)
    g_a, g_b, planes = edge_faces(kernel, g_edges, (got1, got2, *lines))
    g_a, g_b = swap_along_y(g_a, g_b)
    near, gradient = message(
        [(part, add, (total, 0)), (part, add, (got3, 0))], (g_b, g_a), (gradient,)
    )
    far = exchange_with(near, first_way)
    grad_features, token = call(
        back_kernel,
        (shape((slots, brick, channels), BF16), shape((8, channels), F32)),
        (mask, weight, gradient, planes, g_b, g_a),
        (grid, cols),
        name="back",
    )
    far = after(far, token)
    grad_weight = call(
        norm_kernel,
        shape((kernels, channels, channels), F32),
        (near, far, exchange_with(near, by_core), exchange_with(far, by_core)),
        name="normalise",
    )
    return (grad_features, grad_weight)


def solution(mesh):
    in_specs = (
        P(("tx", "ty"), None, None),
        P(("tx", "ty"), None),
        P(None, ("tx", "ty")),
        P(("tx", "ty")),
        P(),
        P(),
        P(None, ("tx", "ty")),
    )
    out_specs = (P(("tx", "ty"), None, None), P())
    return jax.shard_map(
        on_device, mesh=mesh, in_specs=in_specs, out_specs=out_specs, check_vma=False
    )
```

```python
import functools

import jax
import jax.numpy as jnp
from jax import lax
from jax.experimental import pallas as pl
from jax.experimental.pallas import tpu as pltpu
from jax.sharding import PartitionSpec as P

GX = 2
GY = 2
BX = 4
BY = 4
SIDE = 8
PLANE = SIDE * SIDE
TAPS = 9
BF16 = jnp.bfloat16
F32 = jnp.float32
PARTS = 8


def vmem(count):
    return [pl.BlockSpec(memory_space=pltpu.VMEM)] * count


def pin(array):
    return pltpu.with_memory_space_constraint(array, pltpu.HBM)


def call(body, outs, inputs, scratch=(), limit=32 * 2**20, name=None, fetched=0):
    return pl.pallas_call(
        body,
        out_shape=outs,
        in_specs=[pl.BlockSpec(memory_space=pltpu.HBM)] * fetched + vmem(len(inputs) - fetched),
        out_specs=jax.tree.map(lambda _: pl.BlockSpec(memory_space=pltpu.VMEM), outs),
        scratch_shapes=list(scratch),
        compiler_params=pltpu.CompilerParams(vmem_limit_bytes=limit),
        name=name,
    )(*[pin(array) for array in inputs[:fetched]], *inputs[fetched:])


def buffers(*arrays):
    rooms = [pltpu.VMEM(array.shape, array.dtype) for array in arrays]
    return (*rooms, pltpu.SemaphoreType.DMA((len(arrays),)))


def fetch(sources, rooms, semaphores):
    copies = [
        pltpu.make_async_copy(source, room, semaphores.at[i])
        for i, (source, room) in enumerate(zip(sources, rooms))
    ]
    for copy in copies:
        copy.start()
    return copies


def shape(dims, dtype):
    return jax.ShapeDtypeStruct(dims, dtype)


def slot_planes(slot):
    return BX * (slot // GY), (slot % GY) * BY * SIDE


def parity(axis):
    return lax.rem(lax.axis_index(axis), 2) == 0


def occupancy_columns(occ_ref, rows):
    occ = occ_ref[...].astype(F32)
    padded = jnp.concatenate([occ, jnp.zeros((8 - occ.shape[0], occ.shape[1]), F32)], axis=0)
    return padded.T


def write_grid(grid_ref, planes):
    for x in range(SIDE):
        grid_ref[x + 1, SIDE : SIDE + PLANE, :] = planes(x)


def y_faces(planes):
    low = jnp.concatenate([planes(x)[:SIDE] for x in range(SIDE)], axis=0)
    high = jnp.concatenate([planes(x)[PLANE - SIDE :] for x in range(SIDE)], axis=0)
    return low, high


def store_faces(low_plane, high_plane, low_y, high_y, pair_ref, next_ref, edge_ref):
    even = parity("tx")
    pair_ref[...] = jnp.where(even, high_plane, low_plane).astype(BF16)
    next_ref[...] = jnp.where(even, low_plane, high_plane).astype(BF16)
    edge_ref[0] = low_y.astype(BF16)
    edge_ref[1] = high_y.astype(BF16)


def first_faces_kernel(
    feat_hbm, occ_hbm, b_ref, a_ref, ends_ref, masked_ref, mask_ref, feat_ref, occ_ref, semaphores
):
    for copy in fetch((feat_hbm, occ_hbm), (feat_ref, occ_ref), semaphores):
        copy.wait()
    columns = occupancy_columns(occ_ref, 8)
    rows, channels = BY * SIDE, mask_ref.shape[2]
    for slot in range(GX * GY):
        x0, row0 = slot_planes(slot)
        wide = jnp.broadcast_to(columns[:, slot : slot + 1], (columns.shape[0], channels))
        for a in range(BX):
            mask = wide[a * rows : (a + 1) * rows]
            part = feat_ref[slot, a * rows : (a + 1) * rows, :].astype(F32)
            mask_ref[x0 + a, row0 : row0 + rows, :] = mask
            masked_ref[x0 + a, row0 : row0 + rows, :] = part * mask
    low_y, high_y = y_faces(lambda x: masked_ref[x])
    even = parity("ty")
    a_ref[...] = jnp.where(even, high_y, low_y).astype(BF16)
    b_ref[...] = jnp.where(even, low_y, high_y).astype(BF16)
    ends_ref[0] = masked_ref[0].astype(BF16)
    ends_ref[1] = masked_ref[SIDE - 1].astype(BF16)


def halo_along_y(b_ref, a_ref):
    even = parity("ty")
    a, b = a_ref[...].astype(F32), b_ref[...].astype(F32)
    return jnp.where(even, b, a), jnp.where(even, a, b)


def x_faces_kernel(ends_ref, y_b_ref, y_a_ref, *refs):
    pair_ref, next_ref = refs[-2:]
    low, high = halo_along_y(y_b_ref, y_a_ref)
    last = PLANE - SIDE
    first = jnp.concatenate([low[:SIDE], ends_ref[0].astype(F32), high[:SIDE]], axis=0)
    final = jnp.concatenate([low[last:], ends_ref[1].astype(F32), high[last:]], axis=0)
    even = parity("tx")
    pair_ref[...] = jnp.where(even, final, first).astype(BF16)
    next_ref[...] = jnp.where(even, first, final).astype(BF16)


def store_edges(low, high, edge_ref, a_ref, b_ref, planes_ref):
    even_y = parity("ty")
    planes_ref[0] = low.astype(BF16)
    planes_ref[1] = high.astype(BF16)
    last = PLANE - SIDE
    bottom = jnp.concatenate([low[:SIDE], edge_ref[0].astype(F32), high[:SIDE]], axis=0)
    top = jnp.concatenate([low[last:], edge_ref[1].astype(F32), high[last:]], axis=0)
    a_ref[...] = jnp.where(even_y, top, bottom).astype(BF16)
    b_ref[...] = jnp.where(even_y, bottom, top).astype(BF16)


def hand_on_edge_kernel(flips, first_row, edge_ref, got1_ref, got2_ref, *refs):
    lines, (a_ref, b_ref, planes_ref) = refs[: len(flips)], refs[-3:]
    even = parity("tx")
    pair = picked_face(got1_ref[first_row[0] : first_row[0] + PLANE], got2_ref[first_row[1] : first_row[1] + PLANE])
    place = lax.axis_index("tx") // 2
    behind = jnp.where(even, place - 1, place + 1)
    other = jnp.zeros(pair.shape, F32)
    lane = lane_of(lax.axis_index("tx"), lax.axis_index("ty"))
    for both, line_ref in zip(flips, lines):
        flip = jnp.where(lane == 0, *both)
        face = line_ref[first_row[2] : first_row[2] + PLANE].astype(F32)
        other = jnp.where((place ^ behind) == flip, face, other)
    low, high = jnp.where(even, other, pair), jnp.where(even, pair, other)
    store_edges(low, high, edge_ref, a_ref, b_ref, planes_ref)


def picked_face(by_first_way, by_second_way):
    lane = lane_of(lax.axis_index("tx"), lax.axis_index("ty"))
    return jnp.where(lane == 0, by_second_way.astype(F32), by_first_way.astype(F32))


def write_columns(plane, cols_ref):
    channels = plane.shape[1]
    z = lax.broadcasted_iota(jnp.int32, plane.shape, 0) % SIDE
    zeros = jnp.zeros((1, channels), F32)
    before = jnp.where(z == 0, 0.0, jnp.concatenate([zeros, plane[:-1]], axis=0))
    after = jnp.where(z == SIDE - 1, 0.0, jnp.concatenate([plane[1:], zeros], axis=0))
    for dz, moved in enumerate((before, plane, after)):
        for dy in range(3):
            tap = 3 * dy + dz
            window = moved[dy * SIDE : dy * SIDE + PLANE]
            cols_ref[:, tap * channels : (tap + 1) * channels] = window.astype(BF16)


def split3(value):
    high = value.astype(BF16)
    rest = value - high.astype(F32)
    middle = rest.astype(BF16)
    low = (rest - middle.astype(F32)).astype(BF16)
    return high, middle, low


def contract(a, b, dim_a, dim_b):
    return lax.dot_general(a, b, (((dim_a,), (dim_b,)), ((), ())), preferred_element_type=F32)


def voxel_sums(point_ref, teach_ref):
    target = jnp.exp(teach_ref[...].astype(F32))
    target = target / jnp.sum(target, axis=0, keepdims=True)
    classes, points = target.shape
    place = point_ref[...]
    place = (place & 0x11F) | ((place & 0x80) >> 2) | ((place & 0x60) << 1)
    chosen = lax.broadcasted_iota(jnp.int32, (SIDE * PLANE, points), 0) == place
    chosen = jnp.where(chosen, 1.0, 0.0).astype(BF16)
    stack = jnp.concatenate([*split3(target), jnp.ones((classes, points), BF16)], axis=0)
    sums = contract(stack, chosen, 1, 1)
    target_sum = sums[:classes] + sums[classes : 2 * classes] + sums[2 * classes : 3 * classes]
    return jnp.concatenate([target_sum, sums[3 * classes :]], axis=0)


def main_kernel(
    point_hbm, teach_hbm, head_hbm, weight_hbm, masked_ref, y_b_ref, y_a_ref,
    cols_ref, pre_ref, sums_ref, head_ref, weight_ref,
    point_ref, teach_ref, semaphores,
):
    sources = (point_hbm, teach_hbm, head_hbm, weight_hbm)
    copies = fetch(sources, (point_ref, teach_ref, head_ref, weight_ref), semaphores)
    channels = masked_ref.shape[2]
    low, high = halo_along_y(y_b_ref, y_a_ref)
    for x in range(SIDE):
        rows = slice(x * SIDE, (x + 1) * SIDE)
        plane = jnp.concatenate([low[rows], masked_ref[x], high[rows]], axis=0)
        write_columns(plane, cols_ref.at[x])
    wide, inner = TAPS * channels, SIDE - 1
    for copy in copies[:2]:
        copy.wait()
    sums_ref[...] = voxel_sums(point_ref, teach_ref)
    for copy in copies[2:]:
        copy.wait()

    def product(planes, dx):
        window = cols_ref[planes].reshape(-1, wide)
        matrix = weight_ref[TAPS * dx : TAPS * (dx + 1)].reshape(wide, channels)
        return jnp.dot(window, matrix, preferred_element_type=F32)

    edge = jnp.zeros((PLANE, channels), F32)
    pre = product(slice(0, SIDE), 1)
    pre = pre + jnp.concatenate([edge, product(slice(0, inner), 0)], axis=0)
    pre_ref[...] = pre + jnp.concatenate([product(slice(1, SIDE), 2), edge], axis=0)


def tile_kernel(
    cols_ref, pre_ref, mask_ref, sums_ref, head_ref, weight_ref, x_next_ref, x_pair_ref,
    grad_ref, next_ref, edge_ref, keep_ref, send_ref,
    ends_ref, terms_ref,
):
    channels = cols_ref.shape[2] // TAPS
    classes = head_ref.shape[0]
    voxels, wide, inner = SIDE * PLANE, TAPS * channels, (SIDE - 1) * PLANE
    even = parity("tx")
    pair, other = x_pair_ref[...].astype(F32), x_next_ref[...].astype(F32)
    write_columns(jnp.where(even, other, pair), ends_ref.at[0])
    write_columns(jnp.where(even, pair, other), ends_ref.at[1])
    first = weight_ref[:TAPS].reshape(wide, channels)
    final = weight_ref[2 * TAPS :].reshape(wide, channels)
    low = pre_ref[:PLANE] + jnp.dot(ends_ref[0], first, preferred_element_type=F32)
    high = pre_ref[inner:] + jnp.dot(ends_ref[1], final, preferred_element_type=F32)
    pre = jnp.concatenate([low, pre_ref[PLANE:inner], high], axis=0)
    mask = mask_ref[...].reshape(voxels, channels)
    logistic = 1.0 / (1.0 + jnp.exp(-pre))
    slope = logistic * (1.0 + pre * (1.0 - logistic)) * mask
    hidden = (pre / (1.0 + jnp.exp(-pre)) * mask).astype(BF16)

    logits = contract(head_ref[...], hidden, 1, 1)
    student = jnp.exp(logits)
    student = student / jnp.sum(student, axis=0, keepdims=True)
    target_sum, count = sums_ref[:classes], sums_ref[classes:]
    slope_logits = jnp.where(count > 0.0, count * student, 0.0) - target_sum
    heads = jnp.concatenate([head_ref[...]] * 3, axis=0)
    pieces = jnp.concatenate([piece.astype(F32) for piece in split3(slope_logits)], axis=0)
    dhidden = contract(pieces.T.astype(BF16), heads, 1, 0)
    gradient = dhidden * slope
    rounded = gradient.astype(BF16)
    grad_ref[...] = rounded.reshape(SIDE, PLANE, channels)
    low_y, high_y = y_faces(lambda x: gradient[x * PLANE : (x + 1) * PLANE])
    ends = gradient[:PLANE], gradient[voxels - PLANE :]
    pair_ref = send_ref.at[send_ref.shape[0] - PLANE :]
    store_faces(*ends, low_y, high_y, pair_ref, next_ref, edge_ref)

    def term(planes, gradient):
        return contract(planes.reshape(-1, wide), gradient, 0, 0).reshape(TAPS, channels, channels)

    terms_ref[:TAPS] = term(cols_ref[: SIDE - 1], rounded[PLANE:]) + term(
        ends_ref[0], rounded[:PLANE]
    )
    terms_ref[TAPS : 2 * TAPS] = term(cols_ref[...], rounded)
    terms_ref[2 * TAPS :] = term(cols_ref[1:], rounded[:inner]) + term(
        ends_ref[1], rounded[inner:]
    )
    length = channels // PARTS
    for r in range(PARTS):
        first = pl.multiple_of(part_index(r) * length, length)
        part = terms_ref[:, pl.ds(first, length), :].reshape(-1, channels)
        row = (r % (PARTS // 2)) * part.shape[0]
        if r < PARTS // 2:
            keep_ref[row : row + part.shape[0]] = part
        else:
            send_ref[row : row + part.shape[0]] = part.astype(BF16)


def lane_of(tx, ty):
    return (ty ^ (ty >> 1) ^ tx ^ (tx >> 1)) & 1


def part_index(r):
    tx, ty = lax.axis_index("tx"), lax.axis_index("ty")
    lane, across, along = lane_of(tx, ty) ^ (r >> 2), (ty >> 1) & 1, tx & 1
    first = jnp.where(lane == 0, across, along)
    second = jnp.where(lane == 0, along, across)
    return lane * 4 + ((first * 2 + second) ^ (r & 3))


def moved_weights(weight_ref, taps):
    return jnp.concatenate([weight_ref[3 * TAPS - 1 - tap] for tap in taps], axis=1)


def back_kernel(grad_ref, planes_ref, weight_ref, part_ref, cols_ref):
    channels = grad_ref.shape[2]
    edge = jnp.zeros((SIDE, channels), F32)
    for x in range(SIDE + 2):
        plane = planes_ref[0 if x == 0 else 1] if x in (0, SIDE + 1) else grad_ref[x - 1]
        write_columns(jnp.concatenate([edge, plane.astype(F32), edge], axis=0), cols_ref.at[x])
    total = jnp.zeros(part_ref.shape, F32)
    for dx in range(3):
        window = cols_ref[dx : dx + SIDE].reshape(-1, TAPS * channels)
        taps = range(TAPS * dx, TAPS * (dx + 1))
        total = total + contract(window, moved_weights(weight_ref, taps), 1, 1)
    part_ref[...] = total


def y_faces_kernel(extra_ref, part_ref, mask_ref, weight_ref, near_ref, far_ref, line_ref, out_ref, token_ref, cols_ref):
    channels, rows = part_ref.shape[1], (SIDE + 2) * SIDE
    tx, ty = lax.axis_index("tx"), lax.axis_index("ty")
    token_ref[...] = jnp.zeros(token_ref.shape, F32)
    by_first, by_second = far_ref[far_ref.shape[0] - rows :], line_ref[line_ref.shape[0] - rows :]
    other = jnp.where(lane_of(tx, ty) == 0, by_first.astype(F32), by_second.astype(F32))
    beyond = jnp.zeros(other.shape, F32) if extra_ref is None else extra_ref[...].astype(F32)
    other = jnp.where(((ty + 1) & 2) == 2, other, beyond)
    pair = near_ref[near_ref.shape[0] - rows :].astype(F32)
    even = parity("ty")
    added = []
    for dy, face in ((0, jnp.where(even, other, pair)), (2, jnp.where(even, pair, other))):
        write_columns(face, cols_ref)
        taps = [TAPS * dx + 3 * dy + dz for dx in range(3) for dz in range(3)]
        added.append(contract(cols_ref[...], moved_weights(weight_ref, taps), 1, 1))
    low, high = added
    rows = BY * SIDE
    for x in range(SIDE):
        here = slice(x * SIDE, (x + 1) * SIDE)
        total = part_ref[x * PLANE : (x + 1) * PLANE]
        first, final = total[:SIDE] + low[here], total[PLANE - SIDE :] + high[here]
        total = jnp.concatenate([first, total[SIDE : PLANE - SIDE], final], axis=0)
        total = (total * mask_ref[x]).astype(BF16)
        for j in range(GY):
            slot, a = x // BX * GY + j, x % BX
            out_ref[slot, a * rows : (a + 1) * rows, :] = total[j * rows : (j + 1) * rows]


def norm_kernel(near_ref, far_ref, got_near_ref, got_far_ref, token_ref, out_ref):
    del token_ref
    kernels, channels = out_ref.shape[0], out_ref.shape[2]
    length = channels // PARTS
    refs = (near_ref, far_ref, got_near_ref, got_far_ref)
    rows = kernels * length
    pieces = [ref.at[i * rows : (i + 1) * rows] for ref in refs for i in range(2)]
    squares = jnp.zeros((kernels * length, channels), F32)
    for piece in pieces:
        value = piece[...].astype(F32)
        squares = squares + value * value
    mean = jnp.sum(squares) / (kernels * channels * channels)
    scale = 1.0 / jnp.sqrt(jnp.broadcast_to(mean, (1, channels)) + 1e-06)
    for r, piece in enumerate(pieces):
        value = piece[...].astype(F32) * scale
        first = pl.multiple_of(part_index(r) * length, length)
        out_ref[:, pl.ds(first, length), :] = value.reshape(kernels, length, channels)


def swap_pairs(first, count):
    return [pair for i in range(first, count - 1, 2) for pair in ((i, i + 1), (i + 1, i))]


def swap_along_y(b, a):
    count = lax.axis_size("ty")
    got_b = lax.ppermute(b, "ty", swap_pairs(1, count))
    return got_b, lax.ppermute(a, "ty", swap_pairs(0, count))


def edge_faces(kernel, edges, faces, waits=()):
    face = shape(((SIDE + 2) * SIDE, edges.shape[2]), BF16)
    return pl.pallas_call(
        kernel,
        out_shape=(face, face, shape(edges.shape, BF16)),
        in_specs=vmem(1 + len(faces)) + [pl.BlockSpec(memory_space=pl.ANY)] * len(waits),
        out_specs=tuple(vmem(3)),
        compiler_params=pltpu.CompilerParams(vmem_limit_bytes=16 * 2**20),
        name="edge_faces",
    )(edges, *faces, *waits)


def exchange_with(value, partner):
    n_tx, n_ty = lax.axis_size("tx"), lax.axis_size("ty")
    pairs = []
    for tx in range(n_tx):
        for ty in range(n_ty):
            other = partner(tx, ty)
            if other is not None:
                pairs.append((tx * n_ty + ty, other[0] * n_ty + other[1]))
    return lax.ppermute(value, ("tx", "ty"), pairs)


def by_core(tx, ty):
    return tx, ty ^ 1


def same_lane(tx, ty, other_tx, other_ty):
    return other_tx, other_ty ^ lane_of(tx, ty) ^ lane_of(other_tx, other_ty)


def first_way(tx, ty):
    other = (tx, ty ^ 2) if lane_of(tx, ty) == 0 else (tx ^ 1, ty)
    return same_lane(tx, ty, *other)


def second_way(tx, ty):
    other = (tx ^ 1, ty) if lane_of(tx, ty) == 0 else (tx, ty ^ 2)
    return same_lane(tx, ty, *other)


def along_line(flips):
    return lambda tx, ty: same_lane(tx, ty, tx ^ (2 * flips[lane_of(tx, ty)]), ty)


def add(*terms):
    total = terms[0]
    for term in terms[1:]:
        total = total + term
    return total


def message(sections, waits=(), passes=()):
    arrays = []
    for _, _, *terms in sections:
        for array, _ in terms:
            if not any(array is known for known in arrays):
                arrays.append(array)
    place = [[next(i for i, x in enumerate(arrays) if x is array) for array, _ in terms] for _, _, *terms in sections]
    count, others = len(arrays), len(waits) + len(passes)
    total_rows = sum(section[0] for section in sections)

    def body(*refs):
        out_ref, row = refs[count + others], 0
        for places, (rows, fn, *terms) in zip(place, sections):
            values = [refs[i][first : first + rows].astype(F32) for i, (_, first) in zip(places, terms)]
            out_ref[row : row + rows] = fn(*values).astype(BF16)
            row += rows

    plain = pl.BlockSpec(memory_space=pl.ANY)
    outs = [shape((total_rows, arrays[0].shape[1]), BF16)]
    out, *passed = pl.pallas_call(
        body,
        out_shape=outs + [shape(x.shape, x.dtype) for x in passes],
        in_specs=vmem(count) + [plain] * others,
        out_specs=vmem(1) + [plain] * len(passes),
        input_output_aliases={count + len(waits) + i: 1 + i for i in range(len(passes))},
        compiler_params=pltpu.CompilerParams(vmem_limit_bytes=16 * 2**20),
        name="message",
    )(*arrays, *waits, *passes)
    return (out, *passed) if passes else out


def after(value, token):
    plain = pl.BlockSpec(memory_space=pl.ANY)
    return pl.pallas_call(
        lambda value_ref, token_ref, out_ref: None,
        out_shape=shape(value.shape, value.dtype),
        in_specs=[plain] * 2,
        out_specs=plain,
        input_output_aliases={0: 0},
        compiler_params=pltpu.CompilerParams(vmem_limit_bytes=16 * 2**20),
        name="after",
    )(value, token)


def on_device(features, occupancy, neighbors, point_voxel, conv_weight, head_weight, teacher):
    slots, brick, channels = features.shape
    kernels = conv_weight.shape[0]
    n_tx, n_ty = lax.axis_size("tx"), lax.axis_size("ty")
    edges = shape((2, PLANE, channels), BF16)
    ext = (SIDE + 2, (SIDE + 2) * SIDE, channels)
    grid = pltpu.VMEM(ext, F32)
    cols = pltpu.VMEM((SIDE + 2, PLANE, TAPS * channels), BF16)

    fetched = (features, occupancy)
    face = shape((PLANE, channels), BF16)
    planes = shape((SIDE, PLANE, channels), F32)
    y_b, y_a, x_ends, masked, mask = call(
        first_faces_kernel, (face, face, edges, planes, planes), fetched, buffers(*fetched),
        name="first_faces", fetched=2,
    )
    y_b, y_a = swap_along_y(y_b, y_a)
    wide_face = shape(((SIDE + 2) * SIDE, channels), BF16)
    x_pair, x_next = call(
        x_faces_kernel, (wide_face, wide_face), (x_ends, y_b, y_a), name="x_faces"
    )
    x_next = lax.ppermute(x_next, "tx", swap_pairs(1, n_tx))
    x_pair = lax.ppermute(x_pair, "tx", swap_pairs(0, n_tx))
    fetched = (point_voxel.reshape(1, -1), teacher, head_weight, conv_weight)
    tile_cols, pre, sums, head, weight = call(
        main_kernel,
        (
            shape((SIDE, PLANE, TAPS * channels), BF16),
            shape((SIDE * PLANE, channels), F32),
            shape((2 * head_weight.shape[0], SIDE * PLANE), F32),
            shape(head_weight.shape, BF16),
            shape(conv_weight.shape, BF16),
        ),
        (*fetched, masked, y_b, y_a),
        (*buffers(*fetched[:2])[:-1], pltpu.SemaphoreType.DMA((len(fetched),))),
        name="main",
        fetched=len(fetched),
    )
    part = kernels * channels // PARTS
    gradient, g_next, g_edges, keep, send = call(
        tile_kernel,
        (
            shape((SIDE, PLANE, channels), BF16),
            face,
            edges,
            shape((PARTS // 2 * part, channels), F32),
            shape((PARTS // 2 * part + PLANE, channels), BF16),
        ),
        (tile_cols, pre, mask, sums, head, weight, x_next, x_pair),
        (
            pltpu.VMEM((2, PLANE, TAPS * channels), BF16),
            pltpu.VMEM((kernels, channels, channels), F32),
        ),
        name="tile",
    )

    got0 = exchange_with(send, by_core)
    faces = [(PLANE, add, (got0, 4 * part)), (PLANE, add, (g_next, 0))]
    kept = [(2 * part, add, (keep, 2 * part), (got0, 2 * part))]
    got1 = exchange_with(message(kept + faces), first_way)
    kept = [(part, add, (keep, part), (got0, part), (got1, part))]
    got2 = exchange_with(message(kept + faces), second_way)
    at = (2 * part, part, part)
    hand_on = (PLANE, picked_face, (got1, at[0] + PLANE), (got2, at[1] + PLANE))
    total = [(part, add, (keep, 0), (got0, 0), (got1, 0), (got2, 0))]
    flips, lines = [], []
    while 2 ** len(flips) < n_tx // 2:
        flips.append(2 ** (len(flips) + 1) - 1)
    flips = list(zip(flips, flips[::-1]))
    for both in flips:
        own = message(total + [hand_on])
        lines.append(exchange_with(own, along_line(both)))
        total = [(part, add, (own, 0), (lines[-1], 0))]
        hand_on = (PLANE, add, (own, part))
    bit = 4
    while bit < n_ty:
        own = message(total)
        flip = 2 * bit - 4
        got = exchange_with(own, lambda tx, ty, flip=flip: same_lane(tx, ty, tx, ty ^ flip))
        total = [(part, add, (own, 0), (got, 0))]
        bit *= 2
    kernel = functools.partial(hand_on_edge_kernel, flips, at)
    g_a, g_b, planes = edge_faces(kernel, g_edges, (got1, got2, *lines))
    rows = g_a.shape[0]
    total = message(total + [(rows, add, (g_b, 0))])
    got3 = exchange_with(total, second_way)
    near = [(part, add, (total, 0)), (part, add, (got3, 0)), (rows, add, (g_b, 0))]
    near, gradient = message(near, (), (gradient,))
    far = exchange_with(near, first_way)
    back_part = call(
        back_kernel,
        shape((SIDE * PLANE, channels), F32),
        (gradient, planes, weight),
        (cols,),
        name="back",
    )
    got_near = exchange_with(
        message([(2 * part, add, (near, 0)), (rows, add, (g_a, 0))], (back_part,)), by_core
    )
    got_far = exchange_with(far, by_core)
    faces = (back_part, mask, weight, got_near, far, got3)
    kernel = functools.partial(y_faces_kernel, None)
    if n_ty > 4:
        pairs = [pair for i in range(3, n_ty - 1, 4) for pair in ((i, i + 1), (i + 1, i))]
        faces = (lax.ppermute(g_b, "ty", pairs), *faces)
        kernel = y_faces_kernel
    grad_features, token = call(
        kernel,
        (shape((slots, brick, channels), BF16), shape((8, channels), F32)),
        faces,
        (pltpu.VMEM((PLANE, TAPS * channels), BF16),),
        name="y_faces",
    )
    grad_weight = call(
        norm_kernel,
        shape((kernels, channels, channels), F32),
        (near, far, got_near, got_far, token),
        name="normalise",
    )
    return (grad_features, grad_weight)


def solution(mesh):
    in_specs = (
        P(("tx", "ty"), None, None),
        P(("tx", "ty"), None),
        P(None, ("tx", "ty")),
        P(("tx", "ty")),
        P(),
        P(),
        P(None, ("tx", "ty")),
    )
    out_specs = (P(("tx", "ty"), None, None), P())
    return jax.shard_map(
        on_device, mesh=mesh, in_specs=in_specs, out_specs=out_specs, check_vma=False
    )
```

```python
import functools

import jax
import jax.numpy as jnp
from jax import lax
from jax.experimental import pallas as pl
from jax.experimental.pallas import tpu as pltpu
from jax.sharding import PartitionSpec as P

GX = 2
GY = 2
BX = 4
BY = 4
SIDE = 8
PLANE = SIDE * SIDE
TAPS = 9
BF16 = jnp.bfloat16
F32 = jnp.float32
PARTS = 8


def vmem(count):
    return [pl.BlockSpec(memory_space=pltpu.VMEM)] * count


def pin(array):
    return pltpu.with_memory_space_constraint(array, pltpu.HBM)


def call(body, outs, inputs, scratch=(), limit=32 * 2**20, name=None, fetched=0):
    return pl.pallas_call(
        body,
        out_shape=outs,
        in_specs=[pl.BlockSpec(memory_space=pltpu.HBM)] * fetched + vmem(len(inputs) - fetched),
        out_specs=jax.tree.map(lambda _: pl.BlockSpec(memory_space=pltpu.VMEM), outs),
        scratch_shapes=list(scratch),
        compiler_params=pltpu.CompilerParams(vmem_limit_bytes=limit),
        name=name,
    )(*[pin(array) for array in inputs[:fetched]], *inputs[fetched:])


def buffers(*arrays):
    rooms = [pltpu.VMEM(array.shape, array.dtype) for array in arrays]
    return (*rooms, pltpu.SemaphoreType.DMA((len(arrays),)))


def fetch(sources, rooms, semaphores):
    copies = [
        pltpu.make_async_copy(source, room, semaphores.at[i])
        for i, (source, room) in enumerate(zip(sources, rooms))
    ]
    for copy in copies:
        copy.start()
    return copies


def shape(dims, dtype):
    return jax.ShapeDtypeStruct(dims, dtype)


def slot_planes(slot):
    return BX * (slot // GY), (slot % GY) * BY * SIDE


def parity(axis):
    return lax.rem(lax.axis_index(axis), 2) == 0


def occupancy_columns(occ_ref, rows):
    occ = occ_ref[...].astype(F32)
    padded = jnp.concatenate([occ, jnp.zeros((8 - occ.shape[0], occ.shape[1]), F32)], axis=0)
    return padded.T


def write_grid(grid_ref, planes):
    for x in range(SIDE):
        grid_ref[x + 1, SIDE : SIDE + PLANE, :] = planes(x)


def y_faces(planes):
    low = jnp.concatenate([planes(x)[:SIDE] for x in range(SIDE)], axis=0)
    high = jnp.concatenate([planes(x)[PLANE - SIDE :] for x in range(SIDE)], axis=0)
    return low, high


def store_faces(low_plane, high_plane, low_y, high_y, pair_ref, next_ref, edge_ref):
    even = parity("tx")
    pair_ref[...] = jnp.where(even, high_plane, low_plane).astype(BF16)
    next_ref[...] = jnp.where(even, low_plane, high_plane).astype(BF16)
    edge_ref[0] = low_y.astype(BF16)
    edge_ref[1] = high_y.astype(BF16)


def first_faces_kernel(
    feat_hbm, occ_hbm, b_ref, a_ref, ends_ref, masked_ref, mask_ref, feat_ref, occ_ref, semaphores
):
    for copy in fetch((feat_hbm, occ_hbm), (feat_ref, occ_ref), semaphores):
        copy.wait()
    columns = occupancy_columns(occ_ref, 8)
    rows, channels = BY * SIDE, mask_ref.shape[2]
    for slot in range(GX * GY):
        x0, row0 = slot_planes(slot)
        wide = jnp.broadcast_to(columns[:, slot : slot + 1], (columns.shape[0], channels))
        for a in range(BX):
            mask = wide[a * rows : (a + 1) * rows]
            part = feat_ref[slot, a * rows : (a + 1) * rows, :].astype(F32)
            mask_ref[x0 + a, row0 : row0 + rows, :] = mask
            masked_ref[x0 + a, row0 : row0 + rows, :] = part * mask
    low_y, high_y = y_faces(lambda x: masked_ref[x])
    even = parity("ty")
    a_ref[...] = jnp.where(even, high_y, low_y).astype(BF16)
    b_ref[...] = jnp.where(even, low_y, high_y).astype(BF16)
    ends_ref[0] = masked_ref[0].astype(BF16)
    ends_ref[1] = masked_ref[SIDE - 1].astype(BF16)


def halo_along_y(b_ref, a_ref):
    even = parity("ty")
    a, b = a_ref[...].astype(F32), b_ref[...].astype(F32)
    return jnp.where(even, b, a), jnp.where(even, a, b)


def x_faces_kernel(ends_ref, y_b_ref, y_a_ref, *refs):
    pair_ref, next_ref = refs[-2:]
    low, high = halo_along_y(y_b_ref, y_a_ref)
    last = PLANE - SIDE
    first = jnp.concatenate([low[:SIDE], ends_ref[0].astype(F32), high[:SIDE]], axis=0)
    final = jnp.concatenate([low[last:], ends_ref[1].astype(F32), high[last:]], axis=0)
    even = parity("tx")
    pair_ref[...] = jnp.where(even, final, first).astype(BF16)
    next_ref[...] = jnp.where(even, first, final).astype(BF16)


def store_edges(low, high, edge_ref, a_ref, b_ref, planes_ref):
    even_y = parity("ty")
    planes_ref[0] = low.astype(BF16)
    planes_ref[1] = high.astype(BF16)
    last = PLANE - SIDE
    bottom = jnp.concatenate([low[:SIDE], edge_ref[0].astype(F32), high[:SIDE]], axis=0)
    top = jnp.concatenate([low[last:], edge_ref[1].astype(F32), high[last:]], axis=0)
    a_ref[...] = jnp.where(even_y, top, bottom).astype(BF16)
    b_ref[...] = jnp.where(even_y, bottom, top).astype(BF16)


def hand_on_edge_kernel(flips, first_row, edge_ref, got1_ref, got2_ref, *refs):
    lines, (a_ref, b_ref, planes_ref) = refs[: len(flips)], refs[-3:]
    even = parity("tx")
    pair = picked_face(got1_ref[first_row[0] : first_row[0] + PLANE], got2_ref[first_row[1] : first_row[1] + PLANE])
    place = lax.axis_index("tx") // 2
    behind = jnp.where(even, place - 1, place + 1)
    other = jnp.zeros(pair.shape, F32)
    lane = lane_of(lax.axis_index("tx"), lax.axis_index("ty"))
    for both, line_ref in zip(flips, lines):
        flip = jnp.where(lane == 0, *both)
        face = line_ref[first_row[2] : first_row[2] + PLANE].astype(F32)
        other = jnp.where((place ^ behind) == flip, face, other)
    low, high = jnp.where(even, other, pair), jnp.where(even, pair, other)
    store_edges(low, high, edge_ref, a_ref, b_ref, planes_ref)


def picked_face(by_first_way, by_second_way):
    lane = lane_of(lax.axis_index("tx"), lax.axis_index("ty"))
    return jnp.where(lane == 0, by_second_way.astype(F32), by_first_way.astype(F32))


def write_columns(plane, cols_ref):
    channels = plane.shape[1]
    z = lax.broadcasted_iota(jnp.int32, plane.shape, 0) % SIDE
    zeros = jnp.zeros((1, channels), F32)
    before = jnp.where(z == 0, 0.0, jnp.concatenate([zeros, plane[:-1]], axis=0))
    after = jnp.where(z == SIDE - 1, 0.0, jnp.concatenate([plane[1:], zeros], axis=0))
    for dz, moved in enumerate((before, plane, after)):
        for dy in range(3):
            tap = 3 * dy + dz
            window = moved[dy * SIDE : dy * SIDE + PLANE]
            cols_ref[:, tap * channels : (tap + 1) * channels] = window.astype(BF16)


def split3(value):
    high = value.astype(BF16)
    rest = value - high.astype(F32)
    middle = rest.astype(BF16)
    low = (rest - middle.astype(F32)).astype(BF16)
    return high, middle, low


def contract(a, b, dim_a, dim_b):
    return lax.dot_general(a, b, (((dim_a,), (dim_b,)), ((), ())), preferred_element_type=F32)


def voxel_sums(point_ref, teach_ref):
    target = jnp.exp(teach_ref[...].astype(F32))
    target = target / jnp.sum(target, axis=0, keepdims=True)
    classes, points = target.shape
    place = point_ref[...]
    place = (place & 0x11F) | ((place & 0x80) >> 2) | ((place & 0x60) << 1)
    chosen = lax.broadcasted_iota(jnp.int32, (SIDE * PLANE, points), 0) == place
    chosen = jnp.where(chosen, 1.0, 0.0).astype(BF16)
    stack = jnp.concatenate([*split3(target), jnp.ones((classes, points), BF16)], axis=0)
    sums = contract(stack, chosen, 1, 1)
    target_sum = sums[:classes] + sums[classes : 2 * classes] + sums[2 * classes : 3 * classes]
    return jnp.concatenate([target_sum, sums[3 * classes :]], axis=0)


def main_kernel(
    point_hbm, teach_hbm, head_hbm, weight_hbm, masked_ref, y_b_ref, y_a_ref,
    cols_ref, pre_ref, sums_ref, head_ref, weight_ref,
    point_ref, teach_ref, semaphores,
):
    sources = (point_hbm, teach_hbm, head_hbm, weight_hbm)
    copies = fetch(sources, (point_ref, teach_ref, head_ref, weight_ref), semaphores)
    channels = masked_ref.shape[2]
    low, high = halo_along_y(y_b_ref, y_a_ref)
    for x in range(SIDE):
        rows = slice(x * SIDE, (x + 1) * SIDE)
        plane = jnp.concatenate([low[rows], masked_ref[x], high[rows]], axis=0)
        write_columns(plane, cols_ref.at[x])
    wide, inner = TAPS * channels, SIDE - 1
    for copy in copies[:2]:
        copy.wait()
    sums_ref[...] = voxel_sums(point_ref, teach_ref)
    for copy in copies[2:]:
        copy.wait()

    def product(planes, dx):
        window = cols_ref[planes].reshape(-1, wide)
        matrix = weight_ref[TAPS * dx : TAPS * (dx + 1)].reshape(wide, channels)
        return jnp.dot(window, matrix, preferred_element_type=F32)

    edge = jnp.zeros((PLANE, channels), F32)
    pre = product(slice(0, SIDE), 1)
    pre = pre + jnp.concatenate([edge, product(slice(0, inner), 0)], axis=0)
    pre_ref[...] = pre + jnp.concatenate([product(slice(1, SIDE), 2), edge], axis=0)


def tile_kernel(
    cols_ref, pre_ref, mask_ref, sums_ref, head_ref, weight_ref, x_next_ref, x_pair_ref,
    grad_ref, next_ref, edge_ref, keep_ref, first_ref, rest_ref,
    ends_ref, terms_ref,
):
    channels = cols_ref.shape[2] // TAPS
    classes = head_ref.shape[0]
    voxels, wide, inner = SIDE * PLANE, TAPS * channels, (SIDE - 1) * PLANE
    even = parity("tx")
    pair, other = x_pair_ref[...].astype(F32), x_next_ref[...].astype(F32)
    write_columns(jnp.where(even, other, pair), ends_ref.at[0])
    write_columns(jnp.where(even, pair, other), ends_ref.at[1])
    first = weight_ref[:TAPS].reshape(wide, channels)
    final = weight_ref[2 * TAPS :].reshape(wide, channels)
    low = pre_ref[:PLANE] + jnp.dot(ends_ref[0], first, preferred_element_type=F32)
    high = pre_ref[inner:] + jnp.dot(ends_ref[1], final, preferred_element_type=F32)
    pre = jnp.concatenate([low, pre_ref[PLANE:inner], high], axis=0)
    mask = mask_ref[...].reshape(voxels, channels)
    logistic = 1.0 / (1.0 + jnp.exp(-pre))
    slope = logistic * (1.0 + pre * (1.0 - logistic)) * mask
    hidden = (pre / (1.0 + jnp.exp(-pre)) * mask).astype(BF16)

    logits = contract(head_ref[...], hidden, 1, 1)
    student = jnp.exp(logits)
    student = student / jnp.sum(student, axis=0, keepdims=True)
    target_sum, count = sums_ref[:classes], sums_ref[classes:]
    slope_logits = jnp.where(count > 0.0, count * student, 0.0) - target_sum
    heads = jnp.concatenate([head_ref[...]] * 3, axis=0)
    pieces = jnp.concatenate([piece.astype(F32) for piece in split3(slope_logits)], axis=0)
    dhidden = contract(pieces.T.astype(BF16), heads, 1, 0)
    gradient = dhidden * slope
    rounded = gradient.astype(BF16)
    grad_ref[...] = rounded.reshape(SIDE, PLANE, channels)
    low_y, high_y = y_faces(lambda x: gradient[x * PLANE : (x + 1) * PLANE])
    ends = gradient[:PLANE], gradient[voxels - PLANE :]
    pair_ref = rest_ref.at[rest_ref.shape[0] - PLANE :]
    store_faces(*ends, low_y, high_y, pair_ref, next_ref, edge_ref)

    def term(planes, gradient):
        return contract(planes.reshape(-1, wide), gradient, 0, 0)

    terms_ref[:wide] = term(cols_ref[: SIDE - 1], rounded[PLANE:]) + term(
        ends_ref[0], rounded[:PLANE]
    )
    terms_ref[wide : 2 * wide] = term(cols_ref[...], rounded)
    terms_ref[2 * wide :] = term(cols_ref[1:], rounded[:inner]) + term(
        ends_ref[1], rounded[inner:]
    )
    length = terms_ref.shape[0] // PARTS
    for r in range(PARTS):
        part = terms_ref[pl.ds(pl.multiple_of(part_index(r) * length, 16), length)]
        row = (r % 2) * length
        if r < PARTS // 2:
            keep_ref[r * length : (r + 1) * length] = part
        else:
            send_ref = rest_ref if r < PARTS - 2 else first_ref
            send_ref[row : row + length] = part.astype(BF16)


def lane_of(tx, ty):
    return (ty ^ (ty >> 1) ^ tx ^ (tx >> 1)) & 1


def part_index(r):
    tx, ty = lax.axis_index("tx"), lax.axis_index("ty")
    lane, across, along = lane_of(tx, ty) ^ (r >> 2), (ty >> 1) & 1, tx & 1
    first = jnp.where(lane == 0, across, along)
    second = jnp.where(lane == 0, along, across)
    return lane * 4 + ((first * 2 + second) ^ (r & 3))


def moved_weights(weight_ref, taps):
    return jnp.concatenate([weight_ref[3 * TAPS - 1 - tap] for tap in taps], axis=1)


def back_kernel(grad_ref, planes_ref, weight_ref, part_ref, cols_ref):
    channels = grad_ref.shape[2]
    edge = jnp.zeros((SIDE, channels), F32)
    for x in range(SIDE + 2):
        plane = planes_ref[0 if x == 0 else 1] if x in (0, SIDE + 1) else grad_ref[x - 1]
        write_columns(jnp.concatenate([edge, plane.astype(F32), edge], axis=0), cols_ref.at[x])
    total = jnp.zeros(part_ref.shape, F32)
    for dx in range(3):
        window = cols_ref[dx : dx + SIDE].reshape(-1, TAPS * channels)
        taps = range(TAPS * dx, TAPS * (dx + 1))
        total = total + contract(window, moved_weights(weight_ref, taps), 1, 1)
    part_ref[...] = total


def squares(ref, rows):
    value = ref[:rows].astype(F32)
    return jnp.sum(value * value, axis=0, keepdims=True)


def y_faces_kernel(
    extra_ref, part_ref, mask_ref, weight_ref, near_ref, far_ref, line_ref, *refs
):
    pieces, (out_ref, squares_ref, cols_ref) = refs[:-3], refs[-3:]
    channels, rows = part_ref.shape[1], (SIDE + 2) * SIDE
    tx, ty = lax.axis_index("tx"), lax.axis_index("ty")
    total = sum(squares(ref, near_ref.shape[0] - rows) for ref in pieces)
    squares_ref[...] = jnp.broadcast_to(total, squares_ref.shape)
    by_first, by_second = far_ref[far_ref.shape[0] - rows :], line_ref[line_ref.shape[0] - rows :]
    other = jnp.where(lane_of(tx, ty) == 0, by_first.astype(F32), by_second.astype(F32))
    beyond = jnp.zeros(other.shape, F32) if extra_ref is None else extra_ref[...].astype(F32)
    other = jnp.where(((ty + 1) & 2) == 2, other, beyond)
    pair = near_ref[near_ref.shape[0] - rows :].astype(F32)
    even = parity("ty")
    added = []
    for dy, face in ((0, jnp.where(even, other, pair)), (2, jnp.where(even, pair, other))):
        write_columns(face, cols_ref)
        taps = [TAPS * dx + 3 * dy + dz for dx in range(3) for dz in range(3)]
        added.append(contract(cols_ref[...], moved_weights(weight_ref, taps), 1, 1))
    low, high = added
    rows = BY * SIDE
    for x in range(SIDE):
        here = slice(x * SIDE, (x + 1) * SIDE)
        total = part_ref[x * PLANE : (x + 1) * PLANE]
        first, final = total[:SIDE] + low[here], total[PLANE - SIDE :] + high[here]
        total = jnp.concatenate([first, total[SIDE : PLANE - SIDE], final], axis=0)
        total = (total * mask_ref[x]).astype(BF16)
        for j in range(GY):
            slot, a = x // BX * GY + j, x % BX
            out_ref[slot, a * rows : (a + 1) * rows, :] = total[j * rows : (j + 1) * rows]


def norm_kernel(*refs):
    pieces, refs = refs[:PARTS], refs[PARTS:]
    squares_ref, grad_ref, out_hbm, grad_hbm, out_ref, semaphores = refs
    copies = [pltpu.make_async_copy(grad_ref, grad_hbm, semaphores.at[PARTS])]
    copies[0].start()
    rows, channels = out_ref.shape[1:]
    total = squares_ref[:1] + squares(pieces[-1], rows)
    mean = jnp.sum(total, axis=1, keepdims=True) / (PARTS * rows * channels)
    scale = jnp.broadcast_to(1.0 / jnp.sqrt(mean + 1e-06), (1, channels))
    for r, piece in enumerate(pieces):
        out_ref[r] = piece[:rows].astype(F32) * scale
        first = pl.multiple_of(part_index(r) * rows, 16)
        target = out_hbm.at[pl.ds(first, rows)]
        copies.append(pltpu.make_async_copy(out_ref.at[r], target, semaphores.at[r]))
        copies[-1].start()
    for copy in copies:
        copy.wait()


def swap_pairs(first, count):
    return [pair for i in range(first, count - 1, 2) for pair in ((i, i + 1), (i + 1, i))]


def swap_along_y(b, a):
    count = lax.axis_size("ty")
    got_b = lax.ppermute(b, "ty", swap_pairs(1, count))
    return got_b, lax.ppermute(a, "ty", swap_pairs(0, count))


def edge_faces(kernel, edges, faces, waits=()):
    face = shape(((SIDE + 2) * SIDE, edges.shape[2]), BF16)
    return pl.pallas_call(
        kernel,
        out_shape=(face, face, shape(edges.shape, BF16)),
        in_specs=vmem(1 + len(faces)) + [pl.BlockSpec(memory_space=pl.ANY)] * len(waits),
        out_specs=tuple(vmem(3)),
        compiler_params=pltpu.CompilerParams(vmem_limit_bytes=16 * 2**20),
        name="edge_faces",
    )(edges, *faces, *waits)


def exchange_with(value, partner):
    n_tx, n_ty = lax.axis_size("tx"), lax.axis_size("ty")
    pairs = []
    for tx in range(n_tx):
        for ty in range(n_ty):
            other = partner(tx, ty)
            if other is not None:
                pairs.append((tx * n_ty + ty, other[0] * n_ty + other[1]))
    return lax.ppermute(value, ("tx", "ty"), pairs)


def by_core(tx, ty):
    return tx, ty ^ 1


def same_lane(tx, ty, other_tx, other_ty):
    return other_tx, other_ty ^ lane_of(tx, ty) ^ lane_of(other_tx, other_ty)


def first_way(tx, ty):
    other = (tx, ty ^ 2) if lane_of(tx, ty) == 0 else (tx ^ 1, ty)
    return same_lane(tx, ty, *other)


def second_way(tx, ty):
    other = (tx ^ 1, ty) if lane_of(tx, ty) == 0 else (tx, ty ^ 2)
    return same_lane(tx, ty, *other)


def along_line(flips):
    return lambda tx, ty: same_lane(tx, ty, tx ^ (2 * flips[lane_of(tx, ty)]), ty)


def add(*terms):
    total = terms[0]
    for term in terms[1:]:
        total = total + term
    return total


def message(sections, waits=(), passes=()):
    arrays = []
    for _, _, *terms in sections:
        for array, _ in terms:
            if not any(array is known for known in arrays):
                arrays.append(array)
    place = [[next(i for i, x in enumerate(arrays) if x is array) for array, _ in terms] for _, _, *terms in sections]
    count, others = len(arrays), len(waits) + len(passes)
    total_rows = sum(section[0] for section in sections)

    def body(*refs):
        out_ref, row = refs[count + others], 0
        for places, (rows, fn, *terms) in zip(place, sections):
            values = [refs[i][first : first + rows].astype(F32) for i, (_, first) in zip(places, terms)]
            out_ref[row : row + rows] = fn(*values).astype(BF16)
            row += rows

    plain = pl.BlockSpec(memory_space=pl.ANY)
    outs = [shape((total_rows, arrays[0].shape[1]), BF16)]
    out, *passed = pl.pallas_call(
        body,
        out_shape=outs + [shape(x.shape, x.dtype) for x in passes],
        in_specs=vmem(count) + [plain] * others,
        out_specs=vmem(1) + [plain] * len(passes),
        input_output_aliases={count + len(waits) + i: 1 + i for i in range(len(passes))},
        compiler_params=pltpu.CompilerParams(vmem_limit_bytes=16 * 2**20),
        name="message",
    )(*arrays, *waits, *passes)
    return (out, *passed) if passes else out


def after(value, token):
    plain = pl.BlockSpec(memory_space=pl.ANY)
    return pl.pallas_call(
        lambda value_ref, token_ref, out_ref: None,
        out_shape=shape(value.shape, value.dtype),
        in_specs=[plain] * 2,
        out_specs=plain,
        input_output_aliases={0: 0},
        compiler_params=pltpu.CompilerParams(vmem_limit_bytes=16 * 2**20),
        name="after",
    )(value, token)


def on_device(features, occupancy, neighbors, point_voxel, conv_weight, head_weight, teacher):
    slots, brick, channels = features.shape
    kernels = conv_weight.shape[0]
    n_tx, n_ty = lax.axis_size("tx"), lax.axis_size("ty")
    edges = shape((2, PLANE, channels), BF16)
    ext = (SIDE + 2, (SIDE + 2) * SIDE, channels)
    grid = pltpu.VMEM(ext, F32)
    cols = pltpu.VMEM((SIDE + 2, PLANE, TAPS * channels), BF16)

    fetched = (features, occupancy)
    face = shape((PLANE, channels), BF16)
    planes = shape((SIDE, PLANE, channels), F32)
    y_b, y_a, x_ends, masked, mask = call(
        first_faces_kernel, (face, face, edges, planes, planes), fetched, buffers(*fetched),
        name="first_faces", fetched=2,
    )
    y_b, y_a = swap_along_y(y_b, y_a)
    wide_face = shape(((SIDE + 2) * SIDE, channels), BF16)
    x_pair, x_next = call(
        x_faces_kernel, (wide_face, wide_face), (x_ends, y_b, y_a), name="x_faces"
    )
    x_next = lax.ppermute(x_next, "tx", swap_pairs(1, n_tx))
    x_pair = lax.ppermute(x_pair, "tx", swap_pairs(0, n_tx))
    fetched = (point_voxel.reshape(1, -1), teacher, head_weight, conv_weight)
    tile_cols, pre, sums, head, weight = call(
        main_kernel,
        (
            shape((SIDE, PLANE, TAPS * channels), BF16),
            shape((SIDE * PLANE, channels), F32),
            shape((2 * head_weight.shape[0], SIDE * PLANE), F32),
            shape(head_weight.shape, BF16),
            shape(conv_weight.shape, BF16),
        ),
        (*fetched, masked, y_b, y_a),
        (*buffers(*fetched[:2])[:-1], pltpu.SemaphoreType.DMA((len(fetched),))),
        name="main",
        fetched=len(fetched),
    )
    part = kernels * channels // PARTS
    gradient, g_next, g_edges, keep, first, rest = call(
        tile_kernel,
        (
            shape((SIDE, PLANE, channels), BF16),
            face,
            edges,
            shape((PARTS // 2 * part, channels), F32),
            shape((2 * part, channels), BF16),
            shape((2 * part + PLANE, channels), BF16),
        ),
        (tile_cols, pre, mask, sums, head, weight, x_next, x_pair),
        (
            pltpu.VMEM((2, PLANE, TAPS * channels), BF16),
            pltpu.VMEM((kernels * channels, channels), F32),
        ),
        name="tile",
    )

    got_first = exchange_with(first, by_core)
    got_rest = exchange_with(rest, by_core)
    onward = message([(part, add, (keep, 3 * part), (got_first, part))])
    got_onward = exchange_with(onward, first_way)
    faces = [(PLANE, add, (got_rest, 2 * part)), (PLANE, add, (g_next, 0))]
    got1 = exchange_with(
        message([(part, add, (keep, 2 * part), (got_first, 0)), *faces]), first_way
    )
    kept = [(part, add, (keep, part), (got_rest, part), (got_onward, 0))]
    got2 = exchange_with(message(kept + faces), second_way)
    at = (part, part, part)
    hand_on = (PLANE, picked_face, (got1, part + PLANE), (got2, part + PLANE))
    total = [(part, add, (keep, 0), (got_rest, 0), (got1, 0), (got2, 0))]
    flips, lines = [], []
    while 2 ** len(flips) < n_tx // 2:
        flips.append(2 ** (len(flips) + 1) - 1)
    flips = list(zip(flips, flips[::-1]))
    for both in flips:
        own = message(total + [hand_on])
        lines.append(exchange_with(own, along_line(both)))
        total = [(part, add, (own, 0), (lines[-1], 0))]
        hand_on = (PLANE, add, (own, part))
    bit = 4
    while bit < n_ty:
        own = message(total)
        flip = 2 * bit - 4
        got = exchange_with(own, lambda tx, ty, flip=flip: same_lane(tx, ty, tx, ty ^ flip))
        total = [(part, add, (own, 0), (got, 0))]
        bit *= 2
    kernel = functools.partial(hand_on_edge_kernel, flips, at)
    g_a, g_b, planes = edge_faces(kernel, g_edges, (got1, got2, *lines))
    rows = g_a.shape[0]
    total = message(total + [(rows, add, (g_b, 0))])
    piece1 = exchange_with(total, second_way)
    piece2 = exchange_with(total, first_way)
    onward, gradient = message([(part, add, (piece1, 0))], (), (gradient,))
    piece3 = exchange_with(onward, first_way)
    back_part = call(
        back_kernel,
        shape((SIDE * PLANE, channels), F32),
        (gradient, planes, weight),
        (cols,),
        name="back",
    )
    near = message([(part, add, (piece2, 0)), (rows, add, (g_a, 0))], (back_part,))
    pieces = (total, piece1, near, piece3)
    others = [exchange_with(piece, by_core) for piece in pieces]
    faces = (back_part, mask, weight, others[2], piece2, piece1, *pieces, *others[:3])
    kernel = functools.partial(y_faces_kernel, None)
    if n_ty > 4:
        pairs = [pair for i in range(3, n_ty - 1, 4) for pair in ((i, i + 1), (i + 1, i))]
        faces = (lax.ppermute(g_b, "ty", pairs), *faces)
        kernel = y_faces_kernel
    grad_features, squares_of = call(
        kernel,
        (shape((slots, brick, channels), BF16), shape((8, channels), F32)),
        faces,
        (pltpu.VMEM((PLANE, TAPS * channels), BF16),),
        name="y_faces",
    )
    grad_weight, grad_features = pl.pallas_call(
        norm_kernel,
        out_shape=(
            shape((kernels * channels, channels), F32),
            shape((slots, brick, channels), BF16),
        ),
        in_specs=vmem(PARTS + 2),
        out_specs=(pl.BlockSpec(memory_space=pltpu.HBM),) * 2,
        scratch_shapes=[
            pltpu.VMEM((PARTS, part, channels), F32),
            pltpu.SemaphoreType.DMA((PARTS + 1,)),
        ],
        compiler_params=pltpu.CompilerParams(vmem_limit_bytes=16 * 2**20),
        name="normalise",
    )(*pieces, *others, squares_of, grad_features)
    return (grad_features, grad_weight.reshape(conv_weight.shape))


def solution(mesh):
    in_specs = (
        P(("tx", "ty"), None, None),
        P(("tx", "ty"), None),
        P(None, ("tx", "ty")),
        P(("tx", "ty")),
        P(),
        P(),
        P(None, ("tx", "ty")),
    )
    out_specs = (P(("tx", "ty"), None, None), P())
    return jax.shard_map(
        on_device, mesh=mesh, in_specs=in_specs, out_specs=out_specs, check_vma=False
    )
```

```python
import functools

import jax
import jax.numpy as jnp
from jax import lax
from jax.experimental import pallas as pl
from jax.experimental.pallas import tpu as pltpu
from jax.sharding import PartitionSpec as P

GX = 2
GY = 2
BX = 4
BY = 4
SIDE = 8
PLANE = SIDE * SIDE
TAPS = 9
BF16 = jnp.bfloat16
F32 = jnp.float32
PARTS = 8


def vmem(count):
    return [pl.BlockSpec(memory_space=pltpu.VMEM)] * count


def pin(array):
    return pltpu.with_memory_space_constraint(array, pltpu.HBM)


def call(body, outs, inputs, scratch=(), limit=32 * 2**20, name=None, fetched=0):
    return pl.pallas_call(
        body,
        out_shape=outs,
        in_specs=[pl.BlockSpec(memory_space=pltpu.HBM)] * fetched + vmem(len(inputs) - fetched),
        out_specs=jax.tree.map(lambda _: pl.BlockSpec(memory_space=pltpu.VMEM), outs),
        scratch_shapes=list(scratch),
        compiler_params=pltpu.CompilerParams(vmem_limit_bytes=limit),
        name=name,
    )(*[pin(array) for array in inputs[:fetched]], *inputs[fetched:])


def buffers(*arrays):
    rooms = [pltpu.VMEM(array.shape, array.dtype) for array in arrays]
    return (*rooms, pltpu.SemaphoreType.DMA((len(arrays),)))


def fetch(sources, rooms, semaphores):
    copies = [
        pltpu.make_async_copy(source, room, semaphores.at[i])
        for i, (source, room) in enumerate(zip(sources, rooms))
    ]
    for copy in copies:
        copy.start()
    return copies


def shape(dims, dtype):
    return jax.ShapeDtypeStruct(dims, dtype)


def slot_planes(slot):
    return BX * (slot // GY), (slot % GY) * BY * SIDE


def parity(axis):
    return lax.rem(lax.axis_index(axis), 2) == 0


def occupancy_columns(occ_ref, rows):
    occ = occ_ref[...].astype(F32)
    padded = jnp.concatenate([occ, jnp.zeros((8 - occ.shape[0], occ.shape[1]), F32)], axis=0)
    return padded.T


def write_grid(grid_ref, planes):
    for x in range(SIDE):
        grid_ref[x + 1, SIDE : SIDE + PLANE, :] = planes(x)


def y_faces(planes):
    low = jnp.concatenate([planes(x)[:SIDE] for x in range(SIDE)], axis=0)
    high = jnp.concatenate([planes(x)[PLANE - SIDE :] for x in range(SIDE)], axis=0)
    return low, high


def store_faces(low_plane, high_plane, low_y, high_y, pair_ref, next_ref, edge_ref):
    even = parity("tx")
    pair_ref[...] = jnp.where(even, high_plane, low_plane).astype(BF16)
    next_ref[...] = jnp.where(even, low_plane, high_plane).astype(BF16)
    edge_ref[0] = low_y.astype(BF16)
    edge_ref[1] = high_y.astype(BF16)


def first_faces_kernel(
    feat_hbm, occ_hbm, b_ref, a_ref, ends_ref, masked_ref, mask_ref, feat_ref, occ_ref, semaphores
):
    for copy in fetch((feat_hbm, occ_hbm), (feat_ref, occ_ref), semaphores):
        copy.wait()
    columns = occupancy_columns(occ_ref, 8)
    rows, channels = BY * SIDE, mask_ref.shape[2]
    for slot in range(GX * GY):
        x0, row0 = slot_planes(slot)
        wide = jnp.broadcast_to(columns[:, slot : slot + 1], (columns.shape[0], channels))
        for a in range(BX):
            mask = wide[a * rows : (a + 1) * rows]
            part = feat_ref[slot, a * rows : (a + 1) * rows, :].astype(F32)
            mask_ref[x0 + a, row0 : row0 + rows, :] = mask
            masked_ref[x0 + a, row0 : row0 + rows, :] = part * mask
    low_y, high_y = y_faces(lambda x: masked_ref[x])
    even = parity("ty")
    a_ref[...] = jnp.where(even, high_y, low_y).astype(BF16)
    b_ref[...] = jnp.where(even, low_y, high_y).astype(BF16)
    ends_ref[0] = masked_ref[0].astype(BF16)
    ends_ref[1] = masked_ref[SIDE - 1].astype(BF16)


def halo_along_y(b_ref, a_ref):
    even = parity("ty")
    a, b = a_ref[...].astype(F32), b_ref[...].astype(F32)
    return jnp.where(even, b, a), jnp.where(even, a, b)


def x_faces_kernel(ends_ref, y_b_ref, y_a_ref, *refs):
    pair_ref, next_ref = refs[-2:]
    low, high = halo_along_y(y_b_ref, y_a_ref)
    last = PLANE - SIDE
    first = jnp.concatenate([low[:SIDE], ends_ref[0].astype(F32), high[:SIDE]], axis=0)
    final = jnp.concatenate([low[last:], ends_ref[1].astype(F32), high[last:]], axis=0)
    even = parity("tx")
    pair_ref[...] = jnp.where(even, final, first).astype(BF16)
    next_ref[...] = jnp.where(even, first, final).astype(BF16)


def store_edges(low, high, edge_ref, a_ref, b_ref, planes_ref):
    even_y = parity("ty")
    planes_ref[0] = low.astype(BF16)
    planes_ref[1] = high.astype(BF16)
    last = PLANE - SIDE
    bottom = jnp.concatenate([low[:SIDE], edge_ref[0].astype(F32), high[:SIDE]], axis=0)
    top = jnp.concatenate([low[last:], edge_ref[1].astype(F32), high[last:]], axis=0)
    a_ref[...] = jnp.where(even_y, top, bottom).astype(BF16)
    b_ref[...] = jnp.where(even_y, bottom, top).astype(BF16)


def hand_on_edge_kernel(flips, first_row, edge_ref, got1_ref, got2_ref, *refs):
    lines, (a_ref, b_ref, planes_ref) = refs[: len(flips)], refs[-3:]
    even = parity("tx")
    pair = picked_face(got1_ref[first_row[0] : first_row[0] + PLANE], got2_ref[first_row[1] : first_row[1] + PLANE])
    place = lax.axis_index("tx") // 2
    behind = jnp.where(even, place - 1, place + 1)
    other = jnp.zeros(pair.shape, F32)
    lane = lane_of(lax.axis_index("tx"), lax.axis_index("ty"))
    for both, line_ref in zip(flips, lines):
        flip = jnp.where(lane == 0, *both)
        face = line_ref[first_row[2] : first_row[2] + PLANE].astype(F32)
        other = jnp.where((place ^ behind) == flip, face, other)
    low, high = jnp.where(even, other, pair), jnp.where(even, pair, other)
    store_edges(low, high, edge_ref, a_ref, b_ref, planes_ref)


def picked_face(by_first_way, by_second_way):
    lane = lane_of(lax.axis_index("tx"), lax.axis_index("ty"))
    return jnp.where(lane == 0, by_second_way.astype(F32), by_first_way.astype(F32))


def write_columns(plane, cols_ref):
    channels = plane.shape[1]
    z = lax.broadcasted_iota(jnp.int32, plane.shape, 0) % SIDE
    zeros = jnp.zeros((1, channels), F32)
    before = jnp.where(z == 0, 0.0, jnp.concatenate([zeros, plane[:-1]], axis=0))
    after = jnp.where(z == SIDE - 1, 0.0, jnp.concatenate([plane[1:], zeros], axis=0))
    for dz, moved in enumerate((before, plane, after)):
        for dy in range(3):
            tap = 3 * dy + dz
            window = moved[dy * SIDE : dy * SIDE + PLANE]
            cols_ref[:, tap * channels : (tap + 1) * channels] = window.astype(BF16)


def split3(value):
    high = value.astype(BF16)
    rest = value - high.astype(F32)
    middle = rest.astype(BF16)
    low = (rest - middle.astype(F32)).astype(BF16)
    return high, middle, low


def contract(a, b, dim_a, dim_b):
    return lax.dot_general(a, b, (((dim_a,), (dim_b,)), ((), ())), preferred_element_type=F32)


def voxel_sums(point_ref, teach_ref):
    target = jnp.exp(teach_ref[...].astype(F32))
    target = target / jnp.sum(target, axis=0, keepdims=True)
    classes, points = target.shape
    place = point_ref[...]
    place = (place & 0x11F) | ((place & 0x80) >> 2) | ((place & 0x60) << 1)
    chosen = lax.broadcasted_iota(jnp.int32, (SIDE * PLANE, points), 0) == place
    chosen = jnp.where(chosen, 1.0, 0.0).astype(BF16)
    stack = jnp.concatenate([*split3(target), jnp.ones((classes, points), BF16)], axis=0)
    sums = contract(stack, chosen, 1, 1)
    target_sum = sums[:classes] + sums[classes : 2 * classes] + sums[2 * classes : 3 * classes]
    return jnp.concatenate([target_sum, sums[3 * classes :]], axis=0)


def main_kernel(
    point_hbm, teach_hbm, head_hbm, weight_hbm, masked_ref, y_b_ref, y_a_ref,
    cols_ref, pre_ref, sums_ref, head_ref, weight_ref,
    point_ref, teach_ref, semaphores,
):
    sources = (point_hbm, teach_hbm, head_hbm, weight_hbm)
    copies = fetch(sources, (point_ref, teach_ref, head_ref, weight_ref), semaphores)
    channels = masked_ref.shape[2]
    low, high = halo_along_y(y_b_ref, y_a_ref)
    for x in range(SIDE):
        rows = slice(x * SIDE, (x + 1) * SIDE)
        plane = jnp.concatenate([low[rows], masked_ref[x], high[rows]], axis=0)
        write_columns(plane, cols_ref.at[x])
    wide, inner = TAPS * channels, SIDE - 1
    for copy in copies[:2]:
        copy.wait()
    sums_ref[...] = voxel_sums(point_ref, teach_ref)
    for copy in copies[2:]:
        copy.wait()

    def product(planes, dx):
        window = cols_ref[planes].reshape(-1, wide)
        matrix = weight_ref[TAPS * dx : TAPS * (dx + 1)].reshape(wide, channels)
        return jnp.dot(window, matrix, preferred_element_type=F32)

    edge = jnp.zeros((PLANE, channels), F32)
    pre = product(slice(0, SIDE), 1)
    pre = pre + jnp.concatenate([edge, product(slice(0, inner), 0)], axis=0)
    pre_ref[...] = pre + jnp.concatenate([product(slice(1, SIDE), 2), edge], axis=0)


def write_terms(cols_ref, ends_ref, gradient, start, stop, terms_ref, first=0):
    channels = gradient.shape[1]
    inner = (SIDE - 1) * PLANE
    for dx in range(3):
        low, high = max(start, TAPS * dx), min(stop, TAPS * (dx + 1))
        if low >= high:
            continue
        lanes = slice((low - TAPS * dx) * channels, (high - TAPS * dx) * channels)

        def term(planes, gradient):
            return contract(planes.reshape(gradient.shape[0], -1), gradient, 0, 0)

        if dx == 0:
            total = term(cols_ref[: SIDE - 1, :, lanes], gradient[PLANE:])
            total = total + term(ends_ref[0, :, lanes], gradient[:PLANE])
        elif dx == 1:
            total = term(cols_ref[:, :, lanes], gradient)
        else:
            total = term(cols_ref[1:, :, lanes], gradient[:inner])
            total = total + term(ends_ref[1, :, lanes], gradient[inner:])
        terms_ref[(low - first) * channels : (high - first) * channels] = total


def for_quarter(body):
    for i in range(PARTS // 2):
        pl.when((part_index(PARTS - 2) >> 1) == i)(functools.partial(body, i))


def tile_kernel(
    cols_ref, pre_ref, mask_ref, sums_ref, head_ref, weight_ref, x_next_ref, x_pair_ref,
    grad_ref, ends_ref, first_ref,
    terms_ref,
):
    channels = cols_ref.shape[2] // TAPS
    classes = head_ref.shape[0]
    voxels, wide, inner = SIDE * PLANE, TAPS * channels, (SIDE - 1) * PLANE
    even = parity("tx")
    pair, other = x_pair_ref[...].astype(F32), x_next_ref[...].astype(F32)
    write_columns(jnp.where(even, other, pair), ends_ref.at[0])
    write_columns(jnp.where(even, pair, other), ends_ref.at[1])
    first = weight_ref[:TAPS].reshape(wide, channels)
    final = weight_ref[2 * TAPS :].reshape(wide, channels)
    low = pre_ref[:PLANE] + jnp.dot(ends_ref[0], first, preferred_element_type=F32)
    high = pre_ref[inner:] + jnp.dot(ends_ref[1], final, preferred_element_type=F32)
    pre = jnp.concatenate([low, pre_ref[PLANE:inner], high], axis=0)
    mask = mask_ref[...].reshape(voxels, channels)
    logistic = 1.0 / (1.0 + jnp.exp(-pre))
    slope = logistic * (1.0 + pre * (1.0 - logistic)) * mask
    hidden = (pre / (1.0 + jnp.exp(-pre)) * mask).astype(BF16)

    logits = contract(head_ref[...], hidden, 1, 1)
    student = jnp.exp(logits)
    student = student / jnp.sum(student, axis=0, keepdims=True)
    target_sum, count = sums_ref[:classes], sums_ref[classes:]
    slope_logits = jnp.where(count > 0.0, count * student, 0.0) - target_sum
    heads = jnp.concatenate([head_ref[...]] * 3, axis=0)
    pieces = jnp.concatenate([piece.astype(F32) for piece in split3(slope_logits)], axis=0)
    dhidden = contract(pieces.T.astype(BF16), heads, 1, 0)
    rounded = (dhidden * slope).astype(BF16)
    grad_ref[...] = rounded.reshape(SIDE, PLANE, channels)
    length = first_ref.shape[0] // 2

    def parts(i):
        start = 2 * length * i // channels
        stop = -(-2 * length * (i + 1) // channels)
        write_terms(cols_ref, ends_ref, rounded, start, stop, terms_ref, start)
        for r in range(2):
            row = 2 * length * i - start * channels + (part_index(PARTS - 2 + r) & 1) * length
            part = terms_ref[pl.ds(pl.multiple_of(row, 16), length)]
            first_ref[r * length : (r + 1) * length] = part.astype(BF16)

    for_quarter(parts)


def terms_kernel(
    cols_ref, ends_ref, grad_ref, next_ref, edge_ref, keep_ref, rest_ref, terms_ref
):
    channels = grad_ref.shape[2]
    length = terms_ref.shape[0] // PARTS
    gradient = grad_ref[...].reshape(-1, channels)
    low_y, high_y = y_faces(lambda x: grad_ref[x].astype(F32))
    ends = grad_ref[0].astype(F32), grad_ref[SIDE - 1].astype(F32)
    pair_ref = rest_ref.at[rest_ref.shape[0] - PLANE :]
    store_faces(*ends, low_y, high_y, pair_ref, next_ref, edge_ref)

    def parts(i):
        stop = -(-2 * length * i // channels)
        start = 2 * length * (i + 1) // channels
        write_terms(cols_ref, ends_ref, gradient, 0, stop, terms_ref)
        write_terms(cols_ref, ends_ref, gradient, start, 3 * TAPS, terms_ref)

    for_quarter(parts)
    for r in range(PARTS - 2):
        part = terms_ref[pl.ds(pl.multiple_of(part_index(r) * length, 16), length)]
        if r < PARTS // 2:
            keep_ref[r * length : (r + 1) * length] = part
        else:
            row = (r - PARTS // 2) * length
            rest_ref[row : row + length] = part.astype(BF16)


def lane_of(tx, ty):
    return (ty ^ (ty >> 1) ^ tx ^ (tx >> 1)) & 1


def part_index(r):
    tx, ty = lax.axis_index("tx"), lax.axis_index("ty")
    lane, across, along = lane_of(tx, ty) ^ (r >> 2), (ty >> 1) & 1, tx & 1
    first = jnp.where(lane == 0, across, along)
    second = jnp.where(lane == 0, along, across)
    return lane * 4 + ((first * 2 + second) ^ (r & 3))


def moved_weights(weight_ref, taps):
    return jnp.concatenate([weight_ref[3 * TAPS - 1 - tap] for tap in taps], axis=1)


def back_kernel(grad_ref, planes_ref, weight_ref, part_ref, cols_ref):
    channels = grad_ref.shape[2]
    edge = jnp.zeros((SIDE, channels), F32)
    for x in range(SIDE + 2):
        plane = planes_ref[0 if x == 0 else 1] if x in (0, SIDE + 1) else grad_ref[x - 1]
        write_columns(jnp.concatenate([edge, plane.astype(F32), edge], axis=0), cols_ref.at[x])
    total = jnp.zeros(part_ref.shape, F32)
    for dx in range(3):
        window = cols_ref[dx : dx + SIDE].reshape(-1, TAPS * channels)
        taps = range(TAPS * dx, TAPS * (dx + 1))
        total = total + contract(window, moved_weights(weight_ref, taps), 1, 1)
    part_ref[...] = total


def squares(ref, rows):
    value = ref[:rows].astype(F32)
    return jnp.sum(value * value, axis=0, keepdims=True)


def y_faces_kernel(
    extra_ref, part_ref, mask_ref, weight_ref, near_ref, far_ref, line_ref, *refs
):
    pieces, (out_ref, squares_ref, cols_ref) = refs[:-3], refs[-3:]
    channels, rows = part_ref.shape[1], (SIDE + 2) * SIDE
    tx, ty = lax.axis_index("tx"), lax.axis_index("ty")
    total = sum(squares(ref, near_ref.shape[0] - rows) for ref in pieces)
    squares_ref[...] = jnp.broadcast_to(total, squares_ref.shape)
    by_first, by_second = far_ref[far_ref.shape[0] - rows :], line_ref[line_ref.shape[0] - rows :]
    other = jnp.where(lane_of(tx, ty) == 0, by_first.astype(F32), by_second.astype(F32))
    beyond = jnp.zeros(other.shape, F32) if extra_ref is None else extra_ref[...].astype(F32)
    other = jnp.where(((ty + 1) & 2) == 2, other, beyond)
    pair = near_ref[near_ref.shape[0] - rows :].astype(F32)
    even = parity("ty")
    added = []
    for dy, face in ((0, jnp.where(even, other, pair)), (2, jnp.where(even, pair, other))):
        write_columns(face, cols_ref)
        taps = [TAPS * dx + 3 * dy + dz for dx in range(3) for dz in range(3)]
        added.append(contract(cols_ref[...], moved_weights(weight_ref, taps), 1, 1))
    low, high = added
    rows = BY * SIDE
    for x in range(SIDE):
        here = slice(x * SIDE, (x + 1) * SIDE)
        total = part_ref[x * PLANE : (x + 1) * PLANE]
        first, final = total[:SIDE] + low[here], total[PLANE - SIDE :] + high[here]
        total = jnp.concatenate([first, total[SIDE : PLANE - SIDE], final], axis=0)
        total = (total * mask_ref[x]).astype(BF16)
        for j in range(GY):
            slot, a = x // BX * GY + j, x % BX
            out_ref[slot, a * rows : (a + 1) * rows, :] = total[j * rows : (j + 1) * rows]


def norm_kernel(*refs):
    pieces, refs = refs[:PARTS], refs[PARTS:]
    squares_ref, grad_ref, out_hbm, grad_hbm, out_ref, semaphores = refs
    copies = [pltpu.make_async_copy(grad_ref, grad_hbm, semaphores.at[PARTS])]
    copies[0].start()
    rows, channels = out_ref.shape[1:]
    total = squares_ref[:1] + squares(pieces[-1], rows)
    mean = jnp.sum(total, axis=1, keepdims=True) / (PARTS * rows * channels)
    scale = jnp.broadcast_to(1.0 / jnp.sqrt(mean + 1e-06), (1, channels))
    for r, piece in enumerate(pieces):
        out_ref[r] = piece[:rows].astype(F32) * scale
        first = pl.multiple_of(part_index(r) * rows, 16)
        target = out_hbm.at[pl.ds(first, rows)]
        copies.append(pltpu.make_async_copy(out_ref.at[r], target, semaphores.at[r]))
        copies[-1].start()
    for copy in copies:
        copy.wait()


def swap_pairs(first, count):
    return [pair for i in range(first, count - 1, 2) for pair in ((i, i + 1), (i + 1, i))]


def swap_along_y(b, a):
    count = lax.axis_size("ty")
    got_b = lax.ppermute(b, "ty", swap_pairs(1, count))
    return got_b, lax.ppermute(a, "ty", swap_pairs(0, count))


def edge_faces(kernel, edges, faces, waits=()):
    face = shape(((SIDE + 2) * SIDE, edges.shape[2]), BF16)
    return pl.pallas_call(
        kernel,
        out_shape=(face, face, shape(edges.shape, BF16)),
        in_specs=vmem(1 + len(faces)) + [pl.BlockSpec(memory_space=pl.ANY)] * len(waits),
        out_specs=tuple(vmem(3)),
        compiler_params=pltpu.CompilerParams(vmem_limit_bytes=16 * 2**20),
        name="edge_faces",
    )(edges, *faces, *waits)


def exchange_with(value, partner):
    n_tx, n_ty = lax.axis_size("tx"), lax.axis_size("ty")
    pairs = []
    for tx in range(n_tx):
        for ty in range(n_ty):
            other = partner(tx, ty)
            if other is not None:
                pairs.append((tx * n_ty + ty, other[0] * n_ty + other[1]))
    return lax.ppermute(value, ("tx", "ty"), pairs)


def by_core(tx, ty):
    return tx, ty ^ 1


def same_lane(tx, ty, other_tx, other_ty):
    return other_tx, other_ty ^ lane_of(tx, ty) ^ lane_of(other_tx, other_ty)


def first_way(tx, ty):
    other = (tx, ty ^ 2) if lane_of(tx, ty) == 0 else (tx ^ 1, ty)
    return same_lane(tx, ty, *other)


def second_way(tx, ty):
    other = (tx ^ 1, ty) if lane_of(tx, ty) == 0 else (tx, ty ^ 2)
    return same_lane(tx, ty, *other)


def along_line(flips):
    return lambda tx, ty: same_lane(tx, ty, tx ^ (2 * flips[lane_of(tx, ty)]), ty)


def add(*terms):
    total = terms[0]
    for term in terms[1:]:
        total = total + term
    return total


def message(sections, waits=(), passes=()):
    arrays = []
    for _, _, *terms in sections:
        for array, _ in terms:
            if not any(array is known for known in arrays):
                arrays.append(array)
    place = [[next(i for i, x in enumerate(arrays) if x is array) for array, _ in terms] for _, _, *terms in sections]
    count, others = len(arrays), len(waits) + len(passes)
    total_rows = sum(section[0] for section in sections)

    def body(*refs):
        out_ref, row = refs[count + others], 0
        for places, (rows, fn, *terms) in zip(place, sections):
            values = [refs[i][first : first + rows].astype(F32) for i, (_, first) in zip(places, terms)]
            out_ref[row : row + rows] = fn(*values).astype(BF16)
            row += rows

    plain = pl.BlockSpec(memory_space=pl.ANY)
    outs = [shape((total_rows, arrays[0].shape[1]), BF16)]
    out, *passed = pl.pallas_call(
        body,
        out_shape=outs + [shape(x.shape, x.dtype) for x in passes],
        in_specs=vmem(count) + [plain] * others,
        out_specs=vmem(1) + [plain] * len(passes),
        input_output_aliases={count + len(waits) + i: 1 + i for i in range(len(passes))},
        compiler_params=pltpu.CompilerParams(vmem_limit_bytes=16 * 2**20),
        name="message",
    )(*arrays, *waits, *passes)
    return (out, *passed) if passes else out


def after(value, token):
    plain = pl.BlockSpec(memory_space=pl.ANY)
    return pl.pallas_call(
        lambda value_ref, token_ref, out_ref: None,
        out_shape=shape(value.shape, value.dtype),
        in_specs=[plain] * 2,
        out_specs=plain,
        input_output_aliases={0: 0},
        compiler_params=pltpu.CompilerParams(vmem_limit_bytes=16 * 2**20),
        name="after",
    )(value, token)


def on_device(features, occupancy, neighbors, point_voxel, conv_weight, head_weight, teacher):
    slots, brick, channels = features.shape
    kernels = conv_weight.shape[0]
    n_tx, n_ty = lax.axis_size("tx"), lax.axis_size("ty")
    edges = shape((2, PLANE, channels), BF16)
    ext = (SIDE + 2, (SIDE + 2) * SIDE, channels)
    grid = pltpu.VMEM(ext, F32)
    cols = pltpu.VMEM((SIDE + 2, PLANE, TAPS * channels), BF16)

    fetched = (features, occupancy)
    face = shape((PLANE, channels), BF16)
    planes = shape((SIDE, PLANE, channels), F32)
    y_b, y_a, x_ends, masked, mask = call(
        first_faces_kernel, (face, face, edges, planes, planes), fetched, buffers(*fetched),
        name="first_faces", fetched=2,
    )
    y_b, y_a = swap_along_y(y_b, y_a)
    wide_face = shape(((SIDE + 2) * SIDE, channels), BF16)
    x_pair, x_next = call(
        x_faces_kernel, (wide_face, wide_face), (x_ends, y_b, y_a), name="x_faces"
    )
    x_next = lax.ppermute(x_next, "tx", swap_pairs(1, n_tx))
    x_pair = lax.ppermute(x_pair, "tx", swap_pairs(0, n_tx))
    fetched = (point_voxel.reshape(1, -1), teacher, head_weight, conv_weight)
    tile_cols, pre, sums, head, weight = call(
        main_kernel,
        (
            shape((SIDE, PLANE, TAPS * channels), BF16),
            shape((SIDE * PLANE, channels), F32),
            shape((2 * head_weight.shape[0], SIDE * PLANE), F32),
            shape(head_weight.shape, BF16),
            shape(conv_weight.shape, BF16),
        ),
        (*fetched, masked, y_b, y_a),
        (*buffers(*fetched[:2])[:-1], pltpu.SemaphoreType.DMA((len(fetched),))),
        name="main",
        fetched=len(fetched),
    )
    part = kernels * channels // PARTS
    ends = shape((2, PLANE, TAPS * channels), BF16)
    gradient, ends, first = call(
        tile_kernel,
        (shape((SIDE, PLANE, channels), BF16), ends, shape((2 * part, channels), BF16)),
        (tile_cols, pre, mask, sums, head, weight, x_next, x_pair),
        (pltpu.VMEM((2 * part + 2 * channels, channels), F32),),
        name="tile",
    )
    g_next, g_edges, keep, rest = call(
        terms_kernel,
        (
            face,
            edges,
            shape((PARTS // 2 * part, channels), F32),
            shape((2 * part + PLANE, channels), BF16),
        ),
        (tile_cols, ends, gradient),
        (pltpu.VMEM((kernels * channels, channels), F32),),
        name="terms",
    )

    got_first = exchange_with(first, by_core)
    got_rest = exchange_with(rest, by_core)
    onward = message([(part, add, (keep, 3 * part), (got_first, part))])
    got_onward = exchange_with(onward, first_way)
    faces = [(PLANE, add, (got_rest, 2 * part)), (PLANE, add, (g_next, 0))]
    got1 = exchange_with(
        message([(part, add, (keep, 2 * part), (got_first, 0)), *faces]), first_way
    )
    kept = [(part, add, (keep, part), (got_rest, part), (got_onward, 0))]
    got2 = exchange_with(message(kept + faces), second_way)
    at = (part, part, part)
    hand_on = (PLANE, picked_face, (got1, part + PLANE), (got2, part + PLANE))
    total = [(part, add, (keep, 0), (got_rest, 0), (got1, 0), (got2, 0))]
    flips, lines = [], []
    while 2 ** len(flips) < n_tx // 2:
        flips.append(2 ** (len(flips) + 1) - 1)
    flips = list(zip(flips, flips[::-1]))
    for both in flips:
        own = message(total + [hand_on])
        lines.append(exchange_with(own, along_line(both)))
        total = [(part, add, (own, 0), (lines[-1], 0))]
        hand_on = (PLANE, add, (own, part))
    bit = 4
    while bit < n_ty:
        own = message(total)
        flip = 2 * bit - 4
        got = exchange_with(own, lambda tx, ty, flip=flip: same_lane(tx, ty, tx, ty ^ flip))
        total = [(part, add, (own, 0), (got, 0))]
        bit *= 2
    kernel = functools.partial(hand_on_edge_kernel, flips, at)
    g_a, g_b, planes = edge_faces(kernel, g_edges, (got1, got2, *lines))
    rows = g_a.shape[0]
    total, gradient = message(total + [(rows, add, (g_b, 0))], (), (gradient,))
    piece1 = exchange_with(total, second_way)
    back_part = call(
        back_kernel,
        shape((SIDE * PLANE, channels), F32),
        (gradient, planes, weight),
        (cols,),
        name="back",
    )
    piece2 = exchange_with(message([(part + rows, add, (total, 0))], (back_part,)), first_way)
    piece3 = exchange_with(message([(part, add, (piece1, 0))]), first_way)
    near = message([(part, add, (piece2, 0)), (rows, add, (g_a, 0))])
    pieces = (total, piece1, near, piece3)
    others = [exchange_with(piece, by_core) for piece in pieces]
    faces = (back_part, mask, weight, others[2], piece2, piece1, *pieces, *others[:3])
    kernel = functools.partial(y_faces_kernel, None)
    if n_ty > 4:
        pairs = [pair for i in range(3, n_ty - 1, 4) for pair in ((i, i + 1), (i + 1, i))]
        faces = (lax.ppermute(g_b, "ty", pairs), *faces)
        kernel = y_faces_kernel
    grad_features, squares_of = call(
        kernel,
        (shape((slots, brick, channels), BF16), shape((8, channels), F32)),
        faces,
        (pltpu.VMEM((PLANE, TAPS * channels), BF16),),
        name="y_faces",
    )
    grad_weight, grad_features = pl.pallas_call(
        norm_kernel,
        out_shape=(
            shape((kernels * channels, channels), F32),
            shape((slots, brick, channels), BF16),
        ),
        in_specs=vmem(PARTS + 2),
        out_specs=(pl.BlockSpec(memory_space=pltpu.HBM),) * 2,
        scratch_shapes=[
            pltpu.VMEM((PARTS, part, channels), F32),
            pltpu.SemaphoreType.DMA((PARTS + 1,)),
        ],
        compiler_params=pltpu.CompilerParams(vmem_limit_bytes=16 * 2**20),
        name="normalise",
    )(*pieces, *others, squares_of, grad_features)
    return (grad_features, grad_weight.reshape(conv_weight.shape))


def solution(mesh):
    in_specs = (
        P(("tx", "ty"), None, None),
        P(("tx", "ty"), None),
        P(None, ("tx", "ty")),
        P(("tx", "ty")),
        P(),
        P(),
        P(None, ("tx", "ty")),
    )
    out_specs = (P(("tx", "ty"), None, None), P())
    return jax.shard_map(
        on_device, mesh=mesh, in_specs=in_specs, out_specs=out_specs, check_vma=False
    )
```

```python
import functools

import jax
import jax.numpy as jnp
from jax import lax
from jax.experimental import pallas as pl
from jax.experimental.pallas import tpu as pltpu
from jax.sharding import PartitionSpec as P

GX = 2
GY = 2
BX = 4
BY = 4
SIDE = 8
PLANE = SIDE * SIDE
TAPS = 9
BF16 = jnp.bfloat16
F32 = jnp.float32
PARTS = 8


def vmem(count):
    return [pl.BlockSpec(memory_space=pltpu.VMEM)] * count


def pin(array):
    return pltpu.with_memory_space_constraint(array, pltpu.HBM)


def call(body, outs, inputs, scratch=(), limit=32 * 2**20, name=None, fetched=0):
    return pl.pallas_call(
        body,
        out_shape=outs,
        in_specs=[pl.BlockSpec(memory_space=pltpu.HBM)] * fetched + vmem(len(inputs) - fetched),
        out_specs=jax.tree.map(lambda _: pl.BlockSpec(memory_space=pltpu.VMEM), outs),
        scratch_shapes=list(scratch),
        compiler_params=pltpu.CompilerParams(vmem_limit_bytes=limit),
        name=name,
    )(*[pin(array) for array in inputs[:fetched]], *inputs[fetched:])


def buffers(*arrays):
    rooms = [pltpu.VMEM(array.shape, array.dtype) for array in arrays]
    return (*rooms, pltpu.SemaphoreType.DMA((len(arrays),)))


def fetch(sources, rooms, semaphores):
    copies = [
        pltpu.make_async_copy(source, room, semaphores.at[i])
        for i, (source, room) in enumerate(zip(sources, rooms))
    ]
    for copy in copies:
        copy.start()
    return copies


def shape(dims, dtype):
    return jax.ShapeDtypeStruct(dims, dtype)


def slot_planes(slot):
    return BX * (slot // GY), (slot % GY) * BY * SIDE


def parity(axis):
    return lax.rem(lax.axis_index(axis), 2) == 0


def occupancy_columns(occ_ref, rows):
    occ = occ_ref[...].astype(F32)
    padded = jnp.concatenate([occ, jnp.zeros((8 - occ.shape[0], occ.shape[1]), F32)], axis=0)
    return padded.T


def write_grid(grid_ref, planes):
    for x in range(SIDE):
        grid_ref[x + 1, SIDE : SIDE + PLANE, :] = planes(x)


def y_faces(planes):
    low = jnp.concatenate([planes(x)[:SIDE] for x in range(SIDE)], axis=0)
    high = jnp.concatenate([planes(x)[PLANE - SIDE :] for x in range(SIDE)], axis=0)
    return low, high


def occupancy_mask(columns, slot, first, rows, channels):
    return jnp.broadcast_to(columns[first : first + rows, slot : slot + 1], (rows, channels))


def first_faces_kernel(
    feat_hbm, occ_hbm, point_hbm, teach_hbm, head_hbm, weight_hbm,
    b_ref, a_ref, ends_ref, feat_ref, occ_ref, point_ref, teach_ref, head_ref, weight_ref,
    semaphores,
):
    sources = (feat_hbm, occ_hbm, point_hbm, teach_hbm, head_hbm, weight_hbm)
    rooms = (feat_ref, occ_ref, point_ref, teach_ref, head_ref, weight_ref)
    copies = fetch(sources, rooms, semaphores)
    for copy in copies[:2]:
        copy.wait()
    columns = occupancy_columns(occ_ref, 8)
    rows, channels = BY * SIDE, feat_ref.shape[2]

    def masked(x, j, first, count):
        slot, row = x // BX * GY + j, x % BX * rows + first
        mask = occupancy_mask(columns, slot, row, count, channels)
        return feat_ref[slot, row : row + count, :].astype(F32) * mask

    low_y = jnp.concatenate([masked(x, 0, 0, SIDE) for x in range(SIDE)], axis=0)
    high_y = jnp.concatenate([masked(x, GY - 1, rows - SIDE, SIDE) for x in range(SIDE)], axis=0)
    even = parity("ty")
    a_ref[...] = jnp.where(even, high_y, low_y).astype(BF16)
    b_ref[...] = jnp.where(even, low_y, high_y).astype(BF16)
    for i, x in enumerate((0, SIDE - 1)):
        plane = jnp.concatenate([masked(x, j, 0, rows) for j in range(GY)], axis=0)
        ends_ref[i] = plane.astype(BF16)
    for copy in copies[2:]:
        copy.wait()


def halo_along_y(b_ref, a_ref):
    even = parity("ty")
    a, b = a_ref[...].astype(F32), b_ref[...].astype(F32)
    return jnp.where(even, b, a), jnp.where(even, a, b)


def x_faces_kernel(ends_ref, y_b_ref, y_a_ref, *refs):
    pair_ref, next_ref = refs[-2:]
    low, high = halo_along_y(y_b_ref, y_a_ref)
    last = PLANE - SIDE
    first = jnp.concatenate([low[:SIDE], ends_ref[0].astype(F32), high[:SIDE]], axis=0)
    final = jnp.concatenate([low[last:], ends_ref[1].astype(F32), high[last:]], axis=0)
    even = parity("tx")
    pair_ref[...] = jnp.where(even, final, first).astype(BF16)
    next_ref[...] = jnp.where(even, first, final).astype(BF16)


def store_edges(low, high, edge_ref, a_ref, b_ref, planes_ref):
    even_y = parity("ty")
    planes_ref[0] = low.astype(BF16)
    planes_ref[1] = high.astype(BF16)
    last = PLANE - SIDE
    bottom = jnp.concatenate([low[:SIDE], edge_ref[0].astype(F32), high[:SIDE]], axis=0)
    top = jnp.concatenate([low[last:], edge_ref[1].astype(F32), high[last:]], axis=0)
    a_ref[...] = jnp.where(even_y, top, bottom).astype(BF16)
    b_ref[...] = jnp.where(even_y, bottom, top).astype(BF16)


def hand_on_edge_kernel(flips, first_row, edge_ref, got1_ref, got2_ref, *refs):
    lines, (a_ref, b_ref, planes_ref) = refs[: len(flips)], refs[-3:]
    even = parity("tx")
    pair = picked_face(got1_ref[first_row[0] : first_row[0] + PLANE], got2_ref[first_row[1] : first_row[1] + PLANE])
    place = lax.axis_index("tx") // 2
    behind = jnp.where(even, place - 1, place + 1)
    other = jnp.zeros(pair.shape, F32)
    lane = lane_of(lax.axis_index("tx"), lax.axis_index("ty"))
    for both, line_ref in zip(flips, lines):
        flip = jnp.where(lane == 0, *both)
        face = line_ref[first_row[2] : first_row[2] + PLANE].astype(F32)
        other = jnp.where((place ^ behind) == flip, face, other)
    low, high = jnp.where(even, other, pair), jnp.where(even, pair, other)
    store_edges(low, high, edge_ref, a_ref, b_ref, planes_ref)


def picked_face(by_first_way, by_core):
    lane = lane_of(lax.axis_index("tx"), lax.axis_index("ty"))
    return jnp.where(lane == 0, by_core.astype(F32), by_first_way.astype(F32))


def write_columns(plane, cols_ref):
    channels = plane.shape[1]
    z = lax.broadcasted_iota(jnp.int32, plane.shape, 0) % SIDE
    zeros = jnp.zeros((1, channels), F32)
    before = jnp.where(z == 0, 0.0, jnp.concatenate([zeros, plane[:-1]], axis=0))
    after = jnp.where(z == SIDE - 1, 0.0, jnp.concatenate([plane[1:], zeros], axis=0))
    for dz, moved in enumerate((before, plane, after)):
        for dy in range(3):
            tap = 3 * dy + dz
            window = moved[dy * SIDE : dy * SIDE + PLANE]
            cols_ref[:, tap * channels : (tap + 1) * channels] = window.astype(BF16)


def split3(value):
    high = value.astype(BF16)
    rest = value - high.astype(F32)
    middle = rest.astype(BF16)
    low = (rest - middle.astype(F32)).astype(BF16)
    return high, middle, low


def contract(a, b, dim_a, dim_b):
    return lax.dot_general(a, b, (((dim_a,), (dim_b,)), ((), ())), preferred_element_type=F32)


def voxel_sums(point_ref, teach_ref):
    target = jnp.exp(teach_ref[...].astype(F32))
    target = target / jnp.sum(target, axis=0, keepdims=True)
    classes, points = target.shape
    place = point_ref[...]
    place = (place & 0x11F) | ((place & 0x80) >> 2) | ((place & 0x60) << 1)
    chosen = lax.broadcasted_iota(jnp.int32, (SIDE * PLANE, points), 0) == place
    chosen = jnp.where(chosen, 1.0, 0.0).astype(BF16)
    stack = jnp.concatenate([*split3(target), jnp.ones((classes, points), BF16)], axis=0)
    sums = contract(stack, chosen, 1, 1)
    target_sum = sums[:classes] + sums[classes : 2 * classes] + sums[2 * classes : 3 * classes]
    return jnp.concatenate([target_sum, sums[3 * classes :]], axis=0)


def main_kernel(
    feat_ref, occ_ref, point_ref, teach_ref, weight_ref, y_b_ref, y_a_ref,
    cols_ref, pre_ref, mask_ref, sums_ref,
):
    rows, channels = BY * SIDE, feat_ref.shape[2]
    columns = occupancy_columns(occ_ref, 8)
    low, high = halo_along_y(y_b_ref, y_a_ref)
    for x in range(SIDE):
        plane = []
        for j in range(GY):
            slot, row = x // BX * GY + j, x % BX * rows
            mask = occupancy_mask(columns, slot, row, rows, channels)
            mask_ref[x, j * rows : (j + 1) * rows, :] = mask
            plane.append(feat_ref[slot, row : row + rows, :].astype(F32) * mask)
        here = slice(x * SIDE, (x + 1) * SIDE)
        write_columns(jnp.concatenate([low[here], *plane, high[here]], axis=0), cols_ref.at[x])
    wide, inner = TAPS * channels, SIDE - 1
    sums_ref[...] = voxel_sums(point_ref, teach_ref)

    def product(planes, dx):
        window = cols_ref[planes].reshape(-1, wide)
        matrix = weight_ref[TAPS * dx : TAPS * (dx + 1)].reshape(wide, channels)
        return jnp.dot(window, matrix, preferred_element_type=F32)

    edge = jnp.zeros((PLANE, channels), F32)
    pre = product(slice(0, SIDE), 1)
    pre = pre + jnp.concatenate([edge, product(slice(0, inner), 0)], axis=0)
    pre_ref[...] = pre + jnp.concatenate([product(slice(1, SIDE), 2), edge], axis=0)


def write_terms(cols_ref, ends_ref, gradient, start, stop, terms_ref, first=0):
    channels = gradient.shape[1]
    inner = (SIDE - 1) * PLANE
    for dx in range(3):
        low, high = max(start, TAPS * dx), min(stop, TAPS * (dx + 1))
        if low >= high:
            continue
        lanes = slice((low - TAPS * dx) * channels, (high - TAPS * dx) * channels)

        def term(planes, gradient):
            return contract(planes.reshape(gradient.shape[0], -1), gradient, 0, 0)

        if dx == 0:
            total = term(cols_ref[: SIDE - 1, :, lanes], gradient[PLANE:])
            total = total + term(ends_ref[0, :, lanes], gradient[:PLANE])
        elif dx == 1:
            total = term(cols_ref[:, :, lanes], gradient)
        else:
            total = term(cols_ref[1:, :, lanes], gradient[:inner])
            total = total + term(ends_ref[1, :, lanes], gradient[inner:])
        terms_ref[(low - first) * channels : (high - first) * channels] = total


def for_quarter(body):
    for i in range(PARTS // 2):
        pl.when((part_index(PARTS - 2) >> 1) == i)(functools.partial(body, i))


def tile_kernel(
    cols_ref, pre_ref, mask_ref, sums_ref, head_ref, weight_ref, x_next_ref, x_pair_ref,
    grad_ref, ends_ref, first_ref,
    terms_ref,
):
    channels = cols_ref.shape[2] // TAPS
    classes = head_ref.shape[0]
    voxels, wide, inner = SIDE * PLANE, TAPS * channels, (SIDE - 1) * PLANE
    even = parity("tx")
    pair, other = x_pair_ref[...].astype(F32), x_next_ref[...].astype(F32)
    write_columns(jnp.where(even, other, pair), ends_ref.at[0])
    write_columns(jnp.where(even, pair, other), ends_ref.at[1])
    first = weight_ref[:TAPS].reshape(wide, channels)
    final = weight_ref[2 * TAPS :].reshape(wide, channels)
    low = pre_ref[:PLANE] + jnp.dot(ends_ref[0], first, preferred_element_type=F32)
    high = pre_ref[inner:] + jnp.dot(ends_ref[1], final, preferred_element_type=F32)
    pre = jnp.concatenate([low, pre_ref[PLANE:inner], high], axis=0)
    mask = mask_ref[...].reshape(voxels, channels)
    logistic = 1.0 / (1.0 + jnp.exp(-pre))
    slope = logistic * (1.0 + pre * (1.0 - logistic)) * mask
    hidden = (pre / (1.0 + jnp.exp(-pre)) * mask).astype(BF16)

    logits = contract(head_ref[...], hidden, 1, 1)
    student = jnp.exp(logits)
    student = student / jnp.sum(student, axis=0, keepdims=True)
    target_sum, count = sums_ref[:classes], sums_ref[classes:]
    slope_logits = jnp.where(count > 0.0, count * student, 0.0) - target_sum
    heads = jnp.concatenate([head_ref[...]] * 3, axis=0)
    pieces = jnp.concatenate([piece.astype(F32) for piece in split3(slope_logits)], axis=0)
    dhidden = contract(pieces.T.astype(BF16), heads, 1, 0)
    rounded = (dhidden * slope).astype(BF16)
    grad_ref[...] = rounded.reshape(SIDE, PLANE, channels)
    length = 3 * TAPS * channels // PARTS
    even = parity("tx")
    low, high = rounded[:PLANE].astype(F32), rounded[inner:].astype(F32)
    first_ref[2 * length : 2 * length + PLANE] = jnp.where(even, high, low).astype(BF16)
    first_ref[2 * length + PLANE :] = jnp.where(even, low, high).astype(BF16)

    def parts(i):
        start = 2 * length * i // channels
        stop = -(-2 * length * (i + 1) // channels)
        write_terms(cols_ref, ends_ref, rounded, start, stop, terms_ref, start)
        for r in range(2):
            row = 2 * length * i - start * channels + (part_index(PARTS - 2 + r) & 1) * length
            part = terms_ref[pl.ds(pl.multiple_of(row, 16), length)]
            first_ref[r * length : (r + 1) * length] = part.astype(BF16)

    for_quarter(parts)


def terms_kernel(
    cols_ref, ends_ref, grad_ref, edge_ref, keep_ref, rest_ref, terms_ref
):
    channels = grad_ref.shape[2]
    length = terms_ref.shape[0] // PARTS
    gradient = grad_ref[...].reshape(-1, channels)
    low_y, high_y = y_faces(lambda x: grad_ref[x].astype(F32))
    edge_ref[0] = low_y.astype(BF16)
    edge_ref[1] = high_y.astype(BF16)

    def parts(i):
        stop = -(-2 * length * i // channels)
        start = 2 * length * (i + 1) // channels
        write_terms(cols_ref, ends_ref, gradient, 0, stop, terms_ref)
        write_terms(cols_ref, ends_ref, gradient, start, 3 * TAPS, terms_ref)

    for_quarter(parts)
    for r in range(PARTS - 2):
        part = terms_ref[pl.ds(pl.multiple_of(part_index(r) * length, 16), length)]
        if r < PARTS // 2:
            keep_ref[r * length : (r + 1) * length] = part
        else:
            row = (r - PARTS // 2) * length
            rest_ref[row : row + length] = part.astype(BF16)


def lane_of(tx, ty):
    return (ty ^ (ty >> 1) ^ tx ^ (tx >> 1)) & 1


def part_index(r):
    tx, ty = lax.axis_index("tx"), lax.axis_index("ty")
    lane, across, along = lane_of(tx, ty) ^ (r >> 2), (ty >> 1) & 1, tx & 1
    first = jnp.where(lane == 0, across, along)
    second = jnp.where(lane == 0, along, across)
    return lane * 4 + ((first * 2 + second) ^ (r & 3))


def moved_weights(weight_ref, taps):
    return jnp.concatenate([weight_ref[3 * TAPS - 1 - tap] for tap in taps], axis=1)


def back_kernel(grad_ref, planes_ref, weight_ref, part_ref, cols_ref):
    channels = grad_ref.shape[2]
    edge = jnp.zeros((SIDE, channels), F32)
    for x in range(SIDE + 2):
        plane = planes_ref[0 if x == 0 else 1] if x in (0, SIDE + 1) else grad_ref[x - 1]
        write_columns(jnp.concatenate([edge, plane.astype(F32), edge], axis=0), cols_ref.at[x])
    total = jnp.zeros(part_ref.shape, F32)
    for dx in range(3):
        window = cols_ref[dx : dx + SIDE].reshape(-1, TAPS * channels)
        taps = range(TAPS * dx, TAPS * (dx + 1))
        total = total + contract(window, moved_weights(weight_ref, taps), 1, 1)
    part_ref[...] = total


def squares(ref, rows):
    value = ref[:rows].astype(F32)
    return jnp.sum(value * value, axis=0, keepdims=True)


def y_faces_kernel(
    extra_ref, part_ref, mask_ref, weight_ref, near_ref, far_ref, line_ref, *refs
):
    pieces, (out_ref, squares_ref, cols_ref) = refs[:-3], refs[-3:]
    channels, rows = part_ref.shape[1], (SIDE + 2) * SIDE
    tx, ty = lax.axis_index("tx"), lax.axis_index("ty")
    total = sum(squares(ref, near_ref.shape[0] - rows) for ref in pieces)
    squares_ref[...] = jnp.broadcast_to(total, squares_ref.shape)
    by_first, by_second = far_ref[far_ref.shape[0] - rows :], line_ref[line_ref.shape[0] - rows :]
    other = jnp.where(lane_of(tx, ty) == 0, by_first.astype(F32), by_second.astype(F32))
    beyond = jnp.zeros(other.shape, F32) if extra_ref is None else extra_ref[...].astype(F32)
    other = jnp.where(((ty + 1) & 2) == 2, other, beyond)
    pair = near_ref[near_ref.shape[0] - rows :].astype(F32)
    even = parity("ty")
    added = []
    for dy, face in ((0, jnp.where(even, other, pair)), (2, jnp.where(even, pair, other))):
        write_columns(face, cols_ref)
        taps = [TAPS * dx + 3 * dy + dz for dx in range(3) for dz in range(3)]
        added.append(contract(cols_ref[...], moved_weights(weight_ref, taps), 1, 1))
    low, high = added
    rows = BY * SIDE
    for x in range(SIDE):
        here = slice(x * SIDE, (x + 1) * SIDE)
        total = part_ref[x * PLANE : (x + 1) * PLANE]
        first, final = total[:SIDE] + low[here], total[PLANE - SIDE :] + high[here]
        total = jnp.concatenate([first, total[SIDE : PLANE - SIDE], final], axis=0)
        total = (total * mask_ref[x]).astype(BF16)
        for j in range(GY):
            slot, a = x // BX * GY + j, x % BX
            out_ref[slot, a * rows : (a + 1) * rows, :] = total[j * rows : (j + 1) * rows]


def norm_kernel(*refs):
    pieces, refs = refs[:PARTS], refs[PARTS:]
    squares_ref, grad_ref, out_hbm, grad_hbm, out_ref, semaphores = refs
    copies = [pltpu.make_async_copy(grad_ref, grad_hbm, semaphores.at[PARTS])]
    copies[0].start()
    rows, channels = out_ref.shape[1:]
    total = squares_ref[:1] + squares(pieces[-1], rows)
    mean = jnp.sum(total, axis=1, keepdims=True) / (PARTS * rows * channels)
    scale = jnp.broadcast_to(1.0 / jnp.sqrt(mean + 1e-06), (1, channels))
    for r, piece in enumerate(pieces):
        out_ref[r] = piece[:rows].astype(F32) * scale
        first = pl.multiple_of(part_index(r) * rows, 16)
        target = out_hbm.at[pl.ds(first, rows)]
        copies.append(pltpu.make_async_copy(out_ref.at[r], target, semaphores.at[r]))
        copies[-1].start()
    for copy in copies:
        copy.wait()


def swap_pairs(first, count):
    return [pair for i in range(first, count - 1, 2) for pair in ((i, i + 1), (i + 1, i))]


def swap_along_y(b, a):
    count = lax.axis_size("ty")
    got_b = lax.ppermute(b, "ty", swap_pairs(1, count))
    return got_b, lax.ppermute(a, "ty", swap_pairs(0, count))


def edge_faces(kernel, edges, faces, waits=()):
    face = shape(((SIDE + 2) * SIDE, edges.shape[2]), BF16)
    return pl.pallas_call(
        kernel,
        out_shape=(face, face, shape(edges.shape, BF16)),
        in_specs=vmem(1 + len(faces)) + [pl.BlockSpec(memory_space=pl.ANY)] * len(waits),
        out_specs=tuple(vmem(3)),
        compiler_params=pltpu.CompilerParams(vmem_limit_bytes=16 * 2**20),
        name="edge_faces",
    )(edges, *faces, *waits)


def exchange_with(value, partner):
    n_tx, n_ty = lax.axis_size("tx"), lax.axis_size("ty")
    pairs = []
    for tx in range(n_tx):
        for ty in range(n_ty):
            other = partner(tx, ty)
            if other is not None:
                pairs.append((tx * n_ty + ty, other[0] * n_ty + other[1]))
    return lax.ppermute(value, ("tx", "ty"), pairs)


def by_core(tx, ty):
    return tx, ty ^ 1


def same_lane(tx, ty, other_tx, other_ty):
    return other_tx, other_ty ^ lane_of(tx, ty) ^ lane_of(other_tx, other_ty)


def first_way(tx, ty):
    other = (tx, ty ^ 2) if lane_of(tx, ty) == 0 else (tx ^ 1, ty)
    return same_lane(tx, ty, *other)


def second_way(tx, ty):
    other = (tx ^ 1, ty) if lane_of(tx, ty) == 0 else (tx, ty ^ 2)
    return same_lane(tx, ty, *other)


def along_line(flips):
    return lambda tx, ty: same_lane(tx, ty, tx ^ (2 * flips[lane_of(tx, ty)]), ty)


def add(*terms):
    total = terms[0]
    for term in terms[1:]:
        total = total + term
    return total


def message(sections, waits=(), passes=()):
    arrays = []
    for _, _, *terms in sections:
        for array, _ in terms:
            if not any(array is known for known in arrays):
                arrays.append(array)
    place = [[next(i for i, x in enumerate(arrays) if x is array) for array, _ in terms] for _, _, *terms in sections]
    count, others = len(arrays), len(waits) + len(passes)
    total_rows = sum(section[0] for section in sections)

    def body(*refs):
        out_ref, row = refs[count + others], 0
        for places, (rows, fn, *terms) in zip(place, sections):
            values = [refs[i][first : first + rows].astype(F32) for i, (_, first) in zip(places, terms)]
            out_ref[row : row + rows] = fn(*values).astype(BF16)
            row += rows

    plain = pl.BlockSpec(memory_space=pl.ANY)
    outs = [shape((total_rows, arrays[0].shape[1]), BF16)]
    out, *passed = pl.pallas_call(
        body,
        out_shape=outs + [shape(x.shape, x.dtype) for x in passes],
        in_specs=vmem(count) + [plain] * others,
        out_specs=vmem(1) + [plain] * len(passes),
        input_output_aliases={count + len(waits) + i: 1 + i for i in range(len(passes))},
        compiler_params=pltpu.CompilerParams(vmem_limit_bytes=16 * 2**20),
        name="message",
    )(*arrays, *waits, *passes)
    return (out, *passed) if passes else out


def after(value, token):
    plain = pl.BlockSpec(memory_space=pl.ANY)
    return pl.pallas_call(
        lambda value_ref, token_ref, out_ref: None,
        out_shape=shape(value.shape, value.dtype),
        in_specs=[plain] * 2,
        out_specs=plain,
        input_output_aliases={0: 0},
        compiler_params=pltpu.CompilerParams(vmem_limit_bytes=16 * 2**20),
        name="after",
    )(value, token)


def on_device(features, occupancy, neighbors, point_voxel, conv_weight, head_weight, teacher):
    slots, brick, channels = features.shape
    kernels = conv_weight.shape[0]
    n_tx, n_ty = lax.axis_size("tx"), lax.axis_size("ty")
    edges = shape((2, PLANE, channels), BF16)
    ext = (SIDE + 2, (SIDE + 2) * SIDE, channels)
    grid = pltpu.VMEM(ext, F32)
    cols = pltpu.VMEM((SIDE + 2, PLANE, TAPS * channels), BF16)

    points = point_voxel.reshape(1, -1)
    fetched = (features, occupancy, points, teacher, head_weight, conv_weight)
    face = shape((PLANE, channels), BF16)
    planes = shape((SIDE, PLANE, channels), F32)
    y_b, y_a, x_ends, *rooms = call(
        first_faces_kernel,
        (face, face, edges, *[shape(x.shape, x.dtype) for x in fetched]),
        fetched,
        (pltpu.SemaphoreType.DMA((len(fetched),)),),
        name="first_faces",
        fetched=len(fetched),
    )
    feat, occ, point, teach, head, weight = rooms
    y_b, y_a = swap_along_y(y_b, y_a)
    wide_face = shape(((SIDE + 2) * SIDE, channels), BF16)
    x_pair, x_next = call(
        x_faces_kernel, (wide_face, wide_face), (x_ends, y_b, y_a), name="x_faces"
    )
    x_next = lax.ppermute(x_next, "tx", swap_pairs(1, n_tx))
    x_pair = lax.ppermute(x_pair, "tx", swap_pairs(0, n_tx))
    tile_cols, pre, mask, sums = call(
        main_kernel,
        (
            shape((SIDE, PLANE, TAPS * channels), BF16),
            shape((SIDE * PLANE, channels), F32),
            planes,
            shape((2 * head_weight.shape[0], SIDE * PLANE), F32),
        ),
        (feat, occ, point, teach, weight, y_b, y_a),
        name="main",
    )
    part = kernels * channels // PARTS
    ends = shape((2, PLANE, TAPS * channels), BF16)
    gradient, ends, first = call(
        tile_kernel,
        (shape((SIDE, PLANE, channels), BF16), ends, shape((2 * part + 2 * PLANE, channels), BF16)),
        (tile_cols, pre, mask, sums, head, weight, x_next, x_pair),
        (pltpu.VMEM((2 * part + 2 * channels, channels), F32),),
        name="tile",
    )
    g_edges, keep, rest = call(
        terms_kernel,
        (
            edges,
            shape((PARTS // 2 * part, channels), F32),
            shape((2 * part, channels), BF16),
        ),
        (tile_cols, ends, gradient),
        (pltpu.VMEM((kernels * channels, channels), F32),),
        name="terms",
    )

    got_first = exchange_with(first, by_core)
    got_rest = exchange_with(rest, by_core)
    onward = message([(part, add, (keep, 3 * part), (got_first, part))])
    got_onward = exchange_with(onward, first_way)
    pair, following = 2 * part, 2 * part + PLANE
    planes = [(got_first, pair), (first, following), (first, pair), (got_first, following)]
    got1 = exchange_with(
        message(
            [(part, add, (keep, 2 * part), (got_first, 0))]
            + [(PLANE, add, plane) for plane in planes]
        ),
        first_way,
    )
    kept = [(part, add, (keep, part), (got_rest, part), (got_onward, 0))]
    got2 = exchange_with(message(kept), second_way)
    x_faces = exchange_with(message([(2 * PLANE, add, (got1, part + 2 * PLANE))]), by_core)
    at = (part, 0, part)
    hand_on = (PLANE, picked_face, (got1, part + PLANE), (x_faces, PLANE))
    total = [(part, add, (keep, 0), (got_rest, 0), (got1, 0), (got2, 0))]
    flips, lines = [], []
    while 2 ** len(flips) < n_tx // 2:
        flips.append(2 ** (len(flips) + 1) - 1)
    flips = list(zip(flips[::-1], flips))
    for both in flips:
        own = message(total + [hand_on])
        lines.append(exchange_with(own, along_line(both)))
        total = [(part, add, (own, 0), (lines[-1], 0))]
        hand_on = (PLANE, add, (own, part))
    bit = 4
    while bit < n_ty:
        own = message(total)
        flip = 2 * bit - 4
        got = exchange_with(own, lambda tx, ty, flip=flip: same_lane(tx, ty, tx, ty ^ flip))
        total = [(part, add, (own, 0), (got, 0))]
        bit *= 2
    kernel = functools.partial(hand_on_edge_kernel, flips, at)
    g_a, g_b, planes = edge_faces(kernel, g_edges, (got1, x_faces, *lines))
    rows = g_a.shape[0]
    total, gradient = message(total + [(rows, add, (g_b, 0))], (), (gradient,))
    piece1 = exchange_with(total, second_way)
    back_part = call(
        back_kernel,
        shape((SIDE * PLANE, channels), F32),
        (gradient, planes, weight),
        (cols,),
        name="back",
    )
    piece2 = exchange_with(message([(part + rows, add, (total, 0))], (back_part,)), first_way)
    onward = message([(part, add, (piece1, 0))])
    piece3 = exchange_with(onward, first_way)
    near = message([(part, add, (piece2, 0)), (rows, add, (g_a, 0))])
    pieces = (total, piece1, near, piece3)
    late = message([(part, add, (total, 0))], (near,))
    others = [exchange_with(piece, by_core) for piece in (late, *pieces[1:])]
    faces = (back_part, mask, weight, others[2], piece2, piece1, *pieces, *others[:3])
    kernel = functools.partial(y_faces_kernel, None)
    if n_ty > 4:
        pairs = [pair for i in range(3, n_ty - 1, 4) for pair in ((i, i + 1), (i + 1, i))]
        faces = (lax.ppermute(g_b, "ty", pairs), *faces)
        kernel = y_faces_kernel
    grad_features, squares_of = call(
        kernel,
        (shape((slots, brick, channels), BF16), shape((8, channels), F32)),
        faces,
        (pltpu.VMEM((PLANE, TAPS * channels), BF16),),
        name="y_faces",
    )
    grad_weight, grad_features = pl.pallas_call(
        norm_kernel,
        out_shape=(
            shape((kernels * channels, channels), F32),
            shape((slots, brick, channels), BF16),
        ),
        in_specs=vmem(PARTS + 2),
        out_specs=(pl.BlockSpec(memory_space=pltpu.HBM),) * 2,
        scratch_shapes=[
            pltpu.VMEM((PARTS, part, channels), F32),
            pltpu.SemaphoreType.DMA((PARTS + 1,)),
        ],
        compiler_params=pltpu.CompilerParams(vmem_limit_bytes=16 * 2**20),
        name="normalise",
    )(*pieces, *others, squares_of, grad_features)
    return (grad_features, grad_weight.reshape(conv_weight.shape))


def solution(mesh):
    in_specs = (
        P(("tx", "ty"), None, None),
        P(("tx", "ty"), None),
        P(None, ("tx", "ty")),
        P(("tx", "ty")),
        P(),
        P(),
        P(None, ("tx", "ty")),
    )
    out_specs = (P(("tx", "ty"), None, None), P())
    return jax.shard_map(
        on_device, mesh=mesh, in_specs=in_specs, out_specs=out_specs, check_vma=False
    )
```

```python
import functools

import jax
import jax.numpy as jnp
from jax import lax
from jax.experimental import pallas as pl
from jax.experimental.pallas import tpu as pltpu
from jax.sharding import PartitionSpec as P

GX = 2
GY = 2
BX = 4
BY = 4
SIDE = 8
PLANE = SIDE * SIDE
TAPS = 9
BF16 = jnp.bfloat16
F32 = jnp.float32
PARTS = 8


def vmem(count):
    return [pl.BlockSpec(memory_space=pltpu.VMEM)] * count


def pin(array):
    return pltpu.with_memory_space_constraint(array, pltpu.HBM)


def call(body, outs, inputs, scratch=(), limit=32 * 2**20, name=None, fetched=0):
    return pl.pallas_call(
        body,
        out_shape=outs,
        in_specs=[pl.BlockSpec(memory_space=pltpu.HBM)] * fetched + vmem(len(inputs) - fetched),
        out_specs=jax.tree.map(lambda _: pl.BlockSpec(memory_space=pltpu.VMEM), outs),
        scratch_shapes=list(scratch),
        compiler_params=pltpu.CompilerParams(vmem_limit_bytes=limit),
        name=name,
    )(*[pin(array) for array in inputs[:fetched]], *inputs[fetched:])


def fetch(sources, rooms, semaphores):
    copies = [
        pltpu.make_async_copy(source, room, semaphores.at[i])
        for i, (source, room) in enumerate(zip(sources, rooms))
    ]
    for copy in copies:
        copy.start()
    return copies


def shape(dims, dtype):
    return jax.ShapeDtypeStruct(dims, dtype)


def parity(axis):
    return lax.rem(lax.axis_index(axis), 2) == 0


def occupancy_columns(occ_ref, rows):
    occ = occ_ref[...].astype(F32)
    padded = jnp.concatenate([occ, jnp.zeros((8 - occ.shape[0], occ.shape[1]), F32)], axis=0)
    return padded.T


def y_faces(planes):
    low = jnp.concatenate([planes(x)[:SIDE] for x in range(SIDE)], axis=0)
    high = jnp.concatenate([planes(x)[PLANE - SIDE :] for x in range(SIDE)], axis=0)
    return low, high


def occupancy_mask(columns, slot, first, rows, channels):
    return jnp.broadcast_to(columns[first : first + rows, slot : slot + 1], (rows, channels))


def first_faces_kernel(
    feat_hbm, occ_hbm, b_ref, a_ref, ends_ref, feat_ref, occ_ref, semaphores
):
    for copy in fetch((feat_hbm, occ_hbm), (feat_ref, occ_ref), semaphores):
        copy.wait()
    columns = occupancy_columns(occ_ref, 8)
    rows, channels = BY * SIDE, feat_ref.shape[2]

    def masked(x, j, first, count):
        slot, row = x // BX * GY + j, x % BX * rows + first
        mask = occupancy_mask(columns, slot, row, count, channels)
        return feat_ref[slot, row : row + count, :].astype(F32) * mask

    low_y = jnp.concatenate([masked(x, 0, 0, SIDE) for x in range(SIDE)], axis=0)
    high_y = jnp.concatenate([masked(x, GY - 1, rows - SIDE, SIDE) for x in range(SIDE)], axis=0)
    even = parity("ty")
    a_ref[...] = jnp.where(even, high_y, low_y).astype(BF16)
    b_ref[...] = jnp.where(even, low_y, high_y).astype(BF16)
    for i, x in enumerate((0, SIDE - 1)):
        plane = jnp.concatenate([masked(x, j, 0, rows) for j in range(GY)], axis=0)
        ends_ref[i] = plane.astype(BF16)


def fetch_kernel(*refs):
    count = len(refs) // 2 - 1
    for copy in fetch(refs[:count], refs[count + 1 : -1], refs[-1]):
        copy.wait()


def halo_along_y(b_ref, a_ref):
    even = parity("ty")
    a, b = a_ref[...].astype(F32), b_ref[...].astype(F32)
    return jnp.where(even, b, a), jnp.where(even, a, b)


def x_faces_kernel(ends_ref, y_a_ref, y_b_ref, *refs):
    pair_ref, next_ref = refs[-2:]
    low, high = halo_along_y(y_b_ref, y_a_ref)
    last = PLANE - SIDE
    first = jnp.concatenate([low[:SIDE], ends_ref[0].astype(F32), high[:SIDE]], axis=0)
    final = jnp.concatenate([low[last:], ends_ref[1].astype(F32), high[last:]], axis=0)
    even = parity("tx")
    pair_ref[...] = jnp.where(even, final, first).astype(BF16)
    next_ref[...] = jnp.where(even, first, final).astype(BF16)


def store_edges(low, high, edge_ref, a_ref, b_ref, planes_ref):
    even_y = parity("ty")
    planes_ref[0] = low.astype(BF16)
    planes_ref[1] = high.astype(BF16)
    last = PLANE - SIDE
    bottom = jnp.concatenate([low[:SIDE], edge_ref[0].astype(F32), high[:SIDE]], axis=0)
    top = jnp.concatenate([low[last:], edge_ref[1].astype(F32), high[last:]], axis=0)
    a_ref[...] = jnp.where(even_y, top, bottom).astype(BF16)
    b_ref[...] = jnp.where(even_y, bottom, top).astype(BF16)


def hand_on_edge_kernel(flips, first_row, edge_ref, got1_ref, got2_ref, *refs):
    lines, (a_ref, b_ref, planes_ref) = refs[: len(flips)], refs[-3:]
    even = parity("tx")
    pair = picked_face(got1_ref[first_row[0] : first_row[0] + PLANE], got2_ref[first_row[1] : first_row[1] + PLANE])
    place = lax.axis_index("tx") // 2
    behind = jnp.where(even, place - 1, place + 1)
    other = jnp.zeros(pair.shape, F32)
    lane = lane_of(lax.axis_index("tx"), lax.axis_index("ty"))
    for both, line_ref in zip(flips, lines):
        flip = jnp.where(lane == 0, *both)
        face = line_ref[first_row[2] : first_row[2] + PLANE].astype(F32)
        other = jnp.where((place ^ behind) == flip, face, other)
    low, high = jnp.where(even, other, pair), jnp.where(even, pair, other)
    store_edges(low, high, edge_ref, a_ref, b_ref, planes_ref)


def picked_face(by_first_way, by_core):
    lane = lane_of(lax.axis_index("tx"), lax.axis_index("ty"))
    return jnp.where(lane == 0, by_core.astype(F32), by_first_way.astype(F32))


def write_columns(plane, cols_ref):
    channels = plane.shape[1]
    z = lax.broadcasted_iota(jnp.int32, plane.shape, 0) % SIDE
    zeros = jnp.zeros((1, channels), F32)
    before = jnp.where(z == 0, 0.0, jnp.concatenate([zeros, plane[:-1]], axis=0))
    after = jnp.where(z == SIDE - 1, 0.0, jnp.concatenate([plane[1:], zeros], axis=0))
    for dz, moved in enumerate((before, plane, after)):
        for dy in range(3):
            tap = 3 * dy + dz
            window = moved[dy * SIDE : dy * SIDE + PLANE]
            cols_ref[:, tap * channels : (tap + 1) * channels] = window.astype(BF16)


def split3(value):
    high = value.astype(BF16)
    rest = value - high.astype(F32)
    middle = rest.astype(BF16)
    low = (rest - middle.astype(F32)).astype(BF16)
    return high, middle, low


def contract(a, b, dim_a, dim_b):
    return lax.dot_general(a, b, (((dim_a,), (dim_b,)), ((), ())), preferred_element_type=F32)


def voxel_sums(point_ref, teach_ref):
    target = jnp.exp(teach_ref[...].astype(F32))
    target = target / jnp.sum(target, axis=0, keepdims=True)
    classes, points = target.shape
    place = point_ref[...]
    place = (place & 0x11F) | ((place & 0x80) >> 2) | ((place & 0x60) << 1)
    chosen = lax.broadcasted_iota(jnp.int32, (SIDE * PLANE, points), 0) == place
    chosen = jnp.where(chosen, 1.0, 0.0).astype(BF16)
    stack = jnp.concatenate([*split3(target), jnp.ones((classes, points), BF16)], axis=0)
    sums = contract(stack, chosen, 1, 1)
    target_sum = sums[:classes] + sums[classes : 2 * classes] + sums[2 * classes : 3 * classes]
    return jnp.concatenate([target_sum, sums[3 * classes :]], axis=0)


def main_kernel(
    feat_ref, occ_ref, point_ref, teach_ref, weight_ref, y_a_ref, y_b_ref,
    cols_ref, pre_ref, mask_ref, sums_ref,
):
    rows, channels = BY * SIDE, feat_ref.shape[2]
    columns = occupancy_columns(occ_ref, 8)
    low, high = halo_along_y(y_b_ref, y_a_ref)
    for x in range(SIDE):
        plane = []
        for j in range(GY):
            slot, row = x // BX * GY + j, x % BX * rows
            mask = occupancy_mask(columns, slot, row, rows, channels)
            mask_ref[x, j * rows : (j + 1) * rows, :] = mask
            plane.append(feat_ref[slot, row : row + rows, :].astype(F32) * mask)
        here = slice(x * SIDE, (x + 1) * SIDE)
        write_columns(jnp.concatenate([low[here], *plane, high[here]], axis=0), cols_ref.at[x])
    wide, inner = TAPS * channels, SIDE - 1
    sums_ref[...] = voxel_sums(point_ref, teach_ref)

    def product(planes, dx):
        window = cols_ref[planes].reshape(-1, wide)
        matrix = weight_ref[TAPS * dx : TAPS * (dx + 1)].reshape(wide, channels)
        return jnp.dot(window, matrix, preferred_element_type=F32)

    edge = jnp.zeros((PLANE, channels), F32)
    pre = product(slice(0, SIDE), 1)
    pre = pre + jnp.concatenate([edge, product(slice(0, inner), 0)], axis=0)
    pre_ref[...] = pre + jnp.concatenate([product(slice(1, SIDE), 2), edge], axis=0)


def write_terms(cols_ref, ends_ref, gradient, start, stop, terms_ref, first=0):
    channels = gradient.shape[1]
    inner = (SIDE - 1) * PLANE
    for dx in range(3):
        low, high = max(start, TAPS * dx), min(stop, TAPS * (dx + 1))
        if low >= high:
            continue
        lanes = slice((low - TAPS * dx) * channels, (high - TAPS * dx) * channels)

        def term(planes, gradient):
            return contract(planes.reshape(gradient.shape[0], -1), gradient, 0, 0)

        if dx == 0:
            total = term(cols_ref[: SIDE - 1, :, lanes], gradient[PLANE:])
            total = total + term(ends_ref[0, :, lanes], gradient[:PLANE])
        elif dx == 1:
            total = term(cols_ref[:, :, lanes], gradient)
        else:
            total = term(cols_ref[1:, :, lanes], gradient[:inner])
            total = total + term(ends_ref[1, :, lanes], gradient[inner:])
        terms_ref[(low - first) * channels : (high - first) * channels] = total


def for_quarter(body):
    for i in range(PARTS // 2):
        pl.when((part_index(PARTS - 2) >> 1) == i)(functools.partial(body, i))


def tile_kernel(
    cols_ref, pre_ref, mask_ref, sums_ref, head_ref, weight_ref, x_next_ref, x_pair_ref,
    grad_ref, ends_ref, first_ref,
    terms_ref,
):
    channels = cols_ref.shape[2] // TAPS
    classes = head_ref.shape[0]
    voxels, wide, inner = SIDE * PLANE, TAPS * channels, (SIDE - 1) * PLANE
    even = parity("tx")
    pair, other = x_pair_ref[...].astype(F32), x_next_ref[...].astype(F32)
    write_columns(jnp.where(even, other, pair), ends_ref.at[0])
    write_columns(jnp.where(even, pair, other), ends_ref.at[1])
    first = weight_ref[:TAPS].reshape(wide, channels)
    final = weight_ref[2 * TAPS :].reshape(wide, channels)
    low = pre_ref[:PLANE] + jnp.dot(ends_ref[0], first, preferred_element_type=F32)
    high = pre_ref[inner:] + jnp.dot(ends_ref[1], final, preferred_element_type=F32)
    pre = jnp.concatenate([low, pre_ref[PLANE:inner], high], axis=0)
    mask = mask_ref[...].reshape(voxels, channels)
    logistic = 1.0 / (1.0 + jnp.exp(-pre))
    slope = logistic * (1.0 + pre * (1.0 - logistic)) * mask
    hidden = (pre / (1.0 + jnp.exp(-pre)) * mask).astype(BF16)

    logits = contract(head_ref[...], hidden, 1, 1)
    student = jnp.exp(logits)
    student = student / jnp.sum(student, axis=0, keepdims=True)
    target_sum, count = sums_ref[:classes], sums_ref[classes:]
    slope_logits = jnp.where(count > 0.0, count * student, 0.0) - target_sum
    heads = jnp.concatenate([head_ref[...]] * 3, axis=0)
    pieces = jnp.concatenate([piece.astype(F32) for piece in split3(slope_logits)], axis=0)
    dhidden = contract(pieces.T.astype(BF16), heads, 1, 0)
    rounded = (dhidden * slope).astype(BF16)
    grad_ref[...] = rounded.reshape(SIDE, PLANE, channels)
    length = 3 * TAPS * channels // PARTS
    even = parity("tx")
    low, high = rounded[:PLANE].astype(F32), rounded[inner:].astype(F32)
    first_ref[2 * length : 2 * length + PLANE] = jnp.where(even, high, low).astype(BF16)
    first_ref[2 * length + PLANE :] = jnp.where(even, low, high).astype(BF16)

    def parts(i):
        start = 2 * length * i // channels
        stop = -(-2 * length * (i + 1) // channels)
        write_terms(cols_ref, ends_ref, rounded, start, stop, terms_ref, start)
        for r in range(2):
            row = 2 * length * i - start * channels + (part_index(PARTS - 2 + r) & 1) * length
            part = terms_ref[pl.ds(pl.multiple_of(row, 16), length)]
            first_ref[r * length : (r + 1) * length] = part.astype(BF16)

    for_quarter(parts)


def terms_kernel(
    cols_ref, ends_ref, grad_ref, edge_ref, keep_ref, rest_ref, terms_ref
):
    channels = grad_ref.shape[2]
    length = terms_ref.shape[0] // PARTS
    gradient = grad_ref[...].reshape(-1, channels)
    low_y, high_y = y_faces(lambda x: grad_ref[x].astype(F32))
    edge_ref[0] = low_y.astype(BF16)
    edge_ref[1] = high_y.astype(BF16)

    def parts(i):
        stop = -(-2 * length * i // channels)
        start = 2 * length * (i + 1) // channels
        write_terms(cols_ref, ends_ref, gradient, 0, stop, terms_ref)
        write_terms(cols_ref, ends_ref, gradient, start, 3 * TAPS, terms_ref)

    for_quarter(parts)
    for r in range(PARTS - 2):
        part = terms_ref[pl.ds(pl.multiple_of(part_index(r) * length, 16), length)]
        if r < PARTS // 2:
            keep_ref[r * length : (r + 1) * length] = part
        else:
            row = (r - PARTS // 2) * length
            rest_ref[row : row + length] = part.astype(BF16)


def lane_of(tx, ty):
    return (ty ^ (ty >> 1) ^ tx ^ (tx >> 1)) & 1


def part_index(r):
    tx, ty = lax.axis_index("tx"), lax.axis_index("ty")
    lane, across, along = lane_of(tx, ty) ^ (r >> 2), (ty >> 1) & 1, tx & 1
    first = jnp.where(lane == 0, across, along)
    second = jnp.where(lane == 0, along, across)
    return lane * 4 + ((first * 2 + second) ^ (r & 3))


def moved_weights(weight_ref, taps):
    return jnp.concatenate([weight_ref[3 * TAPS - 1 - tap] for tap in taps], axis=1)


def back_kernel(grad_ref, planes_ref, weight_ref, part_ref, cols_ref):
    channels = grad_ref.shape[2]
    edge = jnp.zeros((SIDE, channels), F32)
    for x in range(SIDE + 2):
        plane = planes_ref[0 if x == 0 else 1] if x in (0, SIDE + 1) else grad_ref[x - 1]
        write_columns(jnp.concatenate([edge, plane.astype(F32), edge], axis=0), cols_ref.at[x])
    total = jnp.zeros(part_ref.shape, F32)
    for dx in range(3):
        window = cols_ref[dx : dx + SIDE].reshape(-1, TAPS * channels)
        taps = range(TAPS * dx, TAPS * (dx + 1))
        total = total + contract(window, moved_weights(weight_ref, taps), 1, 1)
    part_ref[...] = total


def squares(ref, rows):
    value = ref[:rows].astype(F32)
    return jnp.sum(value * value, axis=0, keepdims=True)


def y_faces_kernel(
    extra_ref, part_ref, mask_ref, weight_ref, near_ref, far_ref, line_ref, *refs
):
    pieces, (out_ref, squares_ref, cols_ref) = refs[:-3], refs[-3:]
    channels, rows = part_ref.shape[1], (SIDE + 2) * SIDE
    tx, ty = lax.axis_index("tx"), lax.axis_index("ty")
    total = sum(squares(ref, near_ref.shape[0] - rows) for ref in pieces)
    squares_ref[...] = jnp.broadcast_to(total, squares_ref.shape)
    by_first, by_second = far_ref[far_ref.shape[0] - rows :], line_ref[line_ref.shape[0] - rows :]
    other = jnp.where(lane_of(tx, ty) == 0, by_first.astype(F32), by_second.astype(F32))
    beyond = jnp.zeros(other.shape, F32) if extra_ref is None else extra_ref[...].astype(F32)
    other = jnp.where(((ty + 1) & 2) == 2, other, beyond)
    pair = near_ref[near_ref.shape[0] - rows :].astype(F32)
    even = parity("ty")
    added = []
    for dy, face in ((0, jnp.where(even, other, pair)), (2, jnp.where(even, pair, other))):
        write_columns(face, cols_ref)
        taps = [TAPS * dx + 3 * dy + dz for dx in range(3) for dz in range(3)]
        added.append(contract(cols_ref[...], moved_weights(weight_ref, taps), 1, 1))
    low, high = added
    rows = BY * SIDE
    for x in range(SIDE):
        here = slice(x * SIDE, (x + 1) * SIDE)
        total = part_ref[x * PLANE : (x + 1) * PLANE]
        first, final = total[:SIDE] + low[here], total[PLANE - SIDE :] + high[here]
        total = jnp.concatenate([first, total[SIDE : PLANE - SIDE], final], axis=0)
        total = (total * mask_ref[x]).astype(BF16)
        for j in range(GY):
            slot, a = x // BX * GY + j, x % BX
            out_ref[slot, a * rows : (a + 1) * rows, :] = total[j * rows : (j + 1) * rows]


def norm_kernel(*refs):
    pieces, refs = refs[:PARTS], refs[PARTS:]
    squares_ref, grad_ref, out_hbm, grad_hbm, out_ref, semaphores = refs
    copies = [pltpu.make_async_copy(grad_ref, grad_hbm, semaphores.at[PARTS])]
    copies[0].start()
    rows, channels = out_ref.shape[1:]
    total = squares_ref[:1] + squares(pieces[-1], rows)
    mean = jnp.sum(total, axis=1, keepdims=True) / (PARTS * rows * channels)
    scale = jnp.broadcast_to(1.0 / jnp.sqrt(mean + 1e-06), (1, channels))
    for r, piece in enumerate(pieces):
        out_ref[r] = piece[:rows].astype(F32) * scale
        first = pl.multiple_of(part_index(r) * rows, 16)
        target = out_hbm.at[pl.ds(first, rows)]
        copies.append(pltpu.make_async_copy(out_ref.at[r], target, semaphores.at[r]))
        copies[-1].start()
    for copy in copies:
        copy.wait()


def swap_pairs(first, count):
    return [pair for i in range(first, count - 1, 2) for pair in ((i, i + 1), (i + 1, i))]


def swap_along_y(b, a):
    count = lax.axis_size("ty")
    got_a = lax.ppermute(a, "ty", swap_pairs(0, count))
    return lax.ppermute(b, "ty", swap_pairs(1, count)), got_a


def edge_faces(kernel, edges, faces, waits=()):
    face = shape(((SIDE + 2) * SIDE, edges.shape[2]), BF16)
    return pl.pallas_call(
        kernel,
        out_shape=(face, face, shape(edges.shape, BF16)),
        in_specs=vmem(1 + len(faces)) + [pl.BlockSpec(memory_space=pl.ANY)] * len(waits),
        out_specs=tuple(vmem(3)),
        compiler_params=pltpu.CompilerParams(vmem_limit_bytes=16 * 2**20),
        name="edge_faces",
    )(edges, *faces, *waits)


def exchange_with(value, partner):
    n_tx, n_ty = lax.axis_size("tx"), lax.axis_size("ty")
    pairs = []
    for tx in range(n_tx):
        for ty in range(n_ty):
            other = partner(tx, ty)
            if other is not None:
                pairs.append((tx * n_ty + ty, other[0] * n_ty + other[1]))
    return lax.ppermute(value, ("tx", "ty"), pairs)


def by_core(tx, ty):
    return tx, ty ^ 1


def same_lane(tx, ty, other_tx, other_ty):
    return other_tx, other_ty ^ lane_of(tx, ty) ^ lane_of(other_tx, other_ty)


def first_way(tx, ty):
    other = (tx, ty ^ 2) if lane_of(tx, ty) == 0 else (tx ^ 1, ty)
    return same_lane(tx, ty, *other)


def second_way(tx, ty):
    other = (tx ^ 1, ty) if lane_of(tx, ty) == 0 else (tx, ty ^ 2)
    return same_lane(tx, ty, *other)


def along_line(flips):
    return lambda tx, ty: same_lane(tx, ty, tx ^ (2 * flips[lane_of(tx, ty)]), ty)


def add(*terms):
    total = terms[0]
    for term in terms[1:]:
        total = total + term
    return total


def message(sections, waits=(), passes=()):
    arrays = []
    for _, _, *terms in sections:
        for array, _ in terms:
            if not any(array is known for known in arrays):
                arrays.append(array)
    place = [[next(i for i, x in enumerate(arrays) if x is array) for array, _ in terms] for _, _, *terms in sections]
    count, others = len(arrays), len(waits) + len(passes)
    total_rows = sum(section[0] for section in sections)

    def body(*refs):
        out_ref, row = refs[count + others], 0
        for places, (rows, fn, *terms) in zip(place, sections):
            values = [refs[i][first : first + rows].astype(F32) for i, (_, first) in zip(places, terms)]
            out_ref[row : row + rows] = fn(*values).astype(BF16)
            row += rows

    plain = pl.BlockSpec(memory_space=pl.ANY)
    outs = [shape((total_rows, arrays[0].shape[1]), BF16)]
    out, *passed = pl.pallas_call(
        body,
        out_shape=outs + [shape(x.shape, x.dtype) for x in passes],
        in_specs=vmem(count) + [plain] * others,
        out_specs=vmem(1) + [plain] * len(passes),
        input_output_aliases={count + len(waits) + i: 1 + i for i in range(len(passes))},
        compiler_params=pltpu.CompilerParams(vmem_limit_bytes=16 * 2**20),
        name="message",
    )(*arrays, *waits, *passes)
    return (out, *passed) if passes else out


def after(value, token):
    plain = pl.BlockSpec(memory_space=pl.ANY)
    return pl.pallas_call(
        lambda value_ref, token_ref, out_ref: None,
        out_shape=shape(value.shape, value.dtype),
        in_specs=[plain] * 2,
        out_specs=plain,
        input_output_aliases={0: 0},
        compiler_params=pltpu.CompilerParams(vmem_limit_bytes=16 * 2**20),
        name="after",
    )(value, token)


def on_device(features, occupancy, neighbors, point_voxel, conv_weight, head_weight, teacher):
    slots, brick, channels = features.shape
    kernels = conv_weight.shape[0]
    n_tx, n_ty = lax.axis_size("tx"), lax.axis_size("ty")
    edges = shape((2, PLANE, channels), BF16)
    cols = pltpu.VMEM((SIDE + 2, PLANE, TAPS * channels), BF16)

    points = point_voxel.reshape(1, -1)
    fetched = (features, occupancy)
    face = shape((PLANE, channels), BF16)
    wide_face = shape(((SIDE + 2) * SIDE, channels), BF16)
    planes = shape((SIDE, PLANE, channels), F32)
    y_b, y_a, x_ends, feat, occ = call(
        first_faces_kernel,
        (face, face, edges, *[shape(x.shape, x.dtype) for x in fetched]),
        fetched,
        (pltpu.SemaphoreType.DMA((len(fetched),)),),
        name="first_faces",
        fetched=len(fetched),
    )
    fetched = (points, teacher, head_weight, conv_weight)
    point, teach, head, weight = call(
        fetch_kernel,
        tuple(shape(x.shape, x.dtype) for x in fetched),
        (*fetched, x_ends),
        (pltpu.SemaphoreType.DMA((len(fetched),)),),
        name="fetch",
        fetched=len(fetched),
    )
    y_b, y_a = swap_along_y(y_b, y_a)
    x_pair, x_next = pl.pallas_call(
        x_faces_kernel,
        out_shape=(wide_face, wide_face),
        in_specs=vmem(3) + [pl.BlockSpec(memory_space=pl.ANY)],
        out_specs=tuple(vmem(2)),
        compiler_params=pltpu.CompilerParams(vmem_limit_bytes=16 * 2**20),
        name="x_faces",
    )(x_ends, y_a, y_b, weight)
    x_next = lax.ppermute(x_next, "tx", swap_pairs(1, n_tx))
    x_pair = lax.ppermute(x_pair, "tx", swap_pairs(0, n_tx))
    tile_cols, pre, mask, sums = call(
        main_kernel,
        (
            shape((SIDE, PLANE, TAPS * channels), BF16),
            shape((SIDE * PLANE, channels), F32),
            planes,
            shape((2 * head_weight.shape[0], SIDE * PLANE), F32),
        ),
        (feat, occ, point, teach, weight, y_a, y_b),
        name="main",
    )
    part = kernels * channels // PARTS
    ends = shape((2, PLANE, TAPS * channels), BF16)
    gradient, ends, first = call(
        tile_kernel,
        (shape((SIDE, PLANE, channels), BF16), ends, shape((2 * part + 2 * PLANE, channels), BF16)),
        (tile_cols, pre, mask, sums, head, weight, x_next, x_pair),
        (pltpu.VMEM((2 * part + 2 * channels, channels), F32),),
        name="tile",
    )
    g_edges, keep, rest = call(
        terms_kernel,
        (
            edges,
            shape((PARTS // 2 * part, channels), F32),
            shape((2 * part, channels), BF16),
        ),
        (tile_cols, ends, gradient),
        (pltpu.VMEM((kernels * channels, channels), F32),),
        name="terms",
    )

    got_first = exchange_with(first, by_core)
    got_rest = exchange_with(rest, by_core)
    onward = message([(part, add, (keep, 3 * part), (got_first, part))])
    got_onward = exchange_with(onward, first_way)
    pair, following = 2 * part, 2 * part + PLANE
    planes = [(got_first, pair), (first, following), (first, pair), (got_first, following)]
    got1 = exchange_with(
        message(
            [(part, add, (keep, 2 * part), (got_first, 0))]
            + [(PLANE, add, plane) for plane in planes]
        ),
        first_way,
    )
    kept = [(part, add, (keep, part), (got_rest, part), (got_onward, 0))]
    got2 = exchange_with(message(kept), second_way)
    x_faces = exchange_with(message([(2 * PLANE, add, (got1, part + 2 * PLANE))]), by_core)
    at = (part, 0, part)
    hand_on = (PLANE, picked_face, (got1, part + PLANE), (x_faces, PLANE))
    total = [(part, add, (keep, 0), (got_rest, 0), (got1, 0), (got2, 0))]
    flips, lines = [], []
    while 2 ** len(flips) < n_tx // 2:
        flips.append(2 ** (len(flips) + 1) - 1)
    flips = list(zip(flips[::-1], flips))
    for both in flips:
        own = message(total + [hand_on])
        lines.append(exchange_with(own, along_line(both)))
        total = [(part, add, (own, 0), (lines[-1], 0))]
        hand_on = (PLANE, add, (own, part))
    bit = 4
    while bit < n_ty:
        own = message(total)
        flip = 2 * bit - 4
        got = exchange_with(own, lambda tx, ty, flip=flip: same_lane(tx, ty, tx, ty ^ flip))
        total = [(part, add, (own, 0), (got, 0))]
        bit *= 2
    kernel = functools.partial(hand_on_edge_kernel, flips, at)
    g_a, g_b, planes = edge_faces(kernel, g_edges, (got1, x_faces, *lines))
    rows = g_a.shape[0]
    total, gradient = message(total + [(rows, add, (g_b, 0))], (), (gradient,))
    piece1 = exchange_with(total, second_way)
    back_part = call(
        back_kernel,
        shape((SIDE * PLANE, channels), F32),
        (gradient, planes, weight),
        (cols,),
        name="back",
    )
    piece2 = exchange_with(message([(part + rows, add, (total, 0))], (back_part,)), first_way)
    onward = message([(part, add, (piece1, 0))])
    piece3 = exchange_with(onward, first_way)
    near = message([(part, add, (piece2, 0)), (rows, add, (g_a, 0))])
    pieces = (total, piece1, near, piece3)
    late = message([(part, add, (total, 0))], (near,))
    others = [exchange_with(piece, by_core) for piece in (late, *pieces[1:])]
    faces = (back_part, mask, weight, others[2], piece2, piece1, *pieces, *others[:3])
    kernel = functools.partial(y_faces_kernel, None)
    if n_ty > 4:
        pairs = [pair for i in range(3, n_ty - 1, 4) for pair in ((i, i + 1), (i + 1, i))]
        faces = (lax.ppermute(g_b, "ty", pairs), *faces)
        kernel = y_faces_kernel
    grad_features, squares_of = call(
        kernel,
        (shape((slots, brick, channels), BF16), shape((8, channels), F32)),
        faces,
        (pltpu.VMEM((PLANE, TAPS * channels), BF16),),
        name="y_faces",
    )
    grad_weight, grad_features = pl.pallas_call(
        norm_kernel,
        out_shape=(
            shape((kernels * channels, channels), F32),
            shape((slots, brick, channels), BF16),
        ),
        in_specs=vmem(PARTS + 2),
        out_specs=(pl.BlockSpec(memory_space=pltpu.HBM),) * 2,
        scratch_shapes=[
            pltpu.VMEM((PARTS, part, channels), F32),
            pltpu.SemaphoreType.DMA((PARTS + 1,)),
        ],
        compiler_params=pltpu.CompilerParams(vmem_limit_bytes=16 * 2**20),
        name="normalise",
    )(*pieces, *others, squares_of, grad_features)
    return (grad_features, grad_weight.reshape(conv_weight.shape))


def solution(mesh):
    in_specs = (
        P(("tx", "ty"), None, None),
        P(("tx", "ty"), None),
        P(None, ("tx", "ty")),
        P(("tx", "ty")),
        P(),
        P(),
        P(None, ("tx", "ty")),
    )
    out_specs = (P(("tx", "ty"), None, None), P())
    return jax.shard_map(
        on_device, mesh=mesh, in_specs=in_specs, out_specs=out_specs, check_vma=False
    )
```

```python
import functools

import jax
import jax.numpy as jnp
from jax import lax
from jax.experimental import pallas as pl
from jax.experimental.pallas import tpu as pltpu
from jax.sharding import PartitionSpec as P

GX = 2
GY = 2
BX = 4
BY = 4
SIDE = 8
PLANE = SIDE * SIDE
TAPS = 9
BF16 = jnp.bfloat16
F32 = jnp.float32
PARTS = 8


def vmem(count):
    return [pl.BlockSpec(memory_space=pltpu.VMEM)] * count


def pin(array):
    return pltpu.with_memory_space_constraint(array, pltpu.HBM)


def call(body, outs, inputs, scratch=(), limit=32 * 2**20, name=None, fetched=0):
    return pl.pallas_call(
        body,
        out_shape=outs,
        in_specs=[pl.BlockSpec(memory_space=pltpu.HBM)] * fetched + vmem(len(inputs) - fetched),
        out_specs=jax.tree.map(lambda _: pl.BlockSpec(memory_space=pltpu.VMEM), outs),
        scratch_shapes=list(scratch),
        compiler_params=pltpu.CompilerParams(vmem_limit_bytes=limit),
        name=name,
    )(*[pin(array) for array in inputs[:fetched]], *inputs[fetched:])


def fetch(sources, rooms, semaphores):
    copies = [
        pltpu.make_async_copy(source, room, semaphores.at[i])
        for i, (source, room) in enumerate(zip(sources, rooms))
    ]
    for copy in copies:
        copy.start()
    return copies


def shape(dims, dtype):
    return jax.ShapeDtypeStruct(dims, dtype)


def parity(axis):
    return lax.rem(lax.axis_index(axis), 2) == 0


def occupancy_columns(occ_ref, rows):
    occ = occ_ref[...].astype(F32)
    padded = jnp.concatenate([occ, jnp.zeros((8 - occ.shape[0], occ.shape[1]), F32)], axis=0)
    return padded.T


def y_faces(planes):
    low = jnp.concatenate([planes(x)[:SIDE] for x in range(SIDE)], axis=0)
    high = jnp.concatenate([planes(x)[PLANE - SIDE :] for x in range(SIDE)], axis=0)
    return low, high


def occupancy_mask(columns, slot, first, rows, channels):
    return jnp.broadcast_to(columns[first : first + rows, slot : slot + 1], (rows, channels))


def first_faces_kernel(
    feat_hbm, occ_hbm, b_ref, a_ref, ends_ref, feat_ref, occ_ref, semaphores
):
    for copy in fetch((feat_hbm, occ_hbm), (feat_ref, occ_ref), semaphores):
        copy.wait()
    columns = occupancy_columns(occ_ref, 8)
    rows, channels = BY * SIDE, feat_ref.shape[2]

    def masked(x, j, first, count):
        slot, row = x // BX * GY + j, x % BX * rows + first
        mask = occupancy_mask(columns, slot, row, count, channels)
        return feat_ref[slot, row : row + count, :].astype(F32) * mask

    low_y = jnp.concatenate([masked(x, 0, 0, SIDE) for x in range(SIDE)], axis=0)
    high_y = jnp.concatenate([masked(x, GY - 1, rows - SIDE, SIDE) for x in range(SIDE)], axis=0)
    even = parity("ty")
    a_ref[...] = jnp.where(even, high_y, low_y).astype(BF16)
    b_ref[...] = jnp.where(even, low_y, high_y).astype(BF16)
    for i, x in enumerate((0, SIDE - 1)):
        plane = jnp.concatenate([masked(x, j, 0, rows) for j in range(GY)], axis=0)
        ends_ref[i] = plane.astype(BF16)


def fetch_kernel(*refs):
    count = len(refs) // 2 - 1
    for copy in fetch(refs[:count], refs[count + 1 : -1], refs[-1]):
        copy.wait()


def halo_along_y(b_ref, a_ref):
    even = parity("ty")
    a, b = a_ref[...].astype(F32), b_ref[...].astype(F32)
    return jnp.where(even, b, a), jnp.where(even, a, b)


def x_faces_kernel(ends_ref, y_a_ref, y_b_ref, *refs):
    pair_ref, next_ref = refs[-2:]
    low, high = halo_along_y(y_b_ref, y_a_ref)
    last = PLANE - SIDE
    first = jnp.concatenate([low[:SIDE], ends_ref[0].astype(F32), high[:SIDE]], axis=0)
    final = jnp.concatenate([low[last:], ends_ref[1].astype(F32), high[last:]], axis=0)
    even = parity("tx")
    pair_ref[...] = jnp.where(even, final, first).astype(BF16)
    next_ref[...] = jnp.where(even, first, final).astype(BF16)


def store_edges(low, high, edge_ref, a_ref, b_ref, planes_ref):
    even_y = parity("ty")
    planes_ref[0] = low.astype(BF16)
    planes_ref[1] = high.astype(BF16)
    last = PLANE - SIDE
    bottom = jnp.concatenate([low[:SIDE], edge_ref[0].astype(F32), high[:SIDE]], axis=0)
    top = jnp.concatenate([low[last:], edge_ref[1].astype(F32), high[last:]], axis=0)
    a_ref[...] = jnp.where(even_y, top, bottom).astype(BF16)
    b_ref[...] = jnp.where(even_y, bottom, top).astype(BF16)


def hand_on_edge_kernel(flips, first_row, edge_ref, got1_ref, got2_ref, *refs):
    lines, (a_ref, b_ref, planes_ref) = refs[: len(flips)], refs[-3:]
    even = parity("tx")
    pair = picked_face(got1_ref[first_row[0] : first_row[0] + PLANE], got2_ref[first_row[1] : first_row[1] + PLANE])
    place = lax.axis_index("tx") // 2
    behind = jnp.where(even, place - 1, place + 1)
    other = jnp.zeros(pair.shape, F32)
    lane = lane_of(lax.axis_index("tx"), lax.axis_index("ty"))
    for both, line_ref in zip(flips, lines):
        flip = jnp.where(lane == 0, *both)
        face = line_ref[first_row[2] : first_row[2] + PLANE].astype(F32)
        other = jnp.where((place ^ behind) == flip, face, other)
    low, high = jnp.where(even, other, pair), jnp.where(even, pair, other)
    store_edges(low, high, edge_ref, a_ref, b_ref, planes_ref)


def picked_face(by_first_way, by_core):
    lane = lane_of(lax.axis_index("tx"), lax.axis_index("ty"))
    return jnp.where(lane == 0, by_core.astype(F32), by_first_way.astype(F32))


def write_columns(plane, cols_ref):
    channels = plane.shape[1]
    z = lax.broadcasted_iota(jnp.int32, plane.shape, 0) % SIDE
    zeros = jnp.zeros((1, channels), F32)
    before = jnp.where(z == 0, 0.0, jnp.concatenate([zeros, plane[:-1]], axis=0))
    after = jnp.where(z == SIDE - 1, 0.0, jnp.concatenate([plane[1:], zeros], axis=0))
    for dz, moved in enumerate((before, plane, after)):
        for dy in range(3):
            tap = 3 * dy + dz
            window = moved[dy * SIDE : dy * SIDE + PLANE]
            cols_ref[:, tap * channels : (tap + 1) * channels] = window.astype(BF16)


def split3(value):
    high = value.astype(BF16)
    rest = value - high.astype(F32)
    middle = rest.astype(BF16)
    low = (rest - middle.astype(F32)).astype(BF16)
    return high, middle, low


def contract(a, b, dim_a, dim_b):
    return lax.dot_general(a, b, (((dim_a,), (dim_b,)), ((), ())), preferred_element_type=F32)


def voxel_sums(point_ref, teach_ref):
    target = jnp.exp(teach_ref[...].astype(F32))
    target = target / jnp.sum(target, axis=0, keepdims=True)
    classes, points = target.shape
    place = point_ref[...]
    place = (place & 0x11F) | ((place & 0x80) >> 2) | ((place & 0x60) << 1)
    chosen = lax.broadcasted_iota(jnp.int32, (SIDE * PLANE, points), 0) == place
    chosen = jnp.where(chosen, 1.0, 0.0).astype(BF16)
    stack = jnp.concatenate([*split3(target), jnp.ones((classes, points), BF16)], axis=0)
    sums = contract(stack, chosen, 1, 1)
    target_sum = sums[:classes] + sums[classes : 2 * classes] + sums[2 * classes : 3 * classes]
    return jnp.concatenate([target_sum, sums[3 * classes :]], axis=0)


def main_kernel(
    feat_ref, occ_ref, point_ref, teach_ref, weight_ref, y_a_ref, y_b_ref,
    cols_ref, pre_ref, mask_ref, sums_ref,
):
    rows, channels = BY * SIDE, feat_ref.shape[2]
    columns = occupancy_columns(occ_ref, 8)
    low, high = halo_along_y(y_b_ref, y_a_ref)
    for x in range(SIDE):
        plane = []
        for j in range(GY):
            slot, row = x // BX * GY + j, x % BX * rows
            mask = occupancy_mask(columns, slot, row, rows, channels)
            mask_ref[x, j * rows : (j + 1) * rows, :] = mask
            plane.append(feat_ref[slot, row : row + rows, :].astype(F32) * mask)
        here = slice(x * SIDE, (x + 1) * SIDE)
        write_columns(jnp.concatenate([low[here], *plane, high[here]], axis=0), cols_ref.at[x])
    wide, inner = TAPS * channels, SIDE - 1
    sums_ref[...] = voxel_sums(point_ref, teach_ref)

    def product(planes, dx):
        window = cols_ref[planes].reshape(-1, wide)
        matrix = weight_ref[TAPS * dx : TAPS * (dx + 1)].reshape(wide, channels)
        return jnp.dot(window, matrix, preferred_element_type=F32)

    edge = jnp.zeros((PLANE, channels), F32)
    pre = product(slice(0, SIDE), 1)
    pre = pre + jnp.concatenate([edge, product(slice(0, inner), 0)], axis=0)
    pre_ref[...] = pre + jnp.concatenate([product(slice(1, SIDE), 2), edge], axis=0)


def write_terms(cols_ref, ends_ref, gradient, start, stop, terms_ref, first=0):
    channels = gradient.shape[1]
    inner = (SIDE - 1) * PLANE
    for dx in range(3):
        low, high = max(start, TAPS * dx), min(stop, TAPS * (dx + 1))
        if low >= high:
            continue
        lanes = slice((low - TAPS * dx) * channels, (high - TAPS * dx) * channels)

        def term(planes, gradient):
            return contract(planes.reshape(gradient.shape[0], -1), gradient, 0, 0)

        if dx == 0:
            total = term(cols_ref[: SIDE - 1, :, lanes], gradient[PLANE:])
            total = total + term(ends_ref[0, :, lanes], gradient[:PLANE])
        elif dx == 1:
            total = term(cols_ref[:, :, lanes], gradient)
        else:
            total = term(cols_ref[1:, :, lanes], gradient[:inner])
            total = total + term(ends_ref[1, :, lanes], gradient[inner:])
        terms_ref[(low - first) * channels : (high - first) * channels] = total


def for_quarter(body):
    for i in range(PARTS // 2):
        pl.when((part_index(PARTS - 2) >> 1) == i)(functools.partial(body, i))


def tile_kernel(
    cols_ref, pre_ref, mask_ref, sums_ref, head_ref, weight_ref, x_next_ref, x_pair_ref,
    grad_ref, ends_ref, first_ref,
    terms_ref,
):
    channels = cols_ref.shape[2] // TAPS
    classes = head_ref.shape[0]
    voxels, wide, inner = SIDE * PLANE, TAPS * channels, (SIDE - 1) * PLANE
    even = parity("tx")
    pair, other = x_pair_ref[...].astype(F32), x_next_ref[...].astype(F32)
    write_columns(jnp.where(even, other, pair), ends_ref.at[0])
    write_columns(jnp.where(even, pair, other), ends_ref.at[1])
    first = weight_ref[:TAPS].reshape(wide, channels)
    final = weight_ref[2 * TAPS :].reshape(wide, channels)
    low = pre_ref[:PLANE] + jnp.dot(ends_ref[0], first, preferred_element_type=F32)
    high = pre_ref[inner:] + jnp.dot(ends_ref[1], final, preferred_element_type=F32)
    pre = jnp.concatenate([low, pre_ref[PLANE:inner], high], axis=0)
    mask = mask_ref[...].reshape(voxels, channels)
    logistic = 1.0 / (1.0 + jnp.exp(-pre))
    slope = logistic * (1.0 + pre * (1.0 - logistic)) * mask
    hidden = (pre / (1.0 + jnp.exp(-pre)) * mask).astype(BF16)

    logits = contract(head_ref[...], hidden, 1, 1)
    student = jnp.exp(logits)
    student = student / jnp.sum(student, axis=0, keepdims=True)
    target_sum, count = sums_ref[:classes], sums_ref[classes:]
    slope_logits = jnp.where(count > 0.0, count * student, 0.0) - target_sum
    heads = jnp.concatenate([head_ref[...]] * 3, axis=0)
    pieces = jnp.concatenate([piece.astype(F32) for piece in split3(slope_logits)], axis=0)
    dhidden = contract(pieces.T.astype(BF16), heads, 1, 0)
    rounded = (dhidden * slope).astype(BF16)
    grad_ref[...] = rounded.reshape(SIDE, PLANE, channels)
    length = 3 * TAPS * channels // PARTS
    even = parity("tx")
    low, high = rounded[:PLANE].astype(F32), rounded[inner:].astype(F32)
    first_ref[2 * length : 2 * length + PLANE] = jnp.where(even, high, low).astype(BF16)
    first_ref[2 * length + PLANE :] = jnp.where(even, low, high).astype(BF16)

    def parts(i):
        start = 2 * length * i // channels
        stop = -(-2 * length * (i + 1) // channels)
        write_terms(cols_ref, ends_ref, rounded, start, stop, terms_ref, start)
        for r in range(2):
            row = 2 * length * i - start * channels + (part_index(PARTS - 2 + r) & 1) * length
            part = terms_ref[pl.ds(pl.multiple_of(row, 16), length)]
            first_ref[r * length : (r + 1) * length] = part.astype(BF16)

    for_quarter(parts)


def terms_kernel(
    cols_ref, ends_ref, grad_ref, edge_ref, keep_ref, rest_ref, terms_ref
):
    channels = grad_ref.shape[2]
    length = terms_ref.shape[0] // PARTS
    gradient = grad_ref[...].reshape(-1, channels)
    low_y, high_y = y_faces(lambda x: grad_ref[x].astype(F32))
    edge_ref[0] = low_y.astype(BF16)
    edge_ref[1] = high_y.astype(BF16)

    def parts(i):
        stop = -(-2 * length * i // channels)
        start = 2 * length * (i + 1) // channels
        write_terms(cols_ref, ends_ref, gradient, 0, stop, terms_ref)
        write_terms(cols_ref, ends_ref, gradient, start, 3 * TAPS, terms_ref)

    for_quarter(parts)
    for r in range(PARTS - 2):
        part = terms_ref[pl.ds(pl.multiple_of(part_index(r) * length, 16), length)]
        if r < PARTS // 2:
            keep_ref[r * length : (r + 1) * length] = part
        else:
            row = (r - PARTS // 2) * length
            rest_ref[row : row + length] = part.astype(BF16)


def lane_of(tx, ty):
    return (ty ^ (ty >> 1) ^ tx ^ (tx >> 1)) & 1


def part_index(r):
    tx, ty = lax.axis_index("tx"), lax.axis_index("ty")
    lane, across, along = lane_of(tx, ty) ^ (r >> 2), (ty >> 1) & 1, tx & 1
    first = jnp.where(lane == 0, across, along)
    second = jnp.where(lane == 0, along, across)
    return lane * 4 + ((first * 2 + second) ^ (r & 3))


def moved_weights(weight_ref, taps):
    return jnp.concatenate([weight_ref[3 * TAPS - 1 - tap] for tap in taps], axis=1)


def back_kernel(grad_ref, planes_ref, weight_ref, part_ref, cols_ref):
    channels = grad_ref.shape[2]
    edge = jnp.zeros((SIDE, channels), F32)
    for x in range(SIDE + 2):
        plane = planes_ref[0 if x == 0 else 1] if x in (0, SIDE + 1) else grad_ref[x - 1]
        write_columns(jnp.concatenate([edge, plane.astype(F32), edge], axis=0), cols_ref.at[x])
    total = jnp.zeros(part_ref.shape, F32)
    for dx in range(3):
        window = cols_ref[dx : dx + SIDE].reshape(-1, TAPS * channels)
        taps = range(TAPS * dx, TAPS * (dx + 1))
        total = total + contract(window, moved_weights(weight_ref, taps), 1, 1)
    part_ref[...] = total


def squares(ref, rows):
    value = ref[:rows].astype(F32)
    return jnp.sum(value * value, axis=0, keepdims=True)


def y_faces_kernel(
    extra_ref, part_ref, mask_ref, weight_ref, near_ref, far_ref, *refs
):
    pieces, (out_ref, squares_ref, cols_ref) = refs[:-3], refs[-3:]
    channels, rows = part_ref.shape[1], (SIDE + 2) * SIDE
    tx, ty = lax.axis_index("tx"), lax.axis_index("ty")
    part = near_ref.shape[0] - 2 * rows
    total = sum(squares(ref, part) for ref in pieces)
    squares_ref[...] = jnp.broadcast_to(total, squares_ref.shape)
    own, by_core = far_ref[part:].astype(F32), near_ref[part + rows :].astype(F32)
    other = jnp.where(lane_of(tx, ty) == 0, own, by_core)
    beyond = jnp.zeros(other.shape, F32) if extra_ref is None else extra_ref[...].astype(F32)
    other = jnp.where(((ty + 1) & 2) == 2, other, beyond)
    pair = near_ref[part : part + rows].astype(F32)
    even = parity("ty")
    added = []
    for dy, face in ((0, jnp.where(even, other, pair)), (2, jnp.where(even, pair, other))):
        write_columns(face, cols_ref)
        taps = [TAPS * dx + 3 * dy + dz for dx in range(3) for dz in range(3)]
        added.append(contract(cols_ref[...], moved_weights(weight_ref, taps), 1, 1))
    low, high = added
    rows = BY * SIDE
    for x in range(SIDE):
        here = slice(x * SIDE, (x + 1) * SIDE)
        total = part_ref[x * PLANE : (x + 1) * PLANE]
        first, final = total[:SIDE] + low[here], total[PLANE - SIDE :] + high[here]
        total = jnp.concatenate([first, total[SIDE : PLANE - SIDE], final], axis=0)
        total = (total * mask_ref[x]).astype(BF16)
        for j in range(GY):
            slot, a = x // BX * GY + j, x % BX
            out_ref[slot, a * rows : (a + 1) * rows, :] = total[j * rows : (j + 1) * rows]


def norm_kernel(*refs):
    pieces, refs = refs[:PARTS], refs[PARTS:]
    squares_ref, grad_ref, out_hbm, grad_hbm, out_ref, semaphores = refs
    copies = [pltpu.make_async_copy(grad_ref, grad_hbm, semaphores.at[PARTS])]
    copies[0].start()
    rows, channels = out_ref.shape[1:]
    total = squares_ref[:1] + squares(pieces[-1], rows)
    mean = jnp.sum(total, axis=1, keepdims=True) / (PARTS * rows * channels)
    scale = jnp.broadcast_to(1.0 / jnp.sqrt(mean + 1e-06), (1, channels))
    for r, piece in enumerate(pieces):
        out_ref[r] = piece[:rows].astype(F32) * scale
        first = pl.multiple_of(part_index(r) * rows, 16)
        target = out_hbm.at[pl.ds(first, rows)]
        copies.append(pltpu.make_async_copy(out_ref.at[r], target, semaphores.at[r]))
        copies[-1].start()
    for copy in copies:
        copy.wait()


def swap_pairs(first, count):
    return [pair for i in range(first, count - 1, 2) for pair in ((i, i + 1), (i + 1, i))]


def swap_along_y(b, a):
    count = lax.axis_size("ty")
    got_a = lax.ppermute(a, "ty", swap_pairs(0, count))
    return lax.ppermute(b, "ty", swap_pairs(1, count)), got_a


def edge_faces(kernel, edges, faces, waits=()):
    face = shape(((SIDE + 2) * SIDE, edges.shape[2]), BF16)
    return pl.pallas_call(
        kernel,
        out_shape=(face, face, shape(edges.shape, BF16)),
        in_specs=vmem(1 + len(faces)) + [pl.BlockSpec(memory_space=pl.ANY)] * len(waits),
        out_specs=tuple(vmem(3)),
        compiler_params=pltpu.CompilerParams(vmem_limit_bytes=16 * 2**20),
        name="edge_faces",
    )(edges, *faces, *waits)


def exchange_with(value, partner):
    n_tx, n_ty = lax.axis_size("tx"), lax.axis_size("ty")
    pairs = []
    for tx in range(n_tx):
        for ty in range(n_ty):
            other = partner(tx, ty)
            if other is not None:
                pairs.append((tx * n_ty + ty, other[0] * n_ty + other[1]))
    return lax.ppermute(value, ("tx", "ty"), pairs)


def by_core(tx, ty):
    return tx, ty ^ 1


def same_lane(tx, ty, other_tx, other_ty):
    return other_tx, other_ty ^ lane_of(tx, ty) ^ lane_of(other_tx, other_ty)


def first_way(tx, ty):
    other = (tx, ty ^ 2) if lane_of(tx, ty) == 0 else (tx ^ 1, ty)
    return same_lane(tx, ty, *other)


def second_way(tx, ty):
    other = (tx ^ 1, ty) if lane_of(tx, ty) == 0 else (tx, ty ^ 2)
    return same_lane(tx, ty, *other)


def along_line(flips):
    return lambda tx, ty: same_lane(tx, ty, tx ^ (2 * flips[lane_of(tx, ty)]), ty)


def inner_face(own, other):
    inner = ((lax.axis_index("ty") + 1) & 2) == 2
    return jnp.where(inner, own, other)


def add(*terms):
    total = terms[0]
    for term in terms[1:]:
        total = total + term
    return total


def message(sections, waits=(), passes=()):
    arrays = []
    for _, _, *terms in sections:
        for array, _ in terms:
            if not any(array is known for known in arrays):
                arrays.append(array)
    place = [[next(i for i, x in enumerate(arrays) if x is array) for array, _ in terms] for _, _, *terms in sections]
    count, others = len(arrays), len(waits) + len(passes)
    total_rows = sum(section[0] for section in sections)

    def body(*refs):
        out_ref, row = refs[count + others], 0
        for places, (rows, fn, *terms) in zip(place, sections):
            values = [refs[i][first : first + rows].astype(F32) for i, (_, first) in zip(places, terms)]
            out_ref[row : row + rows] = fn(*values).astype(BF16)
            row += rows

    plain = pl.BlockSpec(memory_space=pl.ANY)
    outs = [shape((total_rows, arrays[0].shape[1]), BF16)]
    out, *passed = pl.pallas_call(
        body,
        out_shape=outs + [shape(x.shape, x.dtype) for x in passes],
        in_specs=vmem(count) + [plain] * others,
        out_specs=vmem(1) + [plain] * len(passes),
        input_output_aliases={count + len(waits) + i: 1 + i for i in range(len(passes))},
        compiler_params=pltpu.CompilerParams(vmem_limit_bytes=16 * 2**20),
        name="message",
    )(*arrays, *waits, *passes)
    return (out, *passed) if passes else out


def after(value, token):
    plain = pl.BlockSpec(memory_space=pl.ANY)
    return pl.pallas_call(
        lambda value_ref, token_ref, out_ref: None,
        out_shape=shape(value.shape, value.dtype),
        in_specs=[plain] * 2,
        out_specs=plain,
        input_output_aliases={0: 0},
        compiler_params=pltpu.CompilerParams(vmem_limit_bytes=16 * 2**20),
        name="after",
    )(value, token)


def on_device(features, occupancy, neighbors, point_voxel, conv_weight, head_weight, teacher):
    slots, brick, channels = features.shape
    kernels = conv_weight.shape[0]
    n_tx, n_ty = lax.axis_size("tx"), lax.axis_size("ty")
    edges = shape((2, PLANE, channels), BF16)
    cols = pltpu.VMEM((SIDE + 2, PLANE, TAPS * channels), BF16)

    points = point_voxel.reshape(1, -1)
    fetched = (features, occupancy)
    face = shape((PLANE, channels), BF16)
    wide_face = shape(((SIDE + 2) * SIDE, channels), BF16)
    planes = shape((SIDE, PLANE, channels), F32)
    y_b, y_a, x_ends, feat, occ = call(
        first_faces_kernel,
        (face, face, edges, *[shape(x.shape, x.dtype) for x in fetched]),
        fetched,
        (pltpu.SemaphoreType.DMA((len(fetched),)),),
        name="first_faces",
        fetched=len(fetched),
    )
    fetched = (points, teacher, head_weight, conv_weight)
    point, teach, head, weight = call(
        fetch_kernel,
        tuple(shape(x.shape, x.dtype) for x in fetched),
        (*fetched, x_ends),
        (pltpu.SemaphoreType.DMA((len(fetched),)),),
        name="fetch",
        fetched=len(fetched),
    )
    y_b, y_a = swap_along_y(y_b, y_a)
    x_pair, x_next = pl.pallas_call(
        x_faces_kernel,
        out_shape=(wide_face, wide_face),
        in_specs=vmem(3) + [pl.BlockSpec(memory_space=pl.ANY)],
        out_specs=tuple(vmem(2)),
        compiler_params=pltpu.CompilerParams(vmem_limit_bytes=16 * 2**20),
        name="x_faces",
    )(x_ends, y_a, y_b, weight)
    x_next = lax.ppermute(x_next, "tx", swap_pairs(1, n_tx))
    x_pair = lax.ppermute(x_pair, "tx", swap_pairs(0, n_tx))
    tile_cols, pre, mask, sums = call(
        main_kernel,
        (
            shape((SIDE, PLANE, TAPS * channels), BF16),
            shape((SIDE * PLANE, channels), F32),
            planes,
            shape((2 * head_weight.shape[0], SIDE * PLANE), F32),
        ),
        (feat, occ, point, teach, weight, y_a, y_b),
        name="main",
    )
    part = kernels * channels // PARTS
    ends = shape((2, PLANE, TAPS * channels), BF16)
    gradient, ends, first = call(
        tile_kernel,
        (shape((SIDE, PLANE, channels), BF16), ends, shape((2 * part + 2 * PLANE, channels), BF16)),
        (tile_cols, pre, mask, sums, head, weight, x_next, x_pair),
        (pltpu.VMEM((2 * part + 2 * channels, channels), F32),),
        name="tile",
    )
    g_edges, keep, rest = call(
        terms_kernel,
        (
            edges,
            shape((PARTS // 2 * part, channels), F32),
            shape((2 * part, channels), BF16),
        ),
        (tile_cols, ends, gradient),
        (pltpu.VMEM((kernels * channels, channels), F32),),
        name="terms",
    )

    got_first = exchange_with(first, by_core)
    got_rest = exchange_with(rest, by_core)
    onward = message([(part, add, (keep, 3 * part), (got_first, part))])
    got_onward = exchange_with(onward, first_way)
    pair, following = 2 * part, 2 * part + PLANE
    planes = [(got_first, pair), (first, following), (first, pair), (got_first, following)]
    got1 = exchange_with(
        message(
            [(part, add, (keep, 2 * part), (got_first, 0))]
            + [(PLANE, add, plane) for plane in planes]
        ),
        first_way,
    )
    kept = [(part, add, (keep, part), (got_rest, part), (got_onward, 0))]
    got2 = exchange_with(message(kept), second_way)
    x_faces = exchange_with(message([(2 * PLANE, add, (got1, part + 2 * PLANE))]), by_core)
    at = (part, 0, part)
    hand_on = (PLANE, picked_face, (got1, part + PLANE), (x_faces, PLANE))
    total = [(part, add, (keep, 0), (got_rest, 0), (got1, 0), (got2, 0))]
    flips, lines = [], []
    while 2 ** len(flips) < n_tx // 2:
        flips.append(2 ** (len(flips) + 1) - 1)
    flips = list(zip(flips[::-1], flips))
    for both in flips:
        own = message(total + [hand_on])
        lines.append(exchange_with(own, along_line(both)))
        total = [(part, add, (own, 0), (lines[-1], 0))]
        hand_on = (PLANE, add, (own, part))
    bit = 4
    while bit < n_ty:
        own = message(total)
        flip = 2 * bit - 4
        got = exchange_with(own, lambda tx, ty, flip=flip: same_lane(tx, ty, tx, ty ^ flip))
        total = [(part, add, (own, 0), (got, 0))]
        bit *= 2
    kernel = functools.partial(hand_on_edge_kernel, flips, at)
    g_a, g_b, planes = edge_faces(kernel, g_edges, (got1, x_faces, *lines))
    rows = g_a.shape[0]
    total, gradient = message(total, (), (gradient,))
    piece1 = exchange_with(total, second_way)
    back_part = call(
        back_kernel,
        shape((SIDE * PLANE, channels), F32),
        (gradient, planes, weight),
        (cols,),
        name="back",
    )
    other_b = exchange_with(g_b, by_core)
    face = (rows, inner_face, (g_b, 0), (other_b, 0))
    piece2 = exchange_with(message([(part, add, (total, 0)), face], (back_part,)), first_way)
    piece3 = exchange_with(piece1, first_way)
    near = message([(part, add, (piece2, 0)), (rows, add, (g_a, 0)), (rows, add, (piece2, part))])
    pieces = (total, piece1, near, piece3)
    late = message([(part, add, (total, 0))], (near,))
    others = [exchange_with(piece, by_core) for piece in (late, *pieces[1:])]
    faces = (back_part, mask, weight, others[2], piece2, *pieces, *others[:3])
    kernel = functools.partial(y_faces_kernel, None)
    if n_ty > 4:
        pairs = [pair for i in range(3, n_ty - 1, 4) for pair in ((i, i + 1), (i + 1, i))]
        faces = (lax.ppermute(g_b, "ty", pairs), *faces)
        kernel = y_faces_kernel
    grad_features, squares_of = call(
        kernel,
        (shape((slots, brick, channels), BF16), shape((8, channels), F32)),
        faces,
        (pltpu.VMEM((PLANE, TAPS * channels), BF16),),
        name="y_faces",
    )
    grad_weight, grad_features = pl.pallas_call(
        norm_kernel,
        out_shape=(
            shape((kernels * channels, channels), F32),
            shape((slots, brick, channels), BF16),
        ),
        in_specs=vmem(PARTS + 2),
        out_specs=(pl.BlockSpec(memory_space=pltpu.HBM),) * 2,
        scratch_shapes=[
            pltpu.VMEM((PARTS, part, channels), F32),
            pltpu.SemaphoreType.DMA((PARTS + 1,)),
        ],
        compiler_params=pltpu.CompilerParams(vmem_limit_bytes=16 * 2**20),
        name="normalise",
    )(*pieces, *others, squares_of, grad_features)
    return (grad_features, grad_weight.reshape(conv_weight.shape))


def solution(mesh):
    in_specs = (
        P(("tx", "ty"), None, None),
        P(("tx", "ty"), None),
        P(None, ("tx", "ty")),
        P(("tx", "ty")),
        P(),
        P(),
        P(None, ("tx", "ty")),
    )
    out_specs = (P(("tx", "ty"), None, None), P())
    return jax.shard_map(
        on_device, mesh=mesh, in_specs=in_specs, out_specs=out_specs, check_vma=False
    )
```

```python
import functools

import jax
import jax.numpy as jnp
from jax import lax
from jax.experimental import pallas as pl
from jax.experimental.pallas import tpu as pltpu
from jax.sharding import PartitionSpec as P

GX = 2
GY = 2
BX = 4
BY = 4
SIDE = 8
PLANE = SIDE * SIDE
TAPS = 9
BF16 = jnp.bfloat16
F32 = jnp.float32
PARTS = 8


def vmem(count):
    return [pl.BlockSpec(memory_space=pltpu.VMEM)] * count


def pin(array):
    return pltpu.with_memory_space_constraint(array, pltpu.HBM)


def call(body, outs, inputs, scratch=(), limit=32 * 2**20, name=None, fetched=0):
    return pl.pallas_call(
        body,
        out_shape=outs,
        in_specs=[pl.BlockSpec(memory_space=pltpu.HBM)] * fetched + vmem(len(inputs) - fetched),
        out_specs=jax.tree.map(lambda _: pl.BlockSpec(memory_space=pltpu.VMEM), outs),
        scratch_shapes=list(scratch),
        compiler_params=pltpu.CompilerParams(vmem_limit_bytes=limit),
        name=name,
    )(*[pin(array) for array in inputs[:fetched]], *inputs[fetched:])


def fetch(sources, rooms, semaphores):
    copies = [
        pltpu.make_async_copy(source, room, semaphores.at[i])
        for i, (source, room) in enumerate(zip(sources, rooms))
    ]
    for copy in copies:
        copy.start()
    return copies


def shape(dims, dtype):
    return jax.ShapeDtypeStruct(dims, dtype)


def parity(axis):
    return lax.rem(lax.axis_index(axis), 2) == 0


def occupancy_columns(occ_ref, rows):
    occ = occ_ref[...].astype(F32)
    padded = jnp.concatenate([occ, jnp.zeros((8 - occ.shape[0], occ.shape[1]), F32)], axis=0)
    return padded.T


def y_faces(planes):
    low = jnp.concatenate([planes(x)[:SIDE] for x in range(SIDE)], axis=0)
    high = jnp.concatenate([planes(x)[PLANE - SIDE :] for x in range(SIDE)], axis=0)
    return low, high


def occupancy_mask(columns, slot, first, rows, channels):
    return jnp.broadcast_to(columns[first : first + rows, slot : slot + 1], (rows, channels))


def first_faces_kernel(
    feat_hbm, occ_hbm, b_ref, a_ref, ends_ref, feat_ref, occ_ref, semaphores
):
    for copy in fetch((feat_hbm, occ_hbm), (feat_ref, occ_ref), semaphores):
        copy.wait()
    columns = occupancy_columns(occ_ref, 8)
    rows, channels = BY * SIDE, feat_ref.shape[2]

    def masked(x, j, first, count):
        slot, row = x // BX * GY + j, x % BX * rows + first
        mask = occupancy_mask(columns, slot, row, count, channels)
        return feat_ref[slot, row : row + count, :].astype(F32) * mask

    low_y = jnp.concatenate([masked(x, 0, 0, SIDE) for x in range(SIDE)], axis=0)
    high_y = jnp.concatenate([masked(x, GY - 1, rows - SIDE, SIDE) for x in range(SIDE)], axis=0)
    even = parity("ty")
    a_ref[...] = jnp.where(even, high_y, low_y).astype(BF16)
    b_ref[...] = jnp.where(even, low_y, high_y).astype(BF16)
    for i, x in enumerate((0, SIDE - 1)):
        plane = jnp.concatenate([masked(x, j, 0, rows) for j in range(GY)], axis=0)
        ends_ref[i] = plane.astype(BF16)


def fetch_kernel(*refs):
    count = len(refs) // 2 - 1
    for copy in fetch(refs[:count], refs[count + 1 : -1], refs[-1]):
        copy.wait()


def halo_along_y(b_ref, a_ref):
    even = parity("ty")
    a, b = a_ref[...].astype(F32), b_ref[...].astype(F32)
    return jnp.where(even, b, a), jnp.where(even, a, b)


def x_faces_kernel(ends_ref, y_a_ref, y_b_ref, *refs):
    pair_ref, next_ref = refs[-2:]
    low, high = halo_along_y(y_b_ref, y_a_ref)
    last = PLANE - SIDE
    first = jnp.concatenate([low[:SIDE], ends_ref[0].astype(F32), high[:SIDE]], axis=0)
    final = jnp.concatenate([low[last:], ends_ref[1].astype(F32), high[last:]], axis=0)
    even = parity("tx")
    pair_ref[...] = jnp.where(even, final, first).astype(BF16)
    next_ref[...] = jnp.where(even, first, final).astype(BF16)


def store_edges(low, high, edge_ref, a_ref, b_ref, planes_ref):
    even_y = parity("ty")
    planes_ref[0] = low.astype(BF16)
    planes_ref[1] = high.astype(BF16)
    last = PLANE - SIDE
    bottom = jnp.concatenate([low[:SIDE], edge_ref[0].astype(F32), high[:SIDE]], axis=0)
    top = jnp.concatenate([low[last:], edge_ref[1].astype(F32), high[last:]], axis=0)
    a_ref[...] = jnp.where(even_y, top, bottom).astype(BF16)
    b_ref[...] = jnp.where(even_y, bottom, top).astype(BF16)


def hand_on_edge_kernel(flips, first_row, edge_ref, got1_ref, got2_ref, *refs):
    lines, (a_ref, b_ref, planes_ref) = refs[: len(flips)], refs[-3:]
    even = parity("tx")
    pair = picked_face(got1_ref[first_row[0] : first_row[0] + PLANE], got2_ref[first_row[1] : first_row[1] + PLANE])
    place = lax.axis_index("tx") // 2
    behind = jnp.where(even, place - 1, place + 1)
    other = jnp.zeros(pair.shape, F32)
    lane = lane_of(lax.axis_index("tx"), lax.axis_index("ty"))
    for both, line_ref in zip(flips, lines):
        flip = jnp.where(lane == 0, *both)
        face = line_ref[first_row[2] : first_row[2] + PLANE].astype(F32)
        other = jnp.where((place ^ behind) == flip, face, other)
    low, high = jnp.where(even, other, pair), jnp.where(even, pair, other)
    store_edges(low, high, edge_ref, a_ref, b_ref, planes_ref)


def picked_face(by_first_way, by_core):
    lane = lane_of(lax.axis_index("tx"), lax.axis_index("ty"))
    return jnp.where(lane == 0, by_core.astype(F32), by_first_way.astype(F32))


def write_columns(plane, cols_ref):
    channels = plane.shape[1]
    z = lax.broadcasted_iota(jnp.int32, plane.shape, 0) % SIDE
    zeros = jnp.zeros((1, channels), F32)
    before = jnp.where(z == 0, 0.0, jnp.concatenate([zeros, plane[:-1]], axis=0))
    after = jnp.where(z == SIDE - 1, 0.0, jnp.concatenate([plane[1:], zeros], axis=0))
    for dz, moved in enumerate((before, plane, after)):
        for dy in range(3):
            tap = 3 * dy + dz
            window = moved[dy * SIDE : dy * SIDE + PLANE]
            cols_ref[:, tap * channels : (tap + 1) * channels] = window.astype(BF16)


def split3(value):
    high = value.astype(BF16)
    rest = value - high.astype(F32)
    middle = rest.astype(BF16)
    low = (rest - middle.astype(F32)).astype(BF16)
    return high, middle, low


def contract(a, b, dim_a, dim_b):
    return lax.dot_general(a, b, (((dim_a,), (dim_b,)), ((), ())), preferred_element_type=F32)


def voxel_sums(point_ref, teach_ref):
    target = jnp.exp(teach_ref[...].astype(F32))
    target = target / jnp.sum(target, axis=0, keepdims=True)
    classes, points = target.shape
    place = point_ref[...]
    place = (place & 0x11F) | ((place & 0x80) >> 2) | ((place & 0x60) << 1)
    chosen = lax.broadcasted_iota(jnp.int32, (SIDE * PLANE, points), 0) == place
    chosen = jnp.where(chosen, 1.0, 0.0).astype(BF16)
    stack = jnp.concatenate([*split3(target), jnp.ones((classes, points), BF16)], axis=0)
    sums = contract(stack, chosen, 1, 1)
    target_sum = sums[:classes] + sums[classes : 2 * classes] + sums[2 * classes : 3 * classes]
    return jnp.concatenate([target_sum, sums[3 * classes :]], axis=0)


def main_kernel(
    feat_ref, occ_ref, point_ref, teach_ref, weight_ref, y_a_ref, y_b_ref,
    cols_ref, pre_ref, mask_ref, sums_ref,
):
    rows, channels = BY * SIDE, feat_ref.shape[2]
    columns = occupancy_columns(occ_ref, 8)
    low, high = halo_along_y(y_b_ref, y_a_ref)
    for x in range(SIDE):
        plane = []
        for j in range(GY):
            slot, row = x // BX * GY + j, x % BX * rows
            mask = occupancy_mask(columns, slot, row, rows, channels)
            mask_ref[x, j * rows : (j + 1) * rows, :] = mask
            plane.append(feat_ref[slot, row : row + rows, :].astype(F32) * mask)
        here = slice(x * SIDE, (x + 1) * SIDE)
        write_columns(jnp.concatenate([low[here], *plane, high[here]], axis=0), cols_ref.at[x])
    wide, inner = TAPS * channels, SIDE - 1
    sums_ref[...] = voxel_sums(point_ref, teach_ref)

    def product(planes, dx):
        window = cols_ref[planes].reshape(-1, wide)
        matrix = weight_ref[TAPS * dx : TAPS * (dx + 1)].reshape(wide, channels)
        return jnp.dot(window, matrix, preferred_element_type=F32)

    edge = jnp.zeros((PLANE, channels), F32)
    pre = product(slice(0, SIDE), 1)
    pre = pre + jnp.concatenate([edge, product(slice(0, inner), 0)], axis=0)
    pre_ref[...] = pre + jnp.concatenate([product(slice(1, SIDE), 2), edge], axis=0)


def write_terms(cols_ref, ends_ref, gradient, start, stop, terms_ref, first=0):
    channels = gradient.shape[1]
    inner = (SIDE - 1) * PLANE
    for dx in range(3):
        low, high = max(start, TAPS * dx), min(stop, TAPS * (dx + 1))
        if low >= high:
            continue
        lanes = slice((low - TAPS * dx) * channels, (high - TAPS * dx) * channels)

        def term(planes, gradient):
            return contract(planes.reshape(gradient.shape[0], -1), gradient, 0, 0)

        if dx == 0:
            total = term(cols_ref[: SIDE - 1, :, lanes], gradient[PLANE:])
            total = total + term(ends_ref[0, :, lanes], gradient[:PLANE])
        elif dx == 1:
            total = term(cols_ref[:, :, lanes], gradient)
        else:
            total = term(cols_ref[1:, :, lanes], gradient[:inner])
            total = total + term(ends_ref[1, :, lanes], gradient[inner:])
        terms_ref[(low - first) * channels : (high - first) * channels] = total


def for_quarter(body):
    for i in range(PARTS // 2):
        pl.when((part_index(PARTS - 2) >> 1) == i)(functools.partial(body, i))


def tile_kernel(
    cols_ref, pre_ref, mask_ref, sums_ref, head_ref, weight_ref, x_next_ref, x_pair_ref,
    grad_ref, ends_ref, first_ref,
    terms_ref,
):
    channels = cols_ref.shape[2] // TAPS
    classes = head_ref.shape[0]
    voxels, wide, inner = SIDE * PLANE, TAPS * channels, (SIDE - 1) * PLANE
    even = parity("tx")
    pair, other = x_pair_ref[...].astype(F32), x_next_ref[...].astype(F32)
    write_columns(jnp.where(even, other, pair), ends_ref.at[0])
    write_columns(jnp.where(even, pair, other), ends_ref.at[1])
    first = weight_ref[:TAPS].reshape(wide, channels)
    final = weight_ref[2 * TAPS :].reshape(wide, channels)
    low = pre_ref[:PLANE] + jnp.dot(ends_ref[0], first, preferred_element_type=F32)
    high = pre_ref[inner:] + jnp.dot(ends_ref[1], final, preferred_element_type=F32)
    pre = jnp.concatenate([low, pre_ref[PLANE:inner], high], axis=0)
    mask = mask_ref[...].reshape(voxels, channels)
    logistic = 1.0 / (1.0 + jnp.exp(-pre))
    slope = logistic * (1.0 + pre * (1.0 - logistic)) * mask
    hidden = (pre / (1.0 + jnp.exp(-pre)) * mask).astype(BF16)

    logits = contract(head_ref[...], hidden, 1, 1)
    student = jnp.exp(logits)
    student = student / jnp.sum(student, axis=0, keepdims=True)
    target_sum, count = sums_ref[:classes], sums_ref[classes:]
    slope_logits = jnp.where(count > 0.0, count * student, 0.0) - target_sum
    heads = jnp.concatenate([head_ref[...]] * 3, axis=0)
    pieces = jnp.concatenate([piece.astype(F32) for piece in split3(slope_logits)], axis=0)
    dhidden = contract(pieces.T.astype(BF16), heads, 1, 0)
    rounded = (dhidden * slope).astype(BF16)
    grad_ref[...] = rounded.reshape(SIDE, PLANE, channels)
    length = 3 * TAPS * channels // PARTS
    even = parity("tx")
    low, high = rounded[:PLANE].astype(F32), rounded[inner:].astype(F32)
    first_ref[2 * length : 2 * length + PLANE] = jnp.where(even, high, low).astype(BF16)
    first_ref[2 * length + PLANE :] = jnp.where(even, low, high).astype(BF16)

    def parts(i):
        start = 2 * length * i // channels
        stop = -(-2 * length * (i + 1) // channels)
        write_terms(cols_ref, ends_ref, rounded, start, stop, terms_ref, start)
        for r in range(2):
            row = 2 * length * i - start * channels + (part_index(PARTS - 2 + r) & 1) * length
            part = terms_ref[pl.ds(pl.multiple_of(row, 16), length)]
            first_ref[r * length : (r + 1) * length] = part.astype(BF16)

    for_quarter(parts)


def terms_kernel(
    cols_ref, ends_ref, grad_ref, edge_ref, keep_ref, rest_ref, terms_ref
):
    channels = grad_ref.shape[2]
    length = terms_ref.shape[0] // PARTS
    gradient = grad_ref[...].reshape(-1, channels)
    low_y, high_y = y_faces(lambda x: grad_ref[x].astype(F32))
    edge_ref[0] = low_y.astype(BF16)
    edge_ref[1] = high_y.astype(BF16)

    def parts(i):
        stop = -(-2 * length * i // channels)
        start = 2 * length * (i + 1) // channels
        write_terms(cols_ref, ends_ref, gradient, 0, stop, terms_ref)
        write_terms(cols_ref, ends_ref, gradient, start, 3 * TAPS, terms_ref)

    for_quarter(parts)
    for r in range(PARTS - 2):
        part = terms_ref[pl.ds(pl.multiple_of(part_index(r) * length, 16), length)]
        if r < PARTS // 2:
            keep_ref[r * length : (r + 1) * length] = part
        else:
            row = (r - PARTS // 2) * length
            rest_ref[row : row + length] = part.astype(BF16)


def lane_of(tx, ty):
    return (ty ^ (ty >> 1) ^ tx ^ (tx >> 1)) & 1


def part_index(r):
    tx, ty = lax.axis_index("tx"), lax.axis_index("ty")
    lane, across, along = lane_of(tx, ty) ^ (r >> 2), (ty >> 1) & 1, tx & 1
    first = jnp.where(lane == 0, across, along)
    second = jnp.where(lane == 0, along, across)
    return lane * 4 + ((first * 2 + second) ^ (r & 3))


def moved_weights(weight_ref, taps):
    return jnp.concatenate([weight_ref[3 * TAPS - 1 - tap] for tap in taps], axis=1)


def back_kernel(grad_ref, planes_ref, weight_ref, part_ref, cols_ref):
    channels = grad_ref.shape[2]
    edge = jnp.zeros((SIDE, channels), F32)
    for x in range(SIDE + 2):
        plane = planes_ref[0 if x == 0 else 1] if x in (0, SIDE + 1) else grad_ref[x - 1]
        write_columns(jnp.concatenate([edge, plane.astype(F32), edge], axis=0), cols_ref.at[x])
    total = jnp.zeros(part_ref.shape, F32)
    for dx in range(3):
        window = cols_ref[dx : dx + SIDE].reshape(-1, TAPS * channels)
        taps = range(TAPS * dx, TAPS * (dx + 1))
        total = total + contract(window, moved_weights(weight_ref, taps), 1, 1)
    part_ref[...] = total


def squares(ref, rows):
    value = ref[:rows].astype(F32)
    return jnp.sum(value * value, axis=0, keepdims=True)


def y_faces_kernel(
    extra_ref, part_ref, mask_ref, weight_ref, near_ref, far_ref, *refs
):
    pieces, (out_ref, squares_ref, cols_ref) = refs[:-3], refs[-3:]
    channels, rows = part_ref.shape[1], (SIDE + 2) * SIDE
    tx, ty = lax.axis_index("tx"), lax.axis_index("ty")
    part = near_ref.shape[0] - 2 * rows
    total = sum(squares(ref, part) for ref in pieces)
    squares_ref[...] = jnp.broadcast_to(total, squares_ref.shape)
    own, by_core = far_ref[part:].astype(F32), near_ref[part + rows :].astype(F32)
    other = jnp.where(lane_of(tx, ty) == 0, own, by_core)
    beyond = jnp.zeros(other.shape, F32) if extra_ref is None else extra_ref[...].astype(F32)
    other = jnp.where(((ty + 1) & 2) == 2, other, beyond)
    pair = near_ref[part : part + rows].astype(F32)
    even = parity("ty")
    added = []
    for dy, face in ((0, jnp.where(even, other, pair)), (2, jnp.where(even, pair, other))):
        write_columns(face, cols_ref)
        taps = [TAPS * dx + 3 * dy + dz for dx in range(3) for dz in range(3)]
        added.append(contract(cols_ref[...], moved_weights(weight_ref, taps), 1, 1))
    low, high = added
    rows = BY * SIDE
    for x in range(SIDE):
        here = slice(x * SIDE, (x + 1) * SIDE)
        total = part_ref[x * PLANE : (x + 1) * PLANE]
        first, final = total[:SIDE] + low[here], total[PLANE - SIDE :] + high[here]
        total = jnp.concatenate([first, total[SIDE : PLANE - SIDE], final], axis=0)
        total = (total * mask_ref[x]).astype(BF16)
        for j in range(GY):
            slot, a = x // BX * GY + j, x % BX
            out_ref[slot, a * rows : (a + 1) * rows, :] = total[j * rows : (j + 1) * rows]


def norm_kernel(*refs):
    pieces, refs = refs[:PARTS], refs[PARTS:]
    squares_ref, grad_ref, out_hbm, grad_hbm, out_ref, semaphores = refs
    copies = [pltpu.make_async_copy(grad_ref, grad_hbm, semaphores.at[PARTS])]
    copies[0].start()
    rows, channels = out_ref.shape[1:]
    total = squares_ref[:1] + squares(pieces[-1], rows)
    mean = jnp.sum(total, axis=1, keepdims=True) / (PARTS * rows * channels)
    scale = jnp.broadcast_to(1.0 / jnp.sqrt(mean + 1e-06), (1, channels))
    for r, piece in enumerate(pieces):
        out_ref[r] = piece[:rows].astype(F32) * scale
        first = pl.multiple_of(part_index(r) * rows, 16)
        target = out_hbm.at[pl.ds(first, rows)]
        copies.append(pltpu.make_async_copy(out_ref.at[r], target, semaphores.at[r]))
        copies[-1].start()
    for copy in copies:
        copy.wait()


def swap_pairs(first, count):
    return [pair for i in range(first, count - 1, 2) for pair in ((i, i + 1), (i + 1, i))]


def swap_along_y(b, a):
    count = lax.axis_size("ty")
    got_a = lax.ppermute(a, "ty", swap_pairs(0, count))
    return lax.ppermute(b, "ty", swap_pairs(1, count)), got_a


def edge_faces(kernel, edges, faces, waits=()):
    face = shape(((SIDE + 2) * SIDE, edges.shape[2]), BF16)
    return pl.pallas_call(
        kernel,
        out_shape=(face, face, shape(edges.shape, BF16)),
        in_specs=vmem(1 + len(faces)) + [pl.BlockSpec(memory_space=pl.ANY)] * len(waits),
        out_specs=tuple(vmem(3)),
        compiler_params=pltpu.CompilerParams(vmem_limit_bytes=16 * 2**20),
        name="edge_faces",
    )(edges, *faces, *waits)


def exchange_with(value, partner):
    n_tx, n_ty = lax.axis_size("tx"), lax.axis_size("ty")
    pairs = []
    for tx in range(n_tx):
        for ty in range(n_ty):
            other = partner(tx, ty)
            if other is not None:
                pairs.append((tx * n_ty + ty, other[0] * n_ty + other[1]))
    return lax.ppermute(value, ("tx", "ty"), pairs)


def by_core(tx, ty):
    return tx, ty ^ 1


def same_lane(tx, ty, other_tx, other_ty):
    return other_tx, other_ty ^ lane_of(tx, ty) ^ lane_of(other_tx, other_ty)


def first_way(tx, ty):
    other = (tx, ty ^ 2) if lane_of(tx, ty) == 0 else (tx ^ 1, ty)
    return same_lane(tx, ty, *other)


def second_way(tx, ty):
    other = (tx ^ 1, ty) if lane_of(tx, ty) == 0 else (tx, ty ^ 2)
    return same_lane(tx, ty, *other)


def along_line(flips):
    return lambda tx, ty: same_lane(tx, ty, tx ^ (2 * flips[lane_of(tx, ty)]), ty)


def inner_face(own, other):
    inner = ((lax.axis_index("ty") + 1) & 2) == 2
    return jnp.where(inner, own, other)


def add(*terms):
    total = terms[0]
    for term in terms[1:]:
        total = total + term
    return total


def message(sections, waits=(), passes=()):
    arrays = []
    for _, _, *terms in sections:
        for array, _ in terms:
            if not any(array is known for known in arrays):
                arrays.append(array)
    place = [[next(i for i, x in enumerate(arrays) if x is array) for array, _ in terms] for _, _, *terms in sections]
    count, others = len(arrays), len(waits) + len(passes)
    total_rows = sum(section[0] for section in sections)

    def body(*refs):
        out_ref, row = refs[count + others], 0
        for places, (rows, fn, *terms) in zip(place, sections):
            values = [refs[i][first : first + rows].astype(F32) for i, (_, first) in zip(places, terms)]
            out_ref[row : row + rows] = fn(*values).astype(BF16)
            row += rows

    plain = pl.BlockSpec(memory_space=pl.ANY)
    outs = [shape((total_rows, arrays[0].shape[1]), BF16)]
    out, *passed = pl.pallas_call(
        body,
        out_shape=outs + [shape(x.shape, x.dtype) for x in passes],
        in_specs=vmem(count) + [plain] * others,
        out_specs=vmem(1) + [plain] * len(passes),
        input_output_aliases={count + len(waits) + i: 1 + i for i in range(len(passes))},
        compiler_params=pltpu.CompilerParams(vmem_limit_bytes=16 * 2**20),
        name="message",
    )(*arrays, *waits, *passes)
    return (out, *passed) if passes else out


def after(value, token):
    plain = pl.BlockSpec(memory_space=pl.ANY)
    return pl.pallas_call(
        lambda value_ref, token_ref, out_ref: None,
        out_shape=shape(value.shape, value.dtype),
        in_specs=[plain] * 2,
        out_specs=plain,
        input_output_aliases={0: 0},
        compiler_params=pltpu.CompilerParams(vmem_limit_bytes=16 * 2**20),
        name="after",
    )(value, token)


def on_device(features, occupancy, neighbors, point_voxel, conv_weight, head_weight, teacher):
    slots, brick, channels = features.shape
    kernels = conv_weight.shape[0]
    n_tx, n_ty = lax.axis_size("tx"), lax.axis_size("ty")
    edges = shape((2, PLANE, channels), BF16)
    cols = pltpu.VMEM((SIDE + 2, PLANE, TAPS * channels), BF16)

    points = point_voxel.reshape(1, -1)
    fetched = (features, occupancy)
    face = shape((PLANE, channels), BF16)
    wide_face = shape(((SIDE + 2) * SIDE, channels), BF16)
    planes = shape((SIDE, PLANE, channels), F32)
    y_b, y_a, x_ends, feat, occ = call(
        first_faces_kernel,
        (face, face, edges, *[shape(x.shape, x.dtype) for x in fetched]),
        fetched,
        (pltpu.SemaphoreType.DMA((len(fetched),)),),
        name="first_faces",
        fetched=len(fetched),
    )
    fetched = (points, teacher, head_weight, conv_weight)
    point, teach, head, weight = call(
        fetch_kernel,
        tuple(shape(x.shape, x.dtype) for x in fetched),
        (*fetched, x_ends),
        (pltpu.SemaphoreType.DMA((len(fetched),)),),
        name="fetch",
        fetched=len(fetched),
    )
    y_b, y_a = swap_along_y(y_b, y_a)
    x_pair, x_next = pl.pallas_call(
        x_faces_kernel,
        out_shape=(wide_face, wide_face),
        in_specs=vmem(3) + [pl.BlockSpec(memory_space=pl.ANY)],
        out_specs=tuple(vmem(2)),
        compiler_params=pltpu.CompilerParams(vmem_limit_bytes=16 * 2**20),
        name="x_faces",
    )(x_ends, y_a, y_b, weight)
    x_next = lax.ppermute(x_next, "tx", swap_pairs(1, n_tx))
    x_pair = lax.ppermute(x_pair, "tx", swap_pairs(0, n_tx))
    tile_cols, pre, mask, sums = call(
        main_kernel,
        (
            shape((SIDE, PLANE, TAPS * channels), BF16),
            shape((SIDE * PLANE, channels), F32),
            planes,
            shape((2 * head_weight.shape[0], SIDE * PLANE), F32),
        ),
        (feat, occ, point, teach, weight, y_a, y_b),
        name="main",
    )
    part = kernels * channels // PARTS
    ends = shape((2, PLANE, TAPS * channels), BF16)
    gradient, ends, first = call(
        tile_kernel,
        (shape((SIDE, PLANE, channels), BF16), ends, shape((2 * part + 2 * PLANE, channels), BF16)),
        (tile_cols, pre, mask, sums, head, weight, x_next, x_pair),
        (pltpu.VMEM((2 * part + 2 * channels, channels), F32),),
        name="tile",
    )
    g_edges, keep, rest = call(
        terms_kernel,
        (
            edges,
            shape((PARTS // 2 * part, channels), F32),
            shape((2 * part, channels), BF16),
        ),
        (tile_cols, ends, gradient),
        (pltpu.VMEM((kernels * channels, channels), F32),),
        name="terms",
    )

    got_first = exchange_with(first, by_core)
    got_rest = exchange_with(rest, by_core)
    onward = message([(part, add, (keep, 3 * part), (got_first, part))])
    got_onward = exchange_with(onward, first_way)
    pair, following = 2 * part, 2 * part + PLANE
    planes = [(got_first, pair), (first, following), (first, pair), (got_first, following)]
    got1 = exchange_with(
        message(
            [(part, add, (keep, 2 * part), (got_first, 0))]
            + [(PLANE, add, plane) for plane in planes]
        ),
        first_way,
    )
    kept = [(part, add, (keep, part), (got_rest, part), (got_onward, 0))]
    got2 = exchange_with(message(kept), second_way)
    x_faces = exchange_with(message([(2 * PLANE, add, (got1, part + 2 * PLANE))]), by_core)
    at = (part, 0, part)
    hand_on = (PLANE, picked_face, (got1, part + PLANE), (x_faces, PLANE))
    total = [(part, add, (keep, 0), (got_rest, 0), (got1, 0), (got2, 0))]
    flips, lines = [], []
    while 2 ** len(flips) < n_tx // 2:
        flips.append(2 ** (len(flips) + 1) - 1)
    flips = list(zip(flips[::-1], flips))
    for both in flips:
        own = message(total + [hand_on])
        lines.append(exchange_with(own, along_line(both)))
        total = [(part, add, (own, 0), (lines[-1], 0))]
        hand_on = (PLANE, add, (own, part))
    bit = 4
    while bit < n_ty:
        own = message(total)
        flip = 2 * bit - 4
        got = exchange_with(own, lambda tx, ty, flip=flip: same_lane(tx, ty, tx, ty ^ flip))
        total = [(part, add, (own, 0), (got, 0))]
        bit *= 2
    kernel = functools.partial(hand_on_edge_kernel, flips, at)
    g_a, g_b, planes = edge_faces(kernel, g_edges, (got1, x_faces, *lines))
    rows = g_a.shape[0]
    total, gradient = message(total, (), (gradient,))
    piece1 = exchange_with(total, second_way)
    back_part = call(
        back_kernel,
        shape((SIDE * PLANE, channels), F32),
        (gradient, planes, weight),
        (cols,),
        name="back",
    )
    other_b = exchange_with(g_b, by_core)
    face = (rows, inner_face, (g_b, 0), (other_b, 0))
    piece2 = exchange_with(message([(part, add, (total, 0)), face], (back_part,)), first_way)
    piece3 = exchange_with(piece1, first_way)
    near = message([(part, add, (piece2, 0)), (rows, add, (g_a, 0)), (rows, add, (piece2, part))])
    pieces = (total, piece1, near, piece3)
    others = [exchange_with(piece, by_core) for piece in pieces]
    faces = (back_part, mask, weight, others[2], piece2, *pieces, *others[:3])
    kernel = functools.partial(y_faces_kernel, None)
    if n_ty > 4:
        pairs = [pair for i in range(3, n_ty - 1, 4) for pair in ((i, i + 1), (i + 1, i))]
        faces = (lax.ppermute(g_b, "ty", pairs), *faces)
        kernel = y_faces_kernel
    grad_features, squares_of = call(
        kernel,
        (shape((slots, brick, channels), BF16), shape((8, channels), F32)),
        faces,
        (pltpu.VMEM((PLANE, TAPS * channels), BF16),),
        name="y_faces",
    )
    grad_weight, grad_features = pl.pallas_call(
        norm_kernel,
        out_shape=(
            shape((kernels * channels, channels), F32),
            shape((slots, brick, channels), BF16),
        ),
        in_specs=vmem(PARTS + 2),
        out_specs=(pl.BlockSpec(memory_space=pltpu.HBM),) * 2,
        scratch_shapes=[
            pltpu.VMEM((PARTS, part, channels), F32),
            pltpu.SemaphoreType.DMA((PARTS + 1,)),
        ],
        compiler_params=pltpu.CompilerParams(vmem_limit_bytes=16 * 2**20),
        name="normalise",
    )(*pieces, *others, squares_of, grad_features)
    return (grad_features, grad_weight.reshape(conv_weight.shape))


def solution(mesh):
    in_specs = (
        P(("tx", "ty"), None, None),
        P(("tx", "ty"), None),
        P(None, ("tx", "ty")),
        P(("tx", "ty")),
        P(),
        P(),
        P(None, ("tx", "ty")),
    )
    out_specs = (P(("tx", "ty"), None, None), P())
    return jax.shard_map(
        on_device, mesh=mesh, in_specs=in_specs, out_specs=out_specs, check_vma=False
    )
```

```python
import functools

import jax
import jax.numpy as jnp
from jax import lax
from jax.experimental import pallas as pl
from jax.experimental.pallas import tpu as pltpu
from jax.sharding import PartitionSpec as P

GX = 2
GY = 2
BX = 4
BY = 4
SIDE = 8
PLANE = SIDE * SIDE
TAPS = 9
BF16 = jnp.bfloat16
F32 = jnp.float32
PARTS = 8


def vmem(count):
    return [pl.BlockSpec(memory_space=pltpu.VMEM)] * count


def pin(array):
    return pltpu.with_memory_space_constraint(array, pltpu.HBM)


def call(body, outs, inputs, scratch=(), limit=32 * 2**20, name=None, fetched=0):
    return pl.pallas_call(
        body,
        out_shape=outs,
        in_specs=[pl.BlockSpec(memory_space=pltpu.HBM)] * fetched + vmem(len(inputs) - fetched),
        out_specs=jax.tree.map(lambda _: pl.BlockSpec(memory_space=pltpu.VMEM), outs),
        scratch_shapes=list(scratch),
        compiler_params=pltpu.CompilerParams(vmem_limit_bytes=limit),
        name=name,
    )(*[pin(array) for array in inputs[:fetched]], *inputs[fetched:])


def fetch(sources, rooms, semaphores):
    copies = [
        pltpu.make_async_copy(source, room, semaphores.at[i])
        for i, (source, room) in enumerate(zip(sources, rooms))
    ]
    for copy in copies:
        copy.start()
    return copies


def shape(dims, dtype):
    return jax.ShapeDtypeStruct(dims, dtype)


def parity(axis):
    return lax.rem(lax.axis_index(axis), 2) == 0


def occupancy_columns(occ_ref, rows):
    occ = occ_ref[...].astype(F32)
    padded = jnp.concatenate([occ, jnp.zeros((8 - occ.shape[0], occ.shape[1]), F32)], axis=0)
    return padded.T


def y_faces(planes):
    low = jnp.concatenate([planes(x)[:SIDE] for x in range(SIDE)], axis=0)
    high = jnp.concatenate([planes(x)[PLANE - SIDE :] for x in range(SIDE)], axis=0)
    return low, high


def occupancy_mask(columns, slot, first, rows, channels):
    return jnp.broadcast_to(columns[first : first + rows, slot : slot + 1], (rows, channels))


def first_faces_kernel(
    feat_hbm, occ_hbm, b_ref, a_ref, ends_ref, feat_ref, occ_ref, semaphores
):
    for copy in fetch((feat_hbm, occ_hbm), (feat_ref, occ_ref), semaphores):
        copy.wait()
    columns = occupancy_columns(occ_ref, 8)
    rows, channels = BY * SIDE, feat_ref.shape[2]

    def masked(x, j, first, count):
        slot, row = x // BX * GY + j, x % BX * rows + first
        mask = occupancy_mask(columns, slot, row, count, channels)
        return feat_ref[slot, row : row + count, :].astype(F32) * mask

    low_y = jnp.concatenate([masked(x, 0, 0, SIDE) for x in range(SIDE)], axis=0)
    high_y = jnp.concatenate([masked(x, GY - 1, rows - SIDE, SIDE) for x in range(SIDE)], axis=0)
    even = parity("ty")
    a_ref[...] = jnp.where(even, high_y, low_y).astype(BF16)
    b_ref[...] = jnp.where(even, low_y, high_y).astype(BF16)
    for i, x in enumerate((0, SIDE - 1)):
        plane = jnp.concatenate([masked(x, j, 0, rows) for j in range(GY)], axis=0)
        ends_ref[i] = plane.astype(BF16)


def fetch_kernel(*refs):
    count = len(refs) // 2 - 1
    for copy in fetch(refs[:count], refs[count + 1 : -1], refs[-1]):
        copy.wait()


def halo_along_y(b_ref, a_ref):
    even = parity("ty")
    a, b = a_ref[...].astype(F32), b_ref[...].astype(F32)
    return jnp.where(even, b, a), jnp.where(even, a, b)


def x_faces_kernel(ends_ref, y_a_ref, y_b_ref, *refs):
    pair_ref, next_ref = refs[-2:]
    low, high = halo_along_y(y_b_ref, y_a_ref)
    last = PLANE - SIDE
    first = jnp.concatenate([low[:SIDE], ends_ref[0].astype(F32), high[:SIDE]], axis=0)
    final = jnp.concatenate([low[last:], ends_ref[1].astype(F32), high[last:]], axis=0)
    even = parity("tx")
    pair_ref[...] = jnp.where(even, final, first).astype(BF16)
    next_ref[...] = jnp.where(even, first, final).astype(BF16)


def store_edges(low, high, edge_ref, a_ref, b_ref, planes_ref):
    even_y = parity("ty")
    planes_ref[0] = low.astype(BF16)
    planes_ref[1] = high.astype(BF16)
    last = PLANE - SIDE
    bottom = jnp.concatenate([low[:SIDE], edge_ref[0].astype(F32), high[:SIDE]], axis=0)
    top = jnp.concatenate([low[last:], edge_ref[1].astype(F32), high[last:]], axis=0)
    a_ref[...] = jnp.where(even_y, top, bottom).astype(BF16)
    b_ref[...] = jnp.where(even_y, bottom, top).astype(BF16)


def hand_on_edge_kernel(flips, first_row, edge_ref, got1_ref, got2_ref, *refs):
    lines, (a_ref, b_ref, planes_ref) = refs[: len(flips)], refs[-3:]
    even = parity("tx")
    pair = picked_face(got1_ref[first_row[0] : first_row[0] + PLANE], got2_ref[first_row[1] : first_row[1] + PLANE])
    place = lax.axis_index("tx") // 2
    behind = jnp.where(even, place - 1, place + 1)
    other = jnp.zeros(pair.shape, F32)
    lane = lane_of(lax.axis_index("tx"), lax.axis_index("ty"))
    for both, line_ref in zip(flips, lines):
        flip = jnp.where(lane == 0, *both)
        face = line_ref[first_row[2] : first_row[2] + PLANE].astype(F32)
        other = jnp.where((place ^ behind) == flip, face, other)
    low, high = jnp.where(even, other, pair), jnp.where(even, pair, other)
    store_edges(low, high, edge_ref, a_ref, b_ref, planes_ref)


def picked_face(by_first_way, by_core):
    lane = lane_of(lax.axis_index("tx"), lax.axis_index("ty"))
    return jnp.where(lane == 0, by_core.astype(F32), by_first_way.astype(F32))


def write_columns(plane, cols_ref):
    channels = plane.shape[1]
    z = lax.broadcasted_iota(jnp.int32, plane.shape, 0) % SIDE
    zeros = jnp.zeros((1, channels), F32)
    before = jnp.where(z == 0, 0.0, jnp.concatenate([zeros, plane[:-1]], axis=0))
    after = jnp.where(z == SIDE - 1, 0.0, jnp.concatenate([plane[1:], zeros], axis=0))
    for dz, moved in enumerate((before, plane, after)):
        for dy in range(3):
            tap = 3 * dy + dz
            window = moved[dy * SIDE : dy * SIDE + PLANE]
            cols_ref[:, tap * channels : (tap + 1) * channels] = window.astype(BF16)


def split3(value):
    high = value.astype(BF16)
    rest = value - high.astype(F32)
    middle = rest.astype(BF16)
    low = (rest - middle.astype(F32)).astype(BF16)
    return high, middle, low


def contract(a, b, dim_a, dim_b):
    return lax.dot_general(a, b, (((dim_a,), (dim_b,)), ((), ())), preferred_element_type=F32)


def voxel_sums(point_ref, teach_ref):
    target = jnp.exp(teach_ref[...].astype(F32))
    target = target / jnp.sum(target, axis=0, keepdims=True)
    classes, points = target.shape
    place = point_ref[...]
    place = (place & 0x11F) | ((place & 0x80) >> 2) | ((place & 0x60) << 1)
    chosen = lax.broadcasted_iota(jnp.int32, (SIDE * PLANE, points), 0) == place
    chosen = jnp.where(chosen, 1.0, 0.0).astype(BF16)
    stack = jnp.concatenate([*split3(target), jnp.ones((classes, points), BF16)], axis=0)
    sums = contract(stack, chosen, 1, 1)
    target_sum = sums[:classes] + sums[classes : 2 * classes] + sums[2 * classes : 3 * classes]
    return jnp.concatenate([target_sum, sums[3 * classes :]], axis=0)


def main_kernel(
    feat_ref, occ_ref, point_ref, teach_ref, weight_ref, y_a_ref, y_b_ref,
    cols_ref, pre_ref, mask_ref, sums_ref,
):
    rows, channels = BY * SIDE, feat_ref.shape[2]
    columns = occupancy_columns(occ_ref, 8)
    low, high = halo_along_y(y_b_ref, y_a_ref)
    for x in range(SIDE):
        plane = []
        for j in range(GY):
            slot, row = x // BX * GY + j, x % BX * rows
            mask = occupancy_mask(columns, slot, row, rows, channels)
            mask_ref[x, j * rows : (j + 1) * rows, :] = mask
            plane.append(feat_ref[slot, row : row + rows, :].astype(F32) * mask)
        here = slice(x * SIDE, (x + 1) * SIDE)
        write_columns(jnp.concatenate([low[here], *plane, high[here]], axis=0), cols_ref.at[x])
    wide, inner = TAPS * channels, SIDE - 1
    sums_ref[...] = voxel_sums(point_ref, teach_ref)

    def product(planes, dx):
        window = cols_ref[planes].reshape(-1, wide)
        matrix = weight_ref[TAPS * dx : TAPS * (dx + 1)].reshape(wide, channels)
        return jnp.dot(window, matrix, preferred_element_type=F32)

    edge = jnp.zeros((PLANE, channels), F32)
    pre = product(slice(0, SIDE), 1)
    pre = pre + jnp.concatenate([edge, product(slice(0, inner), 0)], axis=0)
    pre_ref[...] = pre + jnp.concatenate([product(slice(1, SIDE), 2), edge], axis=0)


def write_terms(cols_ref, ends_ref, gradient, start, stop, terms_ref, first=0):
    channels = gradient.shape[1]
    inner = (SIDE - 1) * PLANE
    for dx in range(3):
        low, high = max(start, TAPS * dx), min(stop, TAPS * (dx + 1))
        if low >= high:
            continue
        lanes = slice((low - TAPS * dx) * channels, (high - TAPS * dx) * channels)

        def term(planes, gradient):
            return contract(planes.reshape(gradient.shape[0], -1), gradient, 0, 0)

        if dx == 0:
            total = term(cols_ref[: SIDE - 1, :, lanes], gradient[PLANE:])
            total = total + term(ends_ref[0, :, lanes], gradient[:PLANE])
        elif dx == 1:
            total = term(cols_ref[:, :, lanes], gradient)
        else:
            total = term(cols_ref[1:, :, lanes], gradient[:inner])
            total = total + term(ends_ref[1, :, lanes], gradient[inner:])
        terms_ref[(low - first) * channels : (high - first) * channels] = total


def for_quarter(body):
    for i in range(PARTS // 2):
        pl.when((part_index(PARTS - 2) >> 1) == i)(functools.partial(body, i))


def tile_kernel(
    cols_ref, pre_ref, mask_ref, sums_ref, head_ref, weight_ref, x_next_ref, x_pair_ref,
    grad_ref, ends_ref, first_ref,
    terms_ref,
):
    channels = cols_ref.shape[2] // TAPS
    classes = head_ref.shape[0]
    voxels, wide, inner = SIDE * PLANE, TAPS * channels, (SIDE - 1) * PLANE
    even = parity("tx")
    pair, other = x_pair_ref[...].astype(F32), x_next_ref[...].astype(F32)
    write_columns(jnp.where(even, other, pair), ends_ref.at[0])
    write_columns(jnp.where(even, pair, other), ends_ref.at[1])
    first = weight_ref[:TAPS].reshape(wide, channels)
    final = weight_ref[2 * TAPS :].reshape(wide, channels)
    low = pre_ref[:PLANE] + jnp.dot(ends_ref[0], first, preferred_element_type=F32)
    high = pre_ref[inner:] + jnp.dot(ends_ref[1], final, preferred_element_type=F32)
    pre = jnp.concatenate([low, pre_ref[PLANE:inner], high], axis=0)
    mask = mask_ref[...].reshape(voxels, channels)
    logistic = 1.0 / (1.0 + jnp.exp(-pre))
    slope = logistic * (1.0 + pre * (1.0 - logistic)) * mask
    hidden = (pre * logistic * mask).astype(BF16)

    logits = contract(head_ref[...], hidden, 1, 1)
    student = jnp.exp(logits)
    student = student / jnp.sum(student, axis=0, keepdims=True)
    target_sum, count = sums_ref[:classes], sums_ref[classes:]
    slope_logits = jnp.where(count > 0.0, count * student, 0.0) - target_sum
    heads = jnp.concatenate([head_ref[...]] * 3, axis=0)
    pieces = jnp.concatenate([piece.astype(F32) for piece in split3(slope_logits)], axis=0)
    dhidden = contract(pieces.T.astype(BF16), heads, 1, 0)
    rounded = (dhidden * slope).astype(BF16)
    grad_ref[...] = rounded.reshape(SIDE, PLANE, channels)
    length = 3 * TAPS * channels // PARTS
    even = parity("tx")
    low, high = rounded[:PLANE].astype(F32), rounded[inner:].astype(F32)
    first_ref[2 * length : 2 * length + PLANE] = jnp.where(even, high, low).astype(BF16)
    first_ref[2 * length + PLANE :] = jnp.where(even, low, high).astype(BF16)

    def parts(i):
        start = 2 * length * i // channels
        stop = -(-2 * length * (i + 1) // channels)
        write_terms(cols_ref, ends_ref, rounded, start, stop, terms_ref, start)
        for r in range(2):
            row = 2 * length * i - start * channels + (part_index(PARTS - 2 + r) & 1) * length
            part = terms_ref[pl.ds(pl.multiple_of(row, 16), length)]
            first_ref[r * length : (r + 1) * length] = part.astype(BF16)

    for_quarter(parts)


def terms_kernel(
    cols_ref, ends_ref, grad_ref, edge_ref, keep_ref, rest_ref, terms_ref
):
    channels = grad_ref.shape[2]
    length = terms_ref.shape[0] // PARTS
    gradient = grad_ref[...].reshape(-1, channels)
    low_y, high_y = y_faces(lambda x: grad_ref[x].astype(F32))
    edge_ref[0] = low_y.astype(BF16)
    edge_ref[1] = high_y.astype(BF16)

    def parts(i):
        stop = -(-2 * length * i // channels)
        start = 2 * length * (i + 1) // channels
        write_terms(cols_ref, ends_ref, gradient, 0, stop, terms_ref)
        write_terms(cols_ref, ends_ref, gradient, start, 3 * TAPS, terms_ref)

    for_quarter(parts)
    for r in range(PARTS - 2):
        part = terms_ref[pl.ds(pl.multiple_of(part_index(r) * length, 16), length)]
        if r < PARTS // 2:
            keep_ref[r * length : (r + 1) * length] = part
        else:
            row = (r - PARTS // 2) * length
            rest_ref[row : row + length] = part.astype(BF16)


def lane_of(tx, ty):
    return (ty ^ (ty >> 1) ^ tx ^ (tx >> 1)) & 1


def part_index(r):
    tx, ty = lax.axis_index("tx"), lax.axis_index("ty")
    lane, across, along = lane_of(tx, ty) ^ (r >> 2), (ty >> 1) & 1, tx & 1
    first = jnp.where(lane == 0, across, along)
    second = jnp.where(lane == 0, along, across)
    return lane * 4 + ((first * 2 + second) ^ (r & 3))


def moved_weights(weight_ref, taps):
    return jnp.concatenate([weight_ref[3 * TAPS - 1 - tap] for tap in taps], axis=1)


def back_kernel(grad_ref, planes_ref, weight_ref, part_ref, cols_ref):
    channels = grad_ref.shape[2]
    edge = jnp.zeros((SIDE, channels), F32)
    for x in range(SIDE + 2):
        plane = planes_ref[0 if x == 0 else 1] if x in (0, SIDE + 1) else grad_ref[x - 1]
        write_columns(jnp.concatenate([edge, plane.astype(F32), edge], axis=0), cols_ref.at[x])
    total = jnp.zeros(part_ref.shape, F32)
    for dx in range(3):
        window = cols_ref[dx : dx + SIDE].reshape(-1, TAPS * channels)
        taps = range(TAPS * dx, TAPS * (dx + 1))
        total = total + contract(window, moved_weights(weight_ref, taps), 1, 1)
    part_ref[...] = total


def squares(ref, rows):
    value = ref[:rows].astype(F32)
    return jnp.sum(value * value, axis=0, keepdims=True)


def y_faces_kernel(
    extra_ref, part_ref, mask_ref, weight_ref, near_ref, far_ref, *refs
):
    pieces, (out_ref, squares_ref, cols_ref) = refs[:-3], refs[-3:]
    channels, rows = part_ref.shape[1], (SIDE + 2) * SIDE
    tx, ty = lax.axis_index("tx"), lax.axis_index("ty")
    part = near_ref.shape[0] - 2 * rows
    total = sum(squares(ref, part) for ref in pieces)
    squares_ref[...] = jnp.broadcast_to(total, squares_ref.shape)
    own, by_core = far_ref[part:].astype(F32), near_ref[part + rows :].astype(F32)
    other = jnp.where(lane_of(tx, ty) == 0, own, by_core)
    beyond = jnp.zeros(other.shape, F32) if extra_ref is None else extra_ref[...].astype(F32)
    other = jnp.where(((ty + 1) & 2) == 2, other, beyond)
    pair = near_ref[part : part + rows].astype(F32)
    even = parity("ty")
    added = []
    for dy, face in ((0, jnp.where(even, other, pair)), (2, jnp.where(even, pair, other))):
        write_columns(face, cols_ref)
        taps = [TAPS * dx + 3 * dy + dz for dx in range(3) for dz in range(3)]
        added.append(contract(cols_ref[...], moved_weights(weight_ref, taps), 1, 1))
    low, high = added
    rows = BY * SIDE
    for x in range(SIDE):
        here = slice(x * SIDE, (x + 1) * SIDE)
        total = part_ref[x * PLANE : (x + 1) * PLANE]
        first, final = total[:SIDE] + low[here], total[PLANE - SIDE :] + high[here]
        total = jnp.concatenate([first, total[SIDE : PLANE - SIDE], final], axis=0)
        total = (total * mask_ref[x]).astype(BF16)
        for j in range(GY):
            slot, a = x // BX * GY + j, x % BX
            out_ref[slot, a * rows : (a + 1) * rows, :] = total[j * rows : (j + 1) * rows]


def norm_kernel(*refs):
    pieces, refs = refs[:PARTS], refs[PARTS:]
    squares_ref, grad_ref, out_hbm, grad_hbm, out_ref, semaphores = refs
    copies = [pltpu.make_async_copy(grad_ref, grad_hbm, semaphores.at[PARTS])]
    copies[0].start()
    rows, channels = out_ref.shape[1:]
    total = squares_ref[:1] + squares(pieces[-1], rows)
    mean = jnp.sum(total, axis=1, keepdims=True) / (PARTS * rows * channels)
    scale = jnp.broadcast_to(1.0 / jnp.sqrt(mean + 1e-06), (1, channels))
    for r, piece in enumerate(pieces):
        out_ref[r] = piece[:rows].astype(F32) * scale
        first = pl.multiple_of(part_index(r) * rows, 16)
        target = out_hbm.at[pl.ds(first, rows)]
        copies.append(pltpu.make_async_copy(out_ref.at[r], target, semaphores.at[r]))
        copies[-1].start()
    for copy in copies:
        copy.wait()


def swap_pairs(first, count):
    return [pair for i in range(first, count - 1, 2) for pair in ((i, i + 1), (i + 1, i))]


def swap_along_y(b, a):
    count = lax.axis_size("ty")
    got_a = lax.ppermute(a, "ty", swap_pairs(0, count))
    return lax.ppermute(b, "ty", swap_pairs(1, count)), got_a


def edge_faces(kernel, edges, faces, waits=()):
    face = shape(((SIDE + 2) * SIDE, edges.shape[2]), BF16)
    return pl.pallas_call(
        kernel,
        out_shape=(face, face, shape(edges.shape, BF16)),
        in_specs=vmem(1 + len(faces)) + [pl.BlockSpec(memory_space=pl.ANY)] * len(waits),
        out_specs=tuple(vmem(3)),
        compiler_params=pltpu.CompilerParams(vmem_limit_bytes=16 * 2**20),
        name="edge_faces",
    )(edges, *faces, *waits)


def exchange_with(value, partner):
    n_tx, n_ty = lax.axis_size("tx"), lax.axis_size("ty")
    pairs = []
    for tx in range(n_tx):
        for ty in range(n_ty):
            other = partner(tx, ty)
            if other is not None:
                pairs.append((tx * n_ty + ty, other[0] * n_ty + other[1]))
    return lax.ppermute(value, ("tx", "ty"), pairs)


def by_core(tx, ty):
    return tx, ty ^ 1


def same_lane(tx, ty, other_tx, other_ty):
    return other_tx, other_ty ^ lane_of(tx, ty) ^ lane_of(other_tx, other_ty)


def first_way(tx, ty):
    other = (tx, ty ^ 2) if lane_of(tx, ty) == 0 else (tx ^ 1, ty)
    return same_lane(tx, ty, *other)


def second_way(tx, ty):
    other = (tx ^ 1, ty) if lane_of(tx, ty) == 0 else (tx, ty ^ 2)
    return same_lane(tx, ty, *other)


def along_line(flips):
    return lambda tx, ty: same_lane(tx, ty, tx ^ (2 * flips[lane_of(tx, ty)]), ty)


def inner_face(own, other):
    inner = ((lax.axis_index("ty") + 1) & 2) == 2
    return jnp.where(inner, own, other)


def add(*terms):
    total = terms[0]
    for term in terms[1:]:
        total = total + term
    return total


def message(sections, waits=(), passes=()):
    arrays = []
    for _, _, *terms in sections:
        for array, _ in terms:
            if not any(array is known for known in arrays):
                arrays.append(array)
    place = [[next(i for i, x in enumerate(arrays) if x is array) for array, _ in terms] for _, _, *terms in sections]
    count, others = len(arrays), len(waits) + len(passes)
    total_rows = sum(section[0] for section in sections)

    def body(*refs):
        out_ref, row = refs[count + others], 0
        for places, (rows, fn, *terms) in zip(place, sections):
            values = [refs[i][first : first + rows].astype(F32) for i, (_, first) in zip(places, terms)]
            out_ref[row : row + rows] = fn(*values).astype(BF16)
            row += rows

    plain = pl.BlockSpec(memory_space=pl.ANY)
    outs = [shape((total_rows, arrays[0].shape[1]), BF16)]
    out, *passed = pl.pallas_call(
        body,
        out_shape=outs + [shape(x.shape, x.dtype) for x in passes],
        in_specs=vmem(count) + [plain] * others,
        out_specs=vmem(1) + [plain] * len(passes),
        input_output_aliases={count + len(waits) + i: 1 + i for i in range(len(passes))},
        compiler_params=pltpu.CompilerParams(vmem_limit_bytes=16 * 2**20),
        name="message",
    )(*arrays, *waits, *passes)
    return (out, *passed) if passes else out


def after(value, token):
    plain = pl.BlockSpec(memory_space=pl.ANY)
    return pl.pallas_call(
        lambda value_ref, token_ref, out_ref: None,
        out_shape=shape(value.shape, value.dtype),
        in_specs=[plain] * 2,
        out_specs=plain,
        input_output_aliases={0: 0},
        compiler_params=pltpu.CompilerParams(vmem_limit_bytes=16 * 2**20),
        name="after",
    )(value, token)


def on_device(features, occupancy, neighbors, point_voxel, conv_weight, head_weight, teacher):
    slots, brick, channels = features.shape
    kernels = conv_weight.shape[0]
    n_tx, n_ty = lax.axis_size("tx"), lax.axis_size("ty")
    edges = shape((2, PLANE, channels), BF16)
    cols = pltpu.VMEM((SIDE + 2, PLANE, TAPS * channels), BF16)

    points = point_voxel.reshape(1, -1)
    fetched = (features, occupancy)
    face = shape((PLANE, channels), BF16)
    wide_face = shape(((SIDE + 2) * SIDE, channels), BF16)
    planes = shape((SIDE, PLANE, channels), F32)
    y_b, y_a, x_ends, feat, occ = call(
        first_faces_kernel,
        (face, face, edges, *[shape(x.shape, x.dtype) for x in fetched]),
        fetched,
        (pltpu.SemaphoreType.DMA((len(fetched),)),),
        name="first_faces",
        fetched=len(fetched),
    )
    fetched = (points, teacher, head_weight, conv_weight)
    point, teach, head, weight = call(
        fetch_kernel,
        tuple(shape(x.shape, x.dtype) for x in fetched),
        (*fetched, x_ends),
        (pltpu.SemaphoreType.DMA((len(fetched),)),),
        name="fetch",
        fetched=len(fetched),
    )
    y_b, y_a = swap_along_y(y_b, y_a)
    x_pair, x_next = pl.pallas_call(
        x_faces_kernel,
        out_shape=(wide_face, wide_face),
        in_specs=vmem(3) + [pl.BlockSpec(memory_space=pl.ANY)],
        out_specs=tuple(vmem(2)),
        compiler_params=pltpu.CompilerParams(vmem_limit_bytes=16 * 2**20),
        name="x_faces",
    )(x_ends, y_a, y_b, weight)
    x_next = lax.ppermute(x_next, "tx", swap_pairs(1, n_tx))
    x_pair = lax.ppermute(x_pair, "tx", swap_pairs(0, n_tx))
    tile_cols, pre, mask, sums = call(
        main_kernel,
        (
            shape((SIDE, PLANE, TAPS * channels), BF16),
            shape((SIDE * PLANE, channels), F32),
            planes,
            shape((2 * head_weight.shape[0], SIDE * PLANE), F32),
        ),
        (feat, occ, point, teach, weight, y_a, y_b),
        name="main",
    )
    part = kernels * channels // PARTS
    ends = shape((2, PLANE, TAPS * channels), BF16)
    gradient, ends, first = call(
        tile_kernel,
        (shape((SIDE, PLANE, channels), BF16), ends, shape((2 * part + 2 * PLANE, channels), BF16)),
        (tile_cols, pre, mask, sums, head, weight, x_next, x_pair),
        (pltpu.VMEM((2 * part + 2 * channels, channels), F32),),
        name="tile",
    )
    g_edges, keep, rest = call(
        terms_kernel,
        (
            edges,
            shape((PARTS // 2 * part, channels), F32),
            shape((2 * part, channels), BF16),
        ),
        (tile_cols, ends, gradient),
        (pltpu.VMEM((kernels * channels, channels), F32),),
        name="terms",
    )

    got_first = exchange_with(first, by_core)
    got_rest = exchange_with(rest, by_core)
    onward = message([(part, add, (keep, 3 * part), (got_first, part))])
    got_onward = exchange_with(onward, first_way)
    pair, following = 2 * part, 2 * part + PLANE
    planes = [(got_first, pair), (first, following), (first, pair), (got_first, following)]
    got1 = exchange_with(
        message(
            [(part, add, (keep, 2 * part), (got_first, 0))]
            + [(PLANE, add, plane) for plane in planes]
        ),
        first_way,
    )
    kept = [(part, add, (keep, part), (got_rest, part), (got_onward, 0))]
    got2 = exchange_with(message(kept), second_way)
    x_faces = exchange_with(message([(2 * PLANE, add, (got1, part + 2 * PLANE))]), by_core)
    at = (part, 0, part)
    hand_on = (PLANE, picked_face, (got1, part + PLANE), (x_faces, PLANE))
    total = [(part, add, (keep, 0), (got_rest, 0), (got1, 0), (got2, 0))]
    flips, lines = [], []
    while 2 ** len(flips) < n_tx // 2:
        flips.append(2 ** (len(flips) + 1) - 1)
    flips = list(zip(flips[::-1], flips))
    for both in flips:
        own = message(total + [hand_on])
        lines.append(exchange_with(own, along_line(both)))
        total = [(part, add, (own, 0), (lines[-1], 0))]
        hand_on = (PLANE, add, (own, part))
    bit = 4
    while bit < n_ty:
        own = message(total)
        flip = 2 * bit - 4
        got = exchange_with(own, lambda tx, ty, flip=flip: same_lane(tx, ty, tx, ty ^ flip))
        total = [(part, add, (own, 0), (got, 0))]
        bit *= 2
    kernel = functools.partial(hand_on_edge_kernel, flips, at)
    g_a, g_b, planes = edge_faces(kernel, g_edges, (got1, x_faces, *lines))
    rows = g_a.shape[0]
    total, gradient = message(total, (), (gradient,))
    piece1 = exchange_with(total, second_way)
    back_part = call(
        back_kernel,
        shape((SIDE * PLANE, channels), F32),
        (gradient, planes, weight),
        (cols,),
        name="back",
    )
    other_b = exchange_with(g_b, by_core)
    face = (rows, inner_face, (g_b, 0), (other_b, 0))
    piece2 = exchange_with(message([(part, add, (total, 0)), face], (back_part,)), first_way)
    piece3 = exchange_with(piece1, first_way)
    near = message([(part, add, (piece2, 0)), (rows, add, (g_a, 0)), (rows, add, (piece2, part))])
    pieces = (total, piece1, near, piece3)
    others = [exchange_with(piece, by_core) for piece in pieces]
    faces = (back_part, mask, weight, others[2], piece2, *pieces, *others[:3])
    kernel = functools.partial(y_faces_kernel, None)
    if n_ty > 4:
        pairs = [pair for i in range(3, n_ty - 1, 4) for pair in ((i, i + 1), (i + 1, i))]
        faces = (lax.ppermute(g_b, "ty", pairs), *faces)
        kernel = y_faces_kernel
    grad_features, squares_of = call(
        kernel,
        (shape((slots, brick, channels), BF16), shape((8, channels), F32)),
        faces,
        (pltpu.VMEM((PLANE, TAPS * channels), BF16),),
        name="y_faces",
    )
    grad_weight, grad_features = pl.pallas_call(
        norm_kernel,
        out_shape=(
            shape((kernels * channels, channels), F32),
            shape((slots, brick, channels), BF16),
        ),
        in_specs=vmem(PARTS + 2),
        out_specs=(pl.BlockSpec(memory_space=pltpu.HBM),) * 2,
        scratch_shapes=[
            pltpu.VMEM((PARTS, part, channels), F32),
            pltpu.SemaphoreType.DMA((PARTS + 1,)),
        ],
        compiler_params=pltpu.CompilerParams(vmem_limit_bytes=16 * 2**20),
        name="normalise",
    )(*pieces, *others, squares_of, grad_features)
    return (grad_features, grad_weight.reshape(conv_weight.shape))


def solution(mesh):
    in_specs = (
        P(("tx", "ty"), None, None),
        P(("tx", "ty"), None),
        P(None, ("tx", "ty")),
        P(("tx", "ty")),
        P(),
        P(),
        P(None, ("tx", "ty")),
    )
    out_specs = (P(("tx", "ty"), None, None), P())
    return jax.shard_map(
        on_device, mesh=mesh, in_specs=in_specs, out_specs=out_specs, check_vma=False
    )
```
